32 devices in a mesh: sub: 4 (over z), blk: 8 (over y, x, core).
Axes of the slice: x: 2, y: 2, z: 4, core: 2. Of those that a mesh axis runs over, the one named last changes fastest.
Arguments:
- coords: float32 [3, 1024, 256], P(None, ('sub', 'blk')), may hold values from -3.8 to 3.8
- strain: float32 [1024, 256], P(('sub', 'blk')), may hold values from 0.3 to 8
- history: float32 [1024, 256], P(('sub', 'blk')), may hold values from 1 to 3
- corner_load: float32 [24, 1024, 256], P(None, ('sub', 'blk')), may hold values from -0.4 to 0.4
- tile_count: int32 [1024], P(('sub', 'blk')), may hold values from 128 to 256, as said below
- tile_sub: int32 [1024], P(('sub', 'blk')), may hold values from 0 to 3
- local_pairs: int32 [2, 1024], P(None, ('sub', 'blk')), may hold values from 0 to 31, as said below
- send_tile: int32 [256], P(('sub', 'blk')), may hold values from 0 to 3
- remote_pairs: int32 [2, 256], P(None, ('sub', 'blk')), may hold values from 0 to 7, as said below
- remote_count: int32 [32], P(('sub', 'blk')), may hold values from 2 to 8, as said below
- corner_map: int32 [128, 24], P(('sub', 'blk')), may hold values from 0 to 1023
- external: float32 [4096], P(('sub', 'blk')), may hold values from -6 to 6
Outputs:
- damage: float32 [1024, 256], P(('sub', 'blk'))
- coarse_residual: float32 [4096], P(('sub', 'blk'))
The draws below stay inside these ranges and needn't reach their ends.
Inputs may be any that keep to these rules, and one draw needn't show every extreme that they name: `tile_count`: used slots of a tile come first; some tiles are full. `local_pairs`: each column names two different tiles of its device. `remote_pairs`: first row: one of the first four tiles of the device, by local index. Second row: in each device's block of 8 entries, every blk index exactly once. `remote_count`: some device has all 8 entries live. `send_tile`: one of the first four tiles of the sending device.
All inputs are finite; a program needn't handle non-finite values.
Results may differ from the reference program's by a relative error of at most 0.0001.
Values sent between devices are 32-bit elements; how exact they have to be, the bound alone decides.
No kernel may reach another device: no remote copies, remote signals or barrier semaphores. Data moves between devices by JAX's collectives and lax.ppermute only.
A program may use at most 64 MiB of HBM per device.

```python
import math
import jax
import jax.numpy as jnp
from jax import lax

PTS = 256
TILE_DEV = 32
SUB_DEV = 4
CORNER_DOF = 24
COARSE_DEV = 128
NTILES = 1024
REMOTE_ALL = 256
SUB_ALL = 128
COARSE_ALL = 4096
N_BLK = 8


slab_height = 0.6


cycle_step = 0.3


box_half = 0.2


plan_half = 0.6


def place_points(key):
    key_box = jax.random.fold_in(key, 0)
    tile_ids = jnp.arange(NTILES, dtype=jnp.int32)
    device = tile_ids // TILE_DEV
    local = tile_ids % TILE_DEV
    layer = (device // N_BLK).astype(jnp.float32)
    column = (device % N_BLK).astype(jnp.float32)
    angle = 2.0 * math.pi * (column + 0.5) / N_BLK
    radius = 0.15 + cycle_step * (local // 4).astype(jnp.float32)
    lift = (layer + 0.5) * slab_height + ((local % 4).astype(jnp.float32) - 1.5) * 0.05
    centre = jnp.stack([radius * jnp.cos(angle), radius * jnp.sin(angle), lift])
    extent = jnp.array([plan_half, plan_half, box_half], jnp.float32)
    offsets = jax.random.uniform(key_box, (3, NTILES, PTS), jnp.float32, -1.0, 1.0) * extent[:, None, None]
    return centre[:, :, None] + offsets


def draw_coords(key, part):
    points = place_points(key)
    return points.astype(jnp.float32)


def draw_strain(key, part):
    points = place_points(key)
    key = jax.random.fold_in(key, 16)
    key_phase, key_rough = jax.random.split(key)
    phases = jax.random.uniform(key_phase, (4,), jnp.float32, 0.0, 2.0 * math.pi)
    across = points[0]
    along = points[1]
    height = points[2]
    smooth = jnp.sin(1.1 * across + phases[0]) * jnp.cos(0.9 * along + phases[1]) + 0.5 * jnp.sin(0.7 * height + phases[2])
    band_shape = jnp.sin(math.pi * height / slab_height) / 0.3
    band = 1.2 * (0.7 + 0.3 * jnp.cos(1.3 * across + phases[3])) * jnp.exp(-band_shape * band_shape)
    rough = jnp.clip(0.3 * jax.random.normal(key_rough, (NTILES, PTS), jnp.float32), -0.9, 0.9)
    level = math.log(1.6) + 0.8 * smooth + band + rough
    return jnp.clip(jnp.exp(level), 0.3, 8.0).astype(jnp.float32)


def draw_tile_count(key, part):
    key = jax.random.fold_in(key, 11)
    key_one, key_two = jax.random.split(key)
    partial_fill = jax.random.randint(key_one, (NTILES,), PTS // 2, PTS + 1)
    full_tile = jax.random.randint(key_two, (NTILES,), 0, 4) == 0
    return jnp.where(full_tile, PTS, partial_fill).astype(jnp.int32)


def draw_local_pairs(key, part):
    key = jax.random.fold_in(key, 12)
    key_one, key_two, key_three = jax.random.split(key, 3)
    first = jax.random.randint(key_one, (NTILES,), 0, TILE_DEV)
    reach = jax.random.randint(key_two, (NTILES,), 1, 3)
    upward = jax.random.randint(key_three, (NTILES,), 0, 2) == 1
    step = jnp.where(upward, reach, -reach)
    second = first + step
    second = jnp.where(second < 0, first + reach, second)
    second = jnp.where(second >= TILE_DEV, first - reach, second)
    return jnp.stack([first, second]).astype(jnp.int32)


def draw_remote_pairs(key, part):
    key = jax.random.fold_in(key, 13)
    key_one, key_two = jax.random.split(key)
    nodes = REMOTE_ALL // N_BLK
    own_tiles = jax.random.randint(key_one, (REMOTE_ALL,), 0, 4)
    scores = jax.random.randint(key_two, (nodes, N_BLK), 0, 1 << 20) * N_BLK + jnp.arange(N_BLK, dtype=jnp.int32)[None, :]
    partner_order = jnp.argsort(scores, axis=1, stable=True).astype(jnp.int32)
    return jnp.stack([own_tiles.astype(jnp.int32), partner_order.reshape(-1)])


def draw_remote_count(key, part):
    key = jax.random.fold_in(key, 14)
    key_one, key_two, key_three, key_four = jax.random.split(key, 4)
    nodes = REMOTE_ALL // N_BLK
    spread_top = N_BLK - N_BLK // 4
    product = jax.random.randint(key_one, (nodes,), 0, spread_top + 1)
    product = product * jax.random.randint(key_two, (nodes,), 0, spread_top + 1)
    product = product * jax.random.randint(key_three, (nodes,), 0, spread_top + 1)
    extra = product // (spread_top * spread_top)
    busiest = jax.random.randint(key_four, (), 0, nodes)
    counts = jnp.where(jnp.arange(nodes, dtype=jnp.int32) == busiest, N_BLK, N_BLK // 4 + extra)
    return counts.astype(jnp.int32)


def set_ends(values, rng, least, top_value):
    spot = [jax.random.randint(jax.random.fold_in(rng, axis), (), 0, length) for axis, length in enumerate(values.shape)]
    longest = values.shape.index(max(values.shape))
    neighbour = spot[:longest] + [(spot[longest] + 1) % values.shape[longest]] + spot[longest + 1:]
    return values.at[tuple(spot)].set(least).at[tuple(neighbour)].set(top_value)


def steps_of(key, shape, shards, least, high):
    factor_of, own = 1.0, jax.random.fold_in(key, 6)
    for dim, shards_of in shards:
        heights = jnp.exp(jax.random.uniform(jax.random.fold_in(own, dim), (shards_of,), jnp.float32, least / len(shards), high / len(shards)))
        factor_of = factor_of * jnp.repeat(heights, shape[dim] // shards_of).reshape([-1 if axis == dim else 1 for axis in range(len(shape))])
    return factor_of


def bell_draw(own_key, shape, spread, bound, cuts=(), kind=jnp.bfloat16):
    values = jax.random.normal(own_key, shape, jnp.float32) * spread
    if len(cuts) > 0:
        values = steps_of(own_key, shape, cuts, -0.22, 0.18) * values
    return jnp.clip(values, min=-bound, max=bound).astype(kind)


def setup_inputs(seed: int = 0) -> dict:
    streams_of = jax.random.split(jax.random.key(seed), 13)
    coords = draw_coords(jax.random.fold_in(streams_of[12], 71), 0)
    strain = draw_strain(jax.random.fold_in(streams_of[12], 71), 0)
    history = jnp.clip(1.0 + 2.0 * jax.random.uniform(streams_of[2], (NTILES, PTS), jnp.float32) ** steps_of(streams_of[2], (NTILES, PTS), ((0, 32),), -0.2, 0.2), 1.0, 3.0)
    corner_load = bell_draw(streams_of[3], (CORNER_DOF, NTILES, PTS), 0.06, 0.4, ((1, 32),), jnp.float32)
    tile_count = draw_tile_count(jax.random.fold_in(streams_of[12], 71), 0)
    tile_sub = set_ends(jax.random.randint(streams_of[5], (NTILES,), 0, SUB_DEV), jax.random.fold_in(streams_of[5], 1), 0, SUB_DEV - 1).astype(jnp.int32)
    local_pairs = draw_local_pairs(jax.random.fold_in(streams_of[12], 71), 0)
    send_tile = set_ends(jax.random.randint(streams_of[7], (REMOTE_ALL,), 0, 4), jax.random.fold_in(streams_of[7], 1), 0, 3).astype(jnp.int32)
    remote_pairs = draw_remote_pairs(jax.random.fold_in(streams_of[12], 71), 0)
    remote_count = draw_remote_count(jax.random.fold_in(streams_of[12], 71), 0)
    corner_map = set_ends(jax.random.randint(streams_of[10], (SUB_ALL, CORNER_DOF), 0, COARSE_DEV * N_BLK), jax.random.fold_in(streams_of[10], 1), 0, (COARSE_DEV * N_BLK) - 1).astype(jnp.int32)
    external = bell_draw(streams_of[11], (COARSE_ALL,), 1.0, 6.0, ((0, 32),), jnp.float32)
    return {"coords": coords, "strain": strain, "history": history, "corner_load": corner_load, "tile_count": tile_count, "tile_sub": tile_sub, "local_pairs": local_pairs, "send_tile": send_tile, "remote_pairs": remote_pairs, "remote_count": remote_count, "corner_map": corner_map, "external": external}


gauss_rate = 4.0
keep_share = 0.05
softening = 0.5
group_rows = 64


def pair_block(first, second, weights_on):
    sq_dist = (first[0][:, :, None] - second[0][:, None, :]) ** 2
    sq_dist = sq_dist + (first[1][:, :, None] - second[1][:, None, :]) ** 2
    sq_dist = sq_dist + (first[2][:, :, None] - second[2][:, None, :]) ** 2
    kernel = jnp.exp(-gauss_rate * sq_dist) * first[4][:, :, None] * second[4][:, None, :]
    kernel = kernel * weights_on[:, None, None]
    num_first = jnp.einsum("gpq,gq->gp", kernel, second[3], precision=lax.Precision.HIGHEST)
    den_first = jnp.sum(kernel, axis=2)
    num_second = jnp.einsum("gpq,gp->gq", kernel, first[3], precision=lax.Precision.HIGHEST)
    den_second = jnp.sum(kernel, axis=1)
    return jnp.stack([num_first, den_first]), jnp.stack([num_second, den_second])


def accumulate(tile_data, first_ids, second_ids, weights_on, both_sides, totals):
    count_all = first_ids.shape[0]
    padding = (-count_all) % group_rows
    first_ids = jnp.concatenate([first_ids.astype(jnp.int32), jnp.zeros((padding,), jnp.int32)])
    second_ids = jnp.concatenate([second_ids.astype(jnp.int32), jnp.zeros((padding,), jnp.int32)])
    weights_on = jnp.concatenate([weights_on, jnp.zeros((padding,), jnp.float32)])
    groups = (count_all + padding) // group_rows

    def advance(totals, chosen):
        pick_first, pick_second, weight_now = chosen
        near, far = pair_block(jnp.take(tile_data, pick_first, axis=1), jnp.take(tile_data, pick_second, axis=1), weight_now)
        totals = totals.at[:, pick_first].add(near)
        if both_sides:
            totals = totals.at[:, pick_second].add(far)
        return totals, None

    chosen = (first_ids.reshape(groups, group_rows), second_ids.reshape(groups, group_rows), weights_on.reshape(groups, group_rows))
    totals, unused = lax.scan(advance, totals, chosen)
    return totals


def reference(coords, strain, history, corner_load, tile_count, tile_sub, local_pairs, send_tile, remote_pairs, remote_count, corner_map, external):
    n_nodes = NTILES // TILE_DEV
    positions = jnp.arange(PTS, dtype=jnp.int32)
    valid_mask = (positions[None, :] < tile_count[:, None]).astype(jnp.float32)
    tile_data = jnp.concatenate([coords, strain[None], valid_mask[None]], axis=0)
    nodes = jnp.arange(n_nodes, dtype=jnp.int32)
    ranks = jnp.arange(TILE_DEV, dtype=jnp.int32)

    local_base = jnp.repeat(nodes * TILE_DEV, TILE_DEV)
    local_first = local_pairs[0] + local_base
    local_second = local_pairs[1] + local_base

    upper_nodes = nodes[N_BLK:]
    border_own = (upper_nodes[:, None] * TILE_DEV + ranks[None, :]).reshape(-1)
    border_same = ((upper_nodes[:, None] - N_BLK) * TILE_DEV + ranks[None, :]).reshape(-1)
    border_next = ((upper_nodes[:, None] - N_BLK) * TILE_DEV + ((ranks + 1) % TILE_DEV)[None, :]).reshape(-1)

    remote_node = jnp.repeat(nodes, N_BLK)
    slot_index = jnp.tile(jnp.arange(N_BLK, dtype=jnp.int32), n_nodes)
    remote_live = (slot_index < remote_count[remote_node]).astype(jnp.float32)
    sender = (remote_node // N_BLK) * N_BLK + remote_pairs[1]
    remote_first = remote_node * TILE_DEV + remote_pairs[0]
    remote_second = sender * TILE_DEV + send_tile[sender * N_BLK + remote_node % N_BLK]

    first_ids = jnp.concatenate([local_first, border_own, border_own, remote_first])
    second_ids = jnp.concatenate([local_second, border_same, border_next, remote_second])
    weights_on = jnp.concatenate([jnp.ones((local_first.shape[0] + 2 * border_own.shape[0],), jnp.float32), remote_live])

    totals = jnp.zeros((2, NTILES, PTS), jnp.float32)
    all_tiles = jnp.arange(NTILES, dtype=jnp.int32)
    totals = accumulate(tile_data, all_tiles, all_tiles, jnp.ones((NTILES,), jnp.float32), False, totals)
    totals = accumulate(tile_data, first_ids, second_ids, weights_on, True, totals)

    strain_bar = totals[0] / (totals[1] + 1.0 - valid_mask)
    kappa_new = jnp.maximum(strain_bar, history)
    damage = 1.0 - (keep_share + (1.0 - keep_share) * jnp.exp(-softening * (kappa_new - 1.0))) / kappa_new
    intact = (1.0 - damage) * valid_mask
    tile_part = jnp.einsum("ctp,tp->tc", corner_load, intact, precision=lax.Precision.HIGHEST)
    sub_ids = (all_tiles // TILE_DEV) * SUB_DEV + tile_sub
    sub_part = jax.ops.segment_sum(tile_part, sub_ids, num_segments=SUB_ALL)
    group_of = jnp.arange(SUB_ALL, dtype=jnp.int32) // (SUB_DEV * N_BLK)
    coarse_ids = corner_map + group_of[:, None] * (COARSE_DEV * N_BLK)
    internal = jax.ops.segment_sum(sub_part.reshape(-1), coarse_ids.reshape(-1), num_segments=COARSE_ALL)
    return damage, external - internal
```

```python
import functools
import math

import jax
import jax.numpy as jnp
from jax import lax
from jax.experimental import pallas as pl
from jax.experimental.pallas import tpu as pltpu
from jax.sharding import PartitionSpec as P

gauss_rate = 4.0
keep_share = 0.05
softening = 0.5
coord_scale = math.sqrt(gauss_rate * math.log2(math.e))
far_off = 2048.0
depth = 32
grant = 48 * 1024 * 1024

f32 = jnp.float32
bf16 = jnp.bfloat16
in_vmem = pl.BlockSpec(memory_space=pltpu.VMEM)
in_smem = pl.BlockSpec(memory_space=pltpu.SMEM)


def pieces(value):
    high = value.astype(bf16).astype(f32)
    rest = value - high
    middle = rest.astype(bf16).astype(f32)
    low = (rest - middle).astype(bf16).astype(f32)
    return high, middle, low


def put_rows(rows_ref, tiles, rows):
    for r, row in enumerate(rows):
        for half in range(row.shape[1] // 128):
            rows_ref[half, pl.ds(r, tiles, stride=depth), :] = row[:, half * 128 : (half + 1) * 128]


def point_rows(planes):
    scaled = [p * coord_scale for p in planes[:3]]
    split = [pieces(s) for s in scaled]
    norm = scaled[0] * scaled[0] + scaled[1] * scaled[1] + scaled[2] * scaled[2]
    return split, norm


def build_source(planes, rows_ref, a_ref, s_ref, base):
    tiles = planes[3].shape[0]
    split, norm = point_rows(planes)
    ones = jnp.ones_like(norm)
    zeros = jnp.zeros_like(norm)
    norm = norm + jnp.where(planes[3] > 0.0, 0.0, far_off)
    rows = []
    for high, middle, low in split:
        rows += [high, high, middle, high, low, middle]
    rows += list(pieces(-norm)) + [ones, ones, ones] + [planes[3]]
    rows += [zeros] * (depth - len(rows))
    put_rows(rows_ref, tiles, rows)
    halves = norm.shape[1] // 128

    def one_tile(t, carry):
        for half in range(halves):
            block = rows_ref[half, pl.ds(pl.multiple_of(t * depth, depth), depth), :]
            turned = block.T
            a_ref[base + t, half * 128 : (half + 1) * 128, :] = turned.astype(bf16)
            s_ref[base + t, half * 128 : (half + 1) * 128, :] = jnp.broadcast_to(turned[:, 24:25], (128, 128))
        return carry

    lax.fori_loop(0, tiles, one_tile, 0)


def build_target(planes, rows_ref, b_ref):
    tiles = planes[3].shape[0]
    split, norm = point_rows(planes)
    ones = jnp.ones_like(norm)
    zeros = jnp.zeros_like(norm)
    rows = []
    for high, middle, low in split:
        rows += [2.0 * v for v in (high, middle, high, low, high, middle)]
    rows += [ones, ones, ones] + list(pieces(-norm))
    rows += [zeros] * (depth - len(rows))
    put_rows(rows_ref, tiles, rows)
    halves = norm.shape[1] // 128

    def one_tile(t, carry):
        for half in range(halves):
            block = rows_ref[half, pl.ds(pl.multiple_of(t * depth, depth), depth), :]
            b_ref[t, :, half * 128 : (half + 1) * 128] = block.astype(bf16)
        return carry

    lax.fori_loop(0, tiles, one_tile, 0)


def pair_sums(a, s, b):
    points = a.shape[0]
    width = b.shape[1]
    step = min(points, 128)
    num = jnp.zeros((8, width), f32)
    den = jnp.zeros((8, width), f32)
    for lo in range(0, points, step):
        power = jnp.dot(a[lo : lo + step], b, preferred_element_type=f32)
        weight = jnp.exp2(power)
        load = jnp.concatenate([s[lo : lo + step]] * (width // 128), axis=1)
        den = den + jnp.sum(weight.reshape(step // 8, 8, width), axis=0)
        num = num + jnp.sum((weight * load).reshape(step // 8, 8, width), axis=0)
    return num, den


def pack_kernel(peers, coords, strain, tile_count, send_tile, remote_pairs, remote_count, payload, outbox):
    tiles, points = strain.shape
    payload[0:3] = coords[...]
    lane = lax.broadcasted_iota(jnp.int32, (1, points), 1)
    for t in range(tiles):
        payload[3, t : t + 1, :] = jnp.where(lane < tile_count[t], strain[t : t + 1, :], 0.0)

    def sent(h, carry):
        t = send_tile[h]
        for k in range(4):
            outbox[h, k : k + 1, :] = payload[k, pl.ds(t, 1), :]
        return carry

    def listed(i, carry):
        t = remote_pairs[0, i]
        h = remote_pairs[1, i]
        live = (i < remote_count[0]).astype(f32)
        for k in range(3):
            outbox[h, 4 + k : 5 + k, :] = payload[k, pl.ds(t, 1), :]
        outbox[h, 7:8, :] = payload[3, pl.ds(t, 1), :] * live
        return carry

    lax.fori_loop(0, peers, sent, 0)
    lax.fori_loop(0, peers, listed, 0)


def own_kernel(payload, local_pairs, b_ref, num_ref, den_ref, rows_ref, a_ref, s_ref):
    tiles = payload.shape[1]
    planes = [payload[k] for k in range(4)]
    build_source(planes, rows_ref, a_ref, s_ref, 0)
    build_target(planes, rows_ref, b_ref)

    def own(t, carry):
        num, den = pair_sums(a_ref[t], s_ref[t], b_ref[t])
        num_ref[t] = num
        den_ref[t] = den
        return carry

    lax.fori_loop(0, tiles, own, 0)

    def listed(i, carry):
        one = local_pairs[0, i]
        two = local_pairs[1, i]
        for src, dst in ((one, two), (two, one)):
            num, den = pair_sums(a_ref[src], s_ref[src], b_ref[dst])
            num_ref[dst] = num_ref[dst] + num
            den_ref[dst] = den_ref[dst] + den
        return carry

    lax.fori_loop(0, local_pairs.shape[1], listed, 0)


def rest_kernel(
    peers,
    below,
    above,
    inbox,
    b_ref,
    num_in,
    den_in,
    payload,
    history,
    corner_load,
    tile_sub,
    corner_map,
    send_tile,
    remote_pairs,
    remote_count,
    damage_ref,
    parts_ref,
    rows_ref,
    a_ref,
    s_ref,
    far_rows,
    far_a,
    far_s,
    num_ref,
    den_ref,
    sub_rows,
    map_rows,
):
    tiles, points = history.shape
    num_ref[...] = num_in[...]
    den_ref[...] = den_in[...]

    def border(offset):
        def one(t, carry):
            num = num_ref[t]
            den = den_ref[t]
            other = lax.rem(t + offset, tiles)
            for src in (t, other):
                more_num, more_den = pair_sums(a_ref[src], s_ref[src], b_ref[t])
                num = num + more_num
                den = den + more_den
            num_ref[t] = num
            den_ref[t] = den
            return carry

        lax.fori_loop(0, tiles, one, 0)

    build_source([below[k] for k in range(4)], rows_ref, a_ref, s_ref, 0)
    border(1)
    build_source([above[k] for k in range(4)], rows_ref, a_ref, s_ref, 0)
    border(tiles - 1)

    for which in range(2):
        planes = [
            jnp.concatenate(
                [inbox[half, pl.ds(4 * which + k, peers, stride=8), :] for half in range(points // 128)], axis=1
            )
            for k in range(4)
        ]
        build_source(planes, far_rows, far_a, far_s, which * peers)

    def add_far(src, dst):
        num, den = pair_sums(far_a[src], far_s[src], b_ref[dst])
        num_ref[dst] = num_ref[dst] + num
        den_ref[dst] = den_ref[dst] + den

    def listed(i, carry):
        add_far(remote_pairs[1, i], remote_pairs[0, i])
        return carry

    def named(h, carry):
        add_far(peers + h, send_tile[h])
        return carry

    lax.fori_loop(0, remote_count[0], listed, 0)
    lax.fori_loop(0, peers, named, 0)

    valid = (payload[3] > 0.0).astype(f32)
    num = jnp.sum(num_ref[...], axis=1) * valid
    den = jnp.sum(den_ref[...], axis=1) * valid
    strain_bar = num / (den + 1.0 - valid)
    kappa = jnp.maximum(strain_bar, history[...])
    damage = 1.0 - (keep_share + (1.0 - keep_share) * jnp.exp(-softening * (kappa - 1.0))) / kappa
    damage_ref[...] = damage
    intact = (1.0 - damage) * valid

    for t in range(tiles):
        sub_rows[t : t + 1, :] = jnp.full((1, 128), tile_sub[t], jnp.int32)
    subs, corners = corner_map.shape
    for m in range(subs):
        for c in range(corners):
            r = m * corners + c
            map_rows[r : r + 1, :] = jnp.full((1, 128), corner_map[m, c], jnp.int32)

    folded = corner_load[:, :, 0:128] * intact[None, :, 0:128]
    for half in range(1, points // 128):
        cut = slice(half * 128, (half + 1) * 128)
        folded = folded + corner_load[:, :, cut] * intact[None, :, cut]
    owner = sub_rows[...]
    sums = []
    for m in range(subs):
        chosen = jnp.where((owner == m)[None], folded, 0.0)
        sums.append(jnp.sum(jnp.sum(chosen, axis=1), axis=1, keepdims=True))
    sub_part = jnp.broadcast_to(jnp.concatenate(sums, axis=0), (subs * corners, 128))
    target = map_rows[...] - lax.broadcasted_iota(jnp.int32, (subs * corners, 128), 1)

    def scatter(j, carry):
        parts_ref[pl.ds(j, 1), :] = jnp.sum(jnp.where(target == j * 128, sub_part, 0.0), axis=0, keepdims=True)
        return carry

    lax.fori_loop(0, peers, scatter, 0, unroll=peers <= 8)


def per_device(
    coords,
    strain,
    history,
    corner_load,
    tile_count,
    tile_sub,
    local_pairs,
    send_tile,
    remote_pairs,
    remote_count,
    corner_map,
    external,
):
    tiles, points = strain.shape
    halves = points // 128
    peers = lax.axis_size("blk")
    layers = lax.axis_size("sub")
    subs, corners = corner_map.shape
    params = pltpu.CompilerParams(vmem_limit_bytes=grant)
    block = 2 * points * points

    payload, outbox = pl.pallas_call(
        functools.partial(pack_kernel, peers),
        out_shape=(
            jax.ShapeDtypeStruct((4, tiles, points), f32),
            jax.ShapeDtypeStruct((peers, 8, points), f32),
        ),
        in_specs=[in_vmem] * 2 + [in_smem] * 4,
        out_specs=(in_vmem, in_vmem),
        compiler_params=params,
        name="pack",
    )(coords, strain, tile_count, send_tile, remote_pairs, remote_count)

    up = [(i, i + 1) for i in range(layers - 1)]
    down = [(i + 1, i) for i in range(layers - 1)]
    below = lax.ppermute(payload, "sub", up)
    above = lax.ppermute(payload, "sub", down)
    inbox = lax.all_to_all(outbox, "blk", split_axis=0, concat_axis=0, tiled=True)

    b_own, num, den = pl.pallas_call(
        own_kernel,
        out_shape=(
            jax.ShapeDtypeStruct((tiles, depth, points), bf16),
            jax.ShapeDtypeStruct((tiles, 8, points), f32),
            jax.ShapeDtypeStruct((tiles, 8, points), f32),
        ),
        in_specs=[in_vmem, in_smem],
        out_specs=(in_vmem,) * 3,
        scratch_shapes=[
            pltpu.VMEM((halves, tiles * depth, 128), f32),
            pltpu.VMEM((tiles, points, depth), bf16),
            pltpu.VMEM((tiles, points, 128), f32),
        ],
        compiler_params=params,
        cost_estimate=pl.CostEstimate(
            flops=3 * tiles * block * depth, bytes_accessed=1 << 20, transcendentals=3 * tiles * points * points
        ),
        name="own",
    )(payload, local_pairs)

    inbox = inbox.reshape(peers * 8, halves, 128).transpose(1, 0, 2)
    damage, parts = pl.pallas_call(
        functools.partial(rest_kernel, peers),
        out_shape=(
            jax.ShapeDtypeStruct((tiles, points), f32),
            jax.ShapeDtypeStruct((peers, 128), f32),
        ),
        in_specs=[in_vmem] * 9 + [in_smem] * 5,
        out_specs=(in_vmem,) * 2,
        scratch_shapes=[
            pltpu.VMEM((halves, tiles * depth, 128), f32),
            pltpu.VMEM((tiles, points, depth), bf16),
            pltpu.VMEM((tiles, points, 128), f32),
            pltpu.VMEM((halves, peers * depth, 128), f32),
            pltpu.VMEM((2 * peers, points, depth), bf16),
            pltpu.VMEM((2 * peers, points, 128), f32),
            pltpu.VMEM((tiles, 8, points), f32),
            pltpu.VMEM((tiles, 8, points), f32),
            pltpu.VMEM((tiles, 128), jnp.int32),
            pltpu.VMEM((subs * corners, 128), jnp.int32),
        ],
        compiler_params=params,
        cost_estimate=pl.CostEstimate(
            flops=4 * tiles * block * depth, bytes_accessed=1 << 21, transcendentals=4 * tiles * points * points
        ),
        name="rest",
    )(
        below,
        above,
        inbox,
        b_own,
        num,
        den,
        payload,
        history,
        corner_load,
        tile_sub,
        corner_map,
        send_tile,
        remote_pairs,
        remote_count,
    )
    gathered = lax.all_to_all(parts, "blk", split_axis=0, concat_axis=0, tiled=True)
    return damage, external - jnp.sum(gathered, axis=0)


def solution(mesh):
    placed = (
        P(None, ("sub", "blk"), None),
        P(("sub", "blk"), None),
        P(("sub", "blk"), None),
        P(None, ("sub", "blk"), None),
        P(("sub", "blk")),
        P(("sub", "blk")),
        P(None, ("sub", "blk")),
        P(("sub", "blk")),
        P(None, ("sub", "blk")),
        P(("sub", "blk")),
        P(("sub", "blk"), None),
        P(("sub", "blk")),
    )
    return jax.shard_map(
        per_device,
        mesh=mesh,
        in_specs=placed,
        out_specs=(P(("sub", "blk"), None), P(("sub", "blk"))),
        check_vma=False,
    )
```

```python
import functools
import math

import jax
import jax.numpy as jnp
from jax import lax
from jax.experimental import pallas as pl
from jax.experimental.pallas import tpu as pltpu
from jax.sharding import PartitionSpec as P

gauss_rate = 4.0
keep_share = 0.05
softening = 0.5
coord_scale = math.sqrt(gauss_rate * math.log2(math.e))
far_off = 2048.0
depth = 32
grant = 48 * 1024 * 1024

f32 = jnp.float32
bf16 = jnp.bfloat16
in_vmem = pl.BlockSpec(memory_space=pltpu.VMEM)
anywhere = pl.BlockSpec(memory_space=pl.ANY)


def pieces(value):
    high = value.astype(bf16).astype(f32)
    rest = value - high
    middle = rest.astype(bf16).astype(f32)
    low = (rest - middle).astype(bf16).astype(f32)
    return high, middle, low


def put_rows(rows_ref, tiles, rows):
    for r, row in enumerate(rows):
        for half in range(row.shape[1] // 128):
            rows_ref[half, pl.ds(r, tiles, stride=depth), :] = row[:, half * 128 : (half + 1) * 128]


def point_rows(planes):
    scaled = [p * coord_scale for p in planes[:3]]
    split = [pieces(s) for s in scaled]
    norm = scaled[0] * scaled[0] + scaled[1] * scaled[1] + scaled[2] * scaled[2]
    return split, norm


def build_source(planes, rows_ref, a_ref, s_ref, base):
    tiles = planes[3].shape[0]
    split, norm = point_rows(planes)
    ones = jnp.ones_like(norm)
    zeros = jnp.zeros_like(norm)
    norm = norm + jnp.where(planes[3] > 0.0, 0.0, far_off)
    rows = []
    for high, middle, low in split:
        rows += [high, high, middle, high, low, middle]
    rows += list(pieces(-norm)) + [ones, ones, ones] + [planes[3]]
    rows += [zeros] * (depth - len(rows))
    put_rows(rows_ref, tiles, rows)
    halves = norm.shape[1] // 128

    def one_tile(t, carry):
        for half in range(halves):
            block = rows_ref[half, pl.ds(pl.multiple_of(t * depth, depth), depth), :]
            turned = block.T
            a_ref[base + t, half * 128 : (half + 1) * 128, :] = turned.astype(bf16)
            s_ref[base + t, half * 128 : (half + 1) * 128, :] = jnp.broadcast_to(turned[:, 24:25], (128, 128))
        return carry

    lax.fori_loop(0, tiles, one_tile, 0)


def build_target(planes, rows_ref, b_ref):
    tiles = planes[3].shape[0]
    split, norm = point_rows(planes)
    ones = jnp.ones_like(norm)
    zeros = jnp.zeros_like(norm)
    rows = []
    for high, middle, low in split:
        rows += [2.0 * v for v in (high, middle, high, low, high, middle)]
    rows += [ones, ones, ones] + list(pieces(-norm))
    rows += [zeros] * (depth - len(rows))
    put_rows(rows_ref, tiles, rows)
    halves = norm.shape[1] // 128

    def one_tile(t, carry):
        for half in range(halves):
            block = rows_ref[half, pl.ds(pl.multiple_of(t * depth, depth), depth), :]
            b_ref[t, :, half * 128 : (half + 1) * 128] = block.astype(bf16)
        return carry

    lax.fori_loop(0, tiles, one_tile, 0)


def pair_sums(a, s, b):
    points = a.shape[0]
    width = b.shape[1]
    step = min(points, 128)
    num = jnp.zeros((8, width), f32)
    den = jnp.zeros((8, width), f32)
    for lo in range(0, points, step):
        power = jnp.dot(a[lo : lo + step], b, preferred_element_type=f32)
        weight = jnp.exp2(power)
        load = jnp.concatenate([s[lo : lo + step]] * (width // 128), axis=1)
        den = den + jnp.sum(weight.reshape(step // 8, 8, width), axis=0)
        num = num + jnp.sum((weight * load).reshape(step // 8, 8, width), axis=0)
    return num, den


def fetch(sources, targets, sems):
    copies = [pltpu.make_async_copy(src, dst, sems.at[i]) for i, (src, dst) in enumerate(zip(sources, targets))]
    for copy in copies:
        copy.start()
    return copies


def pack_kernel(
    peers,
    coords,
    strain,
    tile_count_in,
    send_tile_in,
    remote_pairs_in,
    remote_count_in,
    payload,
    outbox,
    strain_here,
    tile_count,
    send_tile,
    remote_pairs,
    remote_count,
    sems,
):
    tiles, points = strain.shape
    copies = fetch(
        (coords, strain, tile_count_in, send_tile_in, remote_pairs_in, remote_count_in),
        (payload.at[0:3], strain_here, tile_count, send_tile, remote_pairs, remote_count),
        sems,
    )
    for copy in copies:
        copy.wait()
    lane = lax.broadcasted_iota(jnp.int32, (1, points), 1)
    for t in range(tiles):
        payload[3, t : t + 1, :] = jnp.where(lane < tile_count[t], strain_here[t : t + 1, :], 0.0)

    def sent(h, carry):
        t = send_tile[h]
        for k in range(4):
            outbox[h, k : k + 1, :] = payload[k, pl.ds(t, 1), :]
        return carry

    def listed(i, carry):
        t = remote_pairs[0, i]
        h = remote_pairs[1, i]
        live = (i < remote_count[0]).astype(f32)
        for k in range(3):
            outbox[h, 4 + k : 5 + k, :] = payload[k, pl.ds(t, 1), :]
        outbox[h, 7:8, :] = payload[3, pl.ds(t, 1), :] * live
        return carry

    lax.fori_loop(0, peers, sent, 0, unroll=peers <= 8)
    lax.fori_loop(0, peers, listed, 0, unroll=peers <= 8)


def own_kernel(payload, local_pairs_in, b_ref, num_ref, den_ref, rows_ref, a_ref, s_ref, local_pairs, sems):
    tiles = payload.shape[1]
    copies = fetch((local_pairs_in,), (local_pairs,), sems)
    planes = [payload[k] for k in range(4)]
    build_source(planes, rows_ref, a_ref, s_ref, 0)
    build_target(planes, rows_ref, b_ref)
    for copy in copies:
        copy.wait()

    def own(step, carry):
        group = [step * 4 + i for i in range(4)]
        sums = [pair_sums(a_ref[t], s_ref[t], b_ref[t]) for t in group]
        for t, (num, den) in zip(group, sums):
            num_ref[t] = num
            den_ref[t] = den
        return carry

    lax.fori_loop(0, tiles // 4, own, 0)

    def listed(step, carry):
        group = []
        for i in range(2):
            one = local_pairs[0, step * 2 + i]
            two = local_pairs[1, step * 2 + i]
            group += [(one, two), (two, one)]
        sums = [pair_sums(a_ref[src], s_ref[src], b_ref[dst]) for src, dst in group]
        for (src, dst), (num, den) in zip(group, sums):
            num_ref[dst] = num_ref[dst] + num
            den_ref[dst] = den_ref[dst] + den
        return carry

    lax.fori_loop(0, local_pairs.shape[1] // 2, listed, 0)


def rest_kernel(
    peers,
    below,
    above,
    inbox,
    b_ref,
    num_in,
    den_in,
    payload,
    history_in,
    corner_load_in,
    external_in,
    tile_sub_in,
    corner_map_in,
    send_tile_in,
    remote_pairs_in,
    remote_count_in,
    damage_ref,
    parts_ref,
    rows_ref,
    a_ref,
    s_ref,
    far_rows,
    far_a,
    far_s,
    num_ref,
    den_ref,
    sub_rows,
    map_rows,
    history,
    corner_load,
    external,
    tile_sub,
    corner_map,
    send_tile,
    remote_pairs,
    remote_count,
    sems,
):
    copies = fetch(
        (
            history_in,
            corner_load_in,
            external_in,
            tile_sub_in,
            corner_map_in,
            send_tile_in,
            remote_pairs_in,
            remote_count_in,
        ),
        (history, corner_load, external, tile_sub, corner_map, send_tile, remote_pairs, remote_count),
        sems,
    )
    tiles, points = history.shape
    num_ref[...] = num_in[...]
    den_ref[...] = den_in[...]

    def border(offset):
        def some(step, carry):
            for t in (2 * step, 2 * step + 1):
                num = num_ref[t]
                den = den_ref[t]
                other = lax.rem(t + offset, tiles)
                for src in (t, other):
                    more_num, more_den = pair_sums(a_ref[src], s_ref[src], b_ref[t])
                    num = num + more_num
                    den = den + more_den
                num_ref[t] = num
                den_ref[t] = den
            return carry

        lax.fori_loop(0, tiles // 2, some, 0)

    build_source([below[k] for k in range(4)], rows_ref, a_ref, s_ref, 0)
    border(1)
    build_source([above[k] for k in range(4)], rows_ref, a_ref, s_ref, 0)
    border(tiles - 1)

    for which in range(2):
        planes = [
            jnp.concatenate(
                [inbox[half, pl.ds(4 * which + k, peers, stride=8), :] for half in range(points // 128)], axis=1
            )
            for k in range(4)
        ]
        build_source(planes, far_rows, far_a, far_s, which * peers)

    for copy in copies:
        copy.wait()

    def far(step, carry):
        group = []
        for i in (2 * step, 2 * step + 1):
            live = (i < remote_count[0]).astype(f32)
            group += [(remote_pairs[1, i], remote_pairs[0, i], live), (peers + i, send_tile[i], None)]
        sums = [pair_sums(far_a[src], far_s[src], b_ref[dst]) for src, dst, live in group]
        for (src, dst, live), (num, den) in zip(group, sums):
            if live is not None:
                num, den = num * live, den * live
            num_ref[dst] = num_ref[dst] + num
            den_ref[dst] = den_ref[dst] + den
        return carry

    lax.fori_loop(0, peers // 2, far, 0)

    valid = (payload[3] > 0.0).astype(f32)
    num = jnp.sum(num_ref[...], axis=1) * valid
    den = jnp.sum(den_ref[...], axis=1) * valid
    strain_bar = num / (den + 1.0 - valid)
    kappa = jnp.maximum(strain_bar, history[...])
    damage = 1.0 - (keep_share + (1.0 - keep_share) * jnp.exp(-softening * (kappa - 1.0))) / kappa
    damage_ref[...] = damage
    intact = (1.0 - damage) * valid

    for t in range(tiles):
        sub_rows[t : t + 1, :] = jnp.full((1, 128), tile_sub[t], jnp.int32)
    subs, corners = corner_map.shape
    for m in range(subs):
        for c in range(corners):
            r = m * corners + c
            map_rows[r : r + 1, :] = jnp.full((1, 128), corner_map[m, c], jnp.int32)

    folded = corner_load[:, :, 0:128] * intact[None, :, 0:128]
    for half in range(1, points // 128):
        cut = slice(half * 128, (half + 1) * 128)
        folded = folded + corner_load[:, :, cut] * intact[None, :, cut]
    owner = sub_rows[...]
    sums = []
    for m in range(subs):
        chosen = jnp.where((owner == m)[None], folded, 0.0)
        sums.append(jnp.sum(jnp.sum(chosen, axis=1), axis=1, keepdims=True))
    sub_part = jnp.broadcast_to(jnp.concatenate(sums, axis=0), (subs * corners, 128))
    target = map_rows[...] - lax.broadcasted_iota(jnp.int32, (subs * corners, 128), 1)

    def scatter(j, carry):
        held = jnp.where(j == lax.axis_index("blk"), external[...], 0.0).reshape(1, 128)
        force = jnp.sum(jnp.where(target == j * 128, sub_part, 0.0), axis=0, keepdims=True)
        parts_ref[pl.ds(j, 1), :] = held - force
        return carry

    lax.fori_loop(0, peers, scatter, 0, unroll=peers <= 8)


def per_device(
    coords,
    strain,
    history,
    corner_load,
    tile_count,
    tile_sub,
    local_pairs,
    send_tile,
    remote_pairs,
    remote_count,
    corner_map,
    external,
):
    tiles, points = strain.shape
    halves = points // 128
    peers = lax.axis_size("blk")
    layers = lax.axis_size("sub")
    subs, corners = corner_map.shape
    params = pltpu.CompilerParams(vmem_limit_bytes=grant)
    block = 2 * points * points

    payload, outbox = pl.pallas_call(
        functools.partial(pack_kernel, peers),
        out_shape=(
            jax.ShapeDtypeStruct((4, tiles, points), f32),
            jax.ShapeDtypeStruct((peers, 8, points), f32),
        ),
        in_specs=[anywhere] * 6,
        out_specs=(in_vmem, in_vmem),
        scratch_shapes=[pltpu.VMEM((tiles, points), f32)]
        + [pltpu.SMEM(v.shape, jnp.int32) for v in (tile_count, send_tile, remote_pairs, remote_count)]
        + [pltpu.SemaphoreType.DMA((6,))],
        compiler_params=params,
        name="pack",
    )(coords, strain, tile_count, send_tile, remote_pairs, remote_count)

    up = [(i, i + 1) for i in range(layers - 1)]
    down = [(i + 1, i) for i in range(layers - 1)]
    below = lax.ppermute(payload, "sub", up)
    above = lax.ppermute(payload, "sub", down)
    inbox = lax.all_to_all(outbox, "blk", split_axis=0, concat_axis=0, tiled=True)

    b_own, num, den = pl.pallas_call(
        own_kernel,
        out_shape=(
            jax.ShapeDtypeStruct((tiles, depth, points), bf16),
            jax.ShapeDtypeStruct((tiles, 8, points), f32),
            jax.ShapeDtypeStruct((tiles, 8, points), f32),
        ),
        in_specs=[in_vmem, anywhere],
        out_specs=(in_vmem,) * 3,
        scratch_shapes=[
            pltpu.VMEM((halves, tiles * depth, 128), f32),
            pltpu.VMEM((tiles, points, depth), bf16),
            pltpu.VMEM((tiles, points, 128), f32),
            pltpu.SMEM(local_pairs.shape, jnp.int32),
            pltpu.SemaphoreType.DMA((1,)),
        ],
        compiler_params=params,
        cost_estimate=pl.CostEstimate(
            flops=3 * tiles * block * depth, bytes_accessed=1 << 20, transcendentals=3 * tiles * points * points
        ),
        name="own",
    )(payload, local_pairs)

    inbox = inbox.reshape(peers * 8, halves, 128).transpose(1, 0, 2)
    damage, parts = pl.pallas_call(
        functools.partial(rest_kernel, peers),
        out_shape=(
            jax.ShapeDtypeStruct((tiles, points), f32),
            jax.ShapeDtypeStruct((peers, 128), f32),
        ),
        in_specs=[in_vmem] * 7 + [anywhere] * 8,
        out_specs=(in_vmem,) * 2,
        scratch_shapes=[
            pltpu.VMEM((halves, tiles * depth, 128), f32),
            pltpu.VMEM((tiles, points, depth), bf16),
            pltpu.VMEM((tiles, points, 128), f32),
            pltpu.VMEM((halves, peers * depth, 128), f32),
            pltpu.VMEM((2 * peers, points, depth), bf16),
            pltpu.VMEM((2 * peers, points, 128), f32),
            pltpu.VMEM((tiles, 8, points), f32),
            pltpu.VMEM((tiles, 8, points), f32),
            pltpu.VMEM((tiles, 128), jnp.int32),
            pltpu.VMEM((subs * corners, 128), jnp.int32),
            pltpu.VMEM(history.shape, f32),
            pltpu.VMEM(corner_load.shape, f32),
            pltpu.VMEM(external.shape, f32),
        ]
        + [pltpu.SMEM(v.shape, jnp.int32) for v in (tile_sub, corner_map, send_tile, remote_pairs, remote_count)]
        + [pltpu.SemaphoreType.DMA((8,))],
        compiler_params=params,
        cost_estimate=pl.CostEstimate(
            flops=4 * tiles * block * depth, bytes_accessed=1 << 21, transcendentals=4 * tiles * points * points
        ),
        name="rest",
    )(
        below,
        above,
        inbox,
        b_own,
        num,
        den,
        payload,
        history,
        corner_load,
        external,
        tile_sub,
        corner_map,
        send_tile,
        remote_pairs,
        remote_count,
    )
    gathered = lax.all_to_all(parts, "blk", split_axis=0, concat_axis=0, tiled=True)
    return damage, jnp.sum(gathered, axis=0)


def solution(mesh):
    placed = (
        P(None, ("sub", "blk"), None),
        P(("sub", "blk"), None),
        P(("sub", "blk"), None),
        P(None, ("sub", "blk"), None),
        P(("sub", "blk")),
        P(("sub", "blk")),
        P(None, ("sub", "blk")),
        P(("sub", "blk")),
        P(None, ("sub", "blk")),
        P(("sub", "blk")),
        P(("sub", "blk"), None),
        P(("sub", "blk")),
    )
    return jax.shard_map(
        per_device,
        mesh=mesh,
        in_specs=placed,
        out_specs=(P(("sub", "blk"), None), P(("sub", "blk"))),
        check_vma=False,
    )
```

```python
import functools
import math

import jax
import jax.numpy as jnp
from jax import lax
from jax.experimental import pallas as pl
from jax.experimental.pallas import tpu as pltpu
from jax.sharding import PartitionSpec as P

gauss_rate = 4.0
keep_share = 0.05
softening = 0.5
coord_scale = math.sqrt(gauss_rate * math.log2(math.e))
far_off = 2048.0
depth = 32
grant = 60 * 1024 * 1024

f32 = jnp.float32
bf16 = jnp.bfloat16
in_vmem = pl.BlockSpec(memory_space=pltpu.VMEM)
in_hbm = pl.BlockSpec(memory_space=pltpu.HBM)


def pieces(value):
    high = value.astype(bf16).astype(f32)
    rest = value - high
    middle = rest.astype(bf16).astype(f32)
    low = (rest - middle).astype(bf16).astype(f32)
    return high, middle, low


def put_rows(rows_ref, tiles, rows):
    for r, row in enumerate(rows):
        for half in range(row.shape[1] // 128):
            rows_ref[half, pl.ds(r, tiles, stride=depth), :] = row[:, half * 128 : (half + 1) * 128]


def point_rows(planes):
    scaled = [p * coord_scale for p in planes[:3]]
    split = [pieces(s) for s in scaled]
    norm = scaled[0] * scaled[0] + scaled[1] * scaled[1] + scaled[2] * scaled[2]
    return split, norm


def build_source(planes, rows_ref, a_ref, s_ref, base):
    tiles = planes[3].shape[0]
    split, norm = point_rows(planes)
    ones = jnp.ones_like(norm)
    zeros = jnp.zeros_like(norm)
    norm = norm + jnp.where(planes[3] > 0.0, 0.0, far_off)
    rows = []
    for high, middle, low in split:
        rows += [high, high, middle, high, low, middle]
    rows += list(pieces(-norm)) + [ones, ones, ones] + [planes[3]]
    rows += [zeros] * (depth - len(rows))
    put_rows(rows_ref, tiles, rows)
    halves = norm.shape[1] // 128

    def some_tiles(step, carry):
        for t in [step * 4 + i for i in range(4)]:
            for half in range(halves):
                block = rows_ref[half, pl.ds(pl.multiple_of(t * depth, depth), depth), :]
                turned = block.T
                a_ref[base + t, half * 128 : (half + 1) * 128, :] = turned.astype(bf16)
                s_ref[base + t, half * 128 : (half + 1) * 128, :] = jnp.broadcast_to(turned[:, 24:25], (128, 128))
        return carry

    lax.fori_loop(0, tiles // 4, some_tiles, 0)


def build_target(planes, rows_ref, b_ref):
    tiles = planes[3].shape[0]
    split, norm = point_rows(planes)
    ones = jnp.ones_like(norm)
    zeros = jnp.zeros_like(norm)
    rows = []
    for high, middle, low in split:
        rows += [2.0 * v for v in (high, middle, high, low, high, middle)]
    rows += [ones, ones, ones] + list(pieces(-norm))
    rows += [zeros] * (depth - len(rows))
    put_rows(rows_ref, tiles, rows)
    halves = norm.shape[1] // 128

    def some_tiles(step, carry):
        for t in [step * 4 + i for i in range(4)]:
            for half in range(halves):
                block = rows_ref[half, pl.ds(pl.multiple_of(t * depth, depth), depth), :]
                b_ref[t, :, half * 128 : (half + 1) * 128] = block.astype(bf16)
        return carry

    lax.fori_loop(0, tiles // 4, some_tiles, 0)


def pair_sums(a, s, b):
    points = a.shape[0]
    width = b.shape[1]
    step = min(points, 128)
    num = jnp.zeros((8, width), f32)
    den = jnp.zeros((8, width), f32)
    for lo in range(0, points, step):
        power = jnp.dot(a[lo : lo + step], b, preferred_element_type=f32)
        weight = jnp.exp2(power)
        load = jnp.concatenate([s[lo : lo + step]] * (width // 128), axis=1)
        den = den + jnp.sum(weight.reshape(step // 8, 8, width), axis=0)
        num = num + jnp.sum((weight * load).reshape(step // 8, 8, width), axis=0)
    return num, den


def fetch(sources, targets, sems):
    copies = [pltpu.make_async_copy(src, dst, sems.at[i]) for i, (src, dst) in enumerate(zip(sources, targets))]
    for copy in copies:
        copy.start()
    return copies


def pack_kernel(
    peers,
    coords,
    strain,
    tile_count_in,
    send_tile_in,
    remote_pairs_in,
    remote_count_in,
    payload,
    outbox,
    strain_here,
    tile_count,
    send_tile,
    remote_pairs,
    remote_count,
    sems,
):
    tiles, points = strain.shape
    copies = fetch(
        (coords, strain, tile_count_in, send_tile_in, remote_pairs_in, remote_count_in),
        (payload.at[0:3], strain_here, tile_count, send_tile, remote_pairs, remote_count),
        sems,
    )
    for copy in copies:
        copy.wait()
    lane = lax.broadcasted_iota(jnp.int32, (1, points), 1)
    for t in range(tiles):
        payload[3, t : t + 1, :] = jnp.where(lane < tile_count[t], strain_here[t : t + 1, :], 0.0)

    def sent(h, carry):
        t = send_tile[h]
        for k in range(4):
            outbox[pl.ds(8 * h + k, 1), :] = payload[k, pl.ds(t, 1), :]
        return carry

    def listed(i, carry):
        t = remote_pairs[0, i]
        h = remote_pairs[1, i]
        live = (i < remote_count[0]).astype(f32)
        for k in range(3):
            outbox[pl.ds(8 * h + 4 + k, 1), :] = payload[k, pl.ds(t, 1), :]
        outbox[pl.ds(8 * h + 7, 1), :] = payload[3, pl.ds(t, 1), :] * live
        return carry

    lax.fori_loop(0, peers, sent, 0, unroll=peers <= 8)
    lax.fori_loop(0, peers, listed, 0, unroll=peers <= 8)


def own_kernel(payload, local_pairs_in, b_ref, num_ref, den_ref, rows_ref, a_ref, s_ref, local_pairs, sems):
    tiles = payload.shape[1]
    copies = fetch((local_pairs_in,), (local_pairs,), sems)
    planes = [payload[k] for k in range(4)]
    build_source(planes, rows_ref, a_ref, s_ref, 0)
    build_target(planes, rows_ref, b_ref)
    for copy in copies:
        copy.wait()

    def own(step, carry):
        group = [step * 4 + i for i in range(4)]
        sums = [pair_sums(a_ref[t], s_ref[t], b_ref[t]) for t in group]
        for t, (num, den) in zip(group, sums):
            num_ref[t] = num
            den_ref[t] = den
        return carry

    lax.fori_loop(0, tiles // 4, own, 0)

    def listed(step, carry):
        group = []
        for i in range(2):
            one = local_pairs[0, step * 2 + i]
            two = local_pairs[1, step * 2 + i]
            group += [(one, two), (two, one)]
        sums = [pair_sums(a_ref[src], s_ref[src], b_ref[dst]) for src, dst in group]
        for (src, dst), (num, den) in zip(group, sums):
            num_ref[dst] = num_ref[dst] + num
            den_ref[dst] = den_ref[dst] + den
        return carry

    lax.fori_loop(0, local_pairs.shape[1] // 2, listed, 0)


def rest_kernel(
    peers,
    layers_in,
    inbox_in,
    b_in,
    num_in,
    den_in,
    payload_in,
    history_in,
    corner_load_in,
    external_in,
    tile_sub_in,
    corner_map_in,
    send_tile_in,
    remote_pairs_in,
    remote_count_in,
    damage_ref,
    parts_ref,
    rows_ref,
    a_ref,
    s_ref,
    far_rows,
    far_a,
    far_s,
    sub_rows,
    map_rows,
    below,
    above,
    inbox,
    b_ref,
    num_ref,
    den_ref,
    own_strain,
    history,
    corner_load,
    external,
    tile_sub,
    corner_map,
    send_tile,
    remote_pairs,
    remote_count,
    layer_sems,
    sum_sems,
    sems,
):
    tiles, points = history.shape
    count = layers_in.shape[0]
    layer = lax.axis_index("sub")
    from_below, from_above = fetch(
        (layers_in.at[jnp.maximum(layer - 1, 0)], layers_in.at[jnp.minimum(layer + 1, count - 1)]),
        (below, above),
        layer_sems,
    )
    sum_copies = fetch((b_in, num_in, den_in), (b_ref, num_ref, den_ref), sum_sems)
    halves = points // 128
    copies = fetch(
        [inbox_in.at[:, half * 128 : (half + 1) * 128] for half in range(halves)]
        + [
            payload_in.at[3],
            history_in,
            corner_load_in,
            external_in,
            tile_sub_in,
            corner_map_in,
            send_tile_in,
            remote_pairs_in,
            remote_count_in,
        ],
        [inbox.at[half] for half in range(halves)]
        + [own_strain, history, corner_load, external, tile_sub, corner_map, send_tile, remote_pairs, remote_count],
        sems,
    )

    def border(offset):
        def some(step, carry):
            for t in (2 * step, 2 * step + 1):
                num = num_ref[t]
                den = den_ref[t]
                other = lax.rem(t + offset, tiles)
                for src in (t, other):
                    more_num, more_den = pair_sums(a_ref[src], s_ref[src], b_ref[t])
                    num = num + more_num
                    den = den + more_den
                num_ref[t] = num
                den_ref[t] = den
            return carry

        lax.fori_loop(0, tiles // 2, some, 0)

    from_below.wait()
    build_source([below[k] for k in range(4)], rows_ref, a_ref, s_ref, 0)
    for copy in sum_copies:
        copy.wait()

    @pl.when(layer > 0)
    def lower():
        border(1)

    from_above.wait()

    @pl.when(layer < count - 1)
    def upper():
        build_source([above[k] for k in range(4)], rows_ref, a_ref, s_ref, 0)
        border(tiles - 1)

    for copy in copies:
        copy.wait()
    for which in range(2):
        planes = [
            jnp.concatenate(
                [inbox[half, pl.ds(4 * which + k, peers, stride=8), :] for half in range(points // 128)], axis=1
            )
            for k in range(4)
        ]
        build_source(planes, far_rows, far_a, far_s, which * peers)

    def far(step, carry):
        group = []
        for i in (2 * step, 2 * step + 1):
            live = (i < remote_count[0]).astype(f32)
            group += [(remote_pairs[1, i], remote_pairs[0, i], live), (peers + i, send_tile[i], None)]
        sums = [pair_sums(far_a[src], far_s[src], b_ref[dst]) for src, dst, live in group]
        for (src, dst, live), (num, den) in zip(group, sums):
            if live is not None:
                num, den = num * live, den * live
            num_ref[dst] = num_ref[dst] + num
            den_ref[dst] = den_ref[dst] + den
        return carry

    lax.fori_loop(0, peers // 2, far, 0)

    valid = (own_strain[...] > 0.0).astype(f32)
    num = jnp.sum(num_ref[...], axis=1) * valid
    den = jnp.sum(den_ref[...], axis=1) * valid
    strain_bar = num / (den + 1.0 - valid)
    kappa = jnp.maximum(strain_bar, history[...])
    damage = 1.0 - (keep_share + (1.0 - keep_share) * jnp.exp(-softening * (kappa - 1.0))) / kappa
    damage_ref[...] = damage
    intact = (1.0 - damage) * valid

    for t in range(tiles):
        sub_rows[t : t + 1, :] = jnp.full((1, 128), tile_sub[t], jnp.int32)
    subs, corners = corner_map.shape
    for m in range(subs):
        for c in range(corners):
            r = m * corners + c
            map_rows[r : r + 1, :] = jnp.full((1, 128), corner_map[m, c], jnp.int32)

    folded = corner_load[:, :, 0:128] * intact[None, :, 0:128]
    for half in range(1, points // 128):
        cut = slice(half * 128, (half + 1) * 128)
        folded = folded + corner_load[:, :, cut] * intact[None, :, cut]
    owner = sub_rows[...]
    sums = []
    for m in range(subs):
        chosen = jnp.where((owner == m)[None], folded, 0.0)
        sums.append(jnp.sum(jnp.sum(chosen, axis=1), axis=1, keepdims=True))
    sub_part = jnp.broadcast_to(jnp.concatenate(sums, axis=0), (subs * corners, 128))
    target = map_rows[...] - lax.broadcasted_iota(jnp.int32, (subs * corners, 128), 1)

    def scatter(j, carry):
        held = jnp.where(j == lax.axis_index("blk"), external[...], 0.0).reshape(1, 128)
        force = jnp.sum(jnp.where(target == j * 128, sub_part, 0.0), axis=0, keepdims=True)
        parts_ref[pl.ds(j, 1), :] = held - force
        return carry

    lax.fori_loop(0, peers, scatter, 0, unroll=peers <= 8)


def per_device(
    coords,
    strain,
    history,
    corner_load,
    tile_count,
    tile_sub,
    local_pairs,
    send_tile,
    remote_pairs,
    remote_count,
    corner_map,
    external,
):
    tiles, points = strain.shape
    halves = points // 128
    peers = lax.axis_size("blk")
    subs, corners = corner_map.shape
    params = pltpu.CompilerParams(vmem_limit_bytes=grant)
    block = 2 * points * points

    payload, outbox = pl.pallas_call(
        functools.partial(pack_kernel, peers),
        out_shape=(
            jax.ShapeDtypeStruct((4, tiles, points), f32),
            jax.ShapeDtypeStruct((peers * 8, points), f32),
        ),
        in_specs=[in_hbm] * 6,
        out_specs=(in_vmem, in_vmem),
        scratch_shapes=[pltpu.VMEM((tiles, points), f32)]
        + [pltpu.SMEM(v.shape, jnp.int32) for v in (tile_count, send_tile, remote_pairs, remote_count)]
        + [pltpu.SemaphoreType.DMA((6,))],
        compiler_params=params,
        name="pack",
    )(coords, strain, tile_count, send_tile, remote_pairs, remote_count)

    layers = lax.all_gather(payload, "sub")
    inbox = lax.all_to_all(outbox, "blk", split_axis=0, concat_axis=0, tiled=True)

    b_own, num, den = pl.pallas_call(
        own_kernel,
        out_shape=(
            jax.ShapeDtypeStruct((tiles, depth, points), bf16),
            jax.ShapeDtypeStruct((tiles, 8, points), f32),
            jax.ShapeDtypeStruct((tiles, 8, points), f32),
        ),
        in_specs=[in_vmem, in_hbm],
        out_specs=(in_vmem,) * 3,
        scratch_shapes=[
            pltpu.VMEM((halves, tiles * depth, 128), f32),
            pltpu.VMEM((tiles, points, depth), bf16),
            pltpu.VMEM((tiles, points, 128), f32),
            pltpu.SMEM(local_pairs.shape, jnp.int32),
            pltpu.SemaphoreType.DMA((1,)),
        ],
        compiler_params=params,
        cost_estimate=pl.CostEstimate(
            flops=3 * tiles * block * depth, bytes_accessed=1 << 20, transcendentals=3 * tiles * points * points
        ),
        name="own",
    )(payload, local_pairs)

    damage, parts = pl.pallas_call(
        functools.partial(rest_kernel, peers),
        out_shape=(
            jax.ShapeDtypeStruct((tiles, points), f32),
            jax.ShapeDtypeStruct((peers, 128), f32),
        ),
        in_specs=[in_hbm] * 14,
        out_specs=(in_vmem,) * 2,
        scratch_shapes=[
            pltpu.VMEM((halves, tiles * depth, 128), f32),
            pltpu.VMEM((tiles, points, depth), bf16),
            pltpu.VMEM((tiles, points, 128), f32),
            pltpu.VMEM((halves, peers * depth, 128), f32),
            pltpu.VMEM((2 * peers, points, depth), bf16),
            pltpu.VMEM((2 * peers, points, 128), f32),
            pltpu.VMEM((tiles, 128), jnp.int32),
            pltpu.VMEM((subs * corners, 128), jnp.int32),
            pltpu.VMEM(payload.shape, f32),
            pltpu.VMEM(payload.shape, f32),
            pltpu.VMEM((halves, peers * 8, 128), f32),
            pltpu.VMEM(b_own.shape, bf16),
            pltpu.VMEM(num.shape, f32),
            pltpu.VMEM(den.shape, f32),
            pltpu.VMEM(strain.shape, f32),
            pltpu.VMEM(history.shape, f32),
            pltpu.VMEM(corner_load.shape, f32),
            pltpu.VMEM(external.shape, f32),
        ]
        + [pltpu.SMEM(v.shape, jnp.int32) for v in (tile_sub, corner_map, send_tile, remote_pairs, remote_count)]
        + [pltpu.SemaphoreType.DMA((n,)) for n in (2, 3, 9 + halves)],
        compiler_params=params,
        cost_estimate=pl.CostEstimate(
            flops=4 * tiles * block * depth, bytes_accessed=1 << 21, transcendentals=4 * tiles * points * points
        ),
        name="rest",
    )(
        layers,
        inbox,
        b_own,
        num,
        den,
        payload,
        history,
        corner_load,
        external,
        tile_sub,
        corner_map,
        send_tile,
        remote_pairs,
        remote_count,
    )
    gathered = lax.all_to_all(parts, "blk", split_axis=0, concat_axis=0, tiled=True)
    return damage, jnp.sum(gathered, axis=0)


def solution(mesh):
    placed = (
        P(None, ("sub", "blk"), None),
        P(("sub", "blk"), None),
        P(("sub", "blk"), None),
        P(None, ("sub", "blk"), None),
        P(("sub", "blk")),
        P(("sub", "blk")),
        P(None, ("sub", "blk")),
        P(("sub", "blk")),
        P(None, ("sub", "blk")),
        P(("sub", "blk")),
        P(("sub", "blk"), None),
        P(("sub", "blk")),
    )
    return jax.shard_map(
        per_device,
        mesh=mesh,
        in_specs=placed,
        out_specs=(P(("sub", "blk"), None), P(("sub", "blk"))),
        check_vma=False,
    )
```

```python
import functools
import math

import jax
import jax.numpy as jnp
from jax import lax
from jax.experimental import pallas as pl
from jax.experimental.pallas import tpu as pltpu
from jax.sharding import PartitionSpec as P

gauss_rate = 4.0
keep_share = 0.05
softening = 0.5
coord_scale = math.sqrt(gauss_rate * math.log2(math.e))
far_off = 2048.0
depth = 32
grant = 60 * 1024 * 1024

f32 = jnp.float32
bf16 = jnp.bfloat16
in_vmem = pl.BlockSpec(memory_space=pltpu.VMEM)
in_hbm = pl.BlockSpec(memory_space=pltpu.HBM)


def pieces(value):
    high = value.astype(bf16).astype(f32)
    rest = value - high
    middle = rest.astype(bf16).astype(f32)
    low = (rest - middle).astype(bf16).astype(f32)
    return high, middle, low


def put_rows(rows_ref, base, rows):
    for r, row in enumerate(rows):
        tiles = row.shape[0]
        for half in range(row.shape[1] // 128):
            rows_ref[half, pl.ds(base * depth + r, tiles, stride=depth), :] = row[:, half * 128 : (half + 1) * 128]


def point_rows(planes):
    scaled = [p * coord_scale for p in planes[:3]]
    split = [pieces(s) for s in scaled]
    norm = scaled[0] * scaled[0] + scaled[1] * scaled[1] + scaled[2] * scaled[2]
    return split, norm


def put_source(planes, rows_ref, base):
    split, norm = point_rows(planes)
    ones = jnp.ones_like(norm)
    norm = norm + jnp.where(planes[3] > 0.0, 0.0, far_off)
    rows = []
    for high, middle, low in split:
        rows += [high, high, middle, high, low, middle]
    rows += list(pieces(-norm)) + [ones, ones, ones] + [planes[3]]
    rows += [jnp.zeros_like(norm)] * (depth - len(rows))
    put_rows(rows_ref, base, rows)


def put_target(planes, rows_ref):
    split, norm = point_rows(planes)
    ones = jnp.ones_like(norm)
    rows = []
    for high, middle, low in split:
        rows += [2.0 * v for v in (high, middle, high, low, high, middle)]
    rows += [ones, ones, ones] + list(pieces(-norm))
    rows += [jnp.zeros_like(norm)] * (depth - len(rows))
    put_rows(rows_ref, 0, rows)


def turn_group(rows_ref, group):
    rows = pl.ds(pl.multiple_of(group * 128, 128), 128)
    turned = jnp.concatenate([rows_ref[half, rows, :].T for half in range(rows_ref.shape[0])], axis=0)
    left = turned.astype(bf16)
    column = lax.broadcasted_iota(jnp.int32, (1, 128), 1) // depth
    operands = []
    for j in range(4):
        mask = (column == j).astype(f32).astype(bf16)
        lane = depth * j + 24
        operands.append((left * mask, jnp.broadcast_to(turned[:, lane : lane + 1], turned.shape)))
    return operands


def pair_sums(a, s, b):
    points = a.shape[0]
    width = b.shape[1]
    weight = jnp.exp2(jnp.dot(a, b, preferred_element_type=f32))
    load = jnp.concatenate([s] * (width // 128), axis=1)
    den = jnp.sum(weight.reshape(points // 8, 8, width), axis=0)
    num = jnp.sum((weight * load).reshape(points // 8, 8, width), axis=0)
    return num, den


def fetch(sources, targets, sems):
    copies = [pltpu.make_async_copy(src, dst, sems.at[i]) for i, (src, dst) in enumerate(zip(sources, targets))]
    for copy in copies:
        copy.start()
    return copies


def pack_kernel(
    peers,
    coords,
    strain,
    tile_count_in,
    send_tile_in,
    remote_pairs_in,
    remote_count_in,
    payload,
    outbox,
    strain_here,
    tile_count,
    send_tile,
    remote_pairs,
    remote_count,
    sems,
):
    tiles, points = strain.shape
    copies = fetch(
        (coords, strain, tile_count_in, send_tile_in, remote_pairs_in, remote_count_in),
        (payload.at[0:3], strain_here, tile_count, send_tile, remote_pairs, remote_count),
        sems,
    )
    for copy in copies:
        copy.wait()
    lane = lax.broadcasted_iota(jnp.int32, (1, points), 1)
    for t in range(tiles):
        payload[3, t : t + 1, :] = jnp.where(lane < tile_count[t], strain_here[t : t + 1, :], 0.0)

    def sent(h, carry):
        t = send_tile[h]
        for k in range(4):
            outbox[pl.ds(8 * h + k, 1), :] = payload[k, pl.ds(t, 1), :]
        return carry

    def listed(i, carry):
        t = remote_pairs[0, i]
        h = remote_pairs[1, i]
        live = (i < remote_count[0]).astype(f32)
        for k in range(3):
            outbox[pl.ds(8 * h + 4 + k, 1), :] = payload[k, pl.ds(t, 1), :]
        outbox[pl.ds(8 * h + 7, 1), :] = payload[3, pl.ds(t, 1), :] * live
        return carry

    lax.fori_loop(0, peers, sent, 0, unroll=peers <= 8)
    lax.fori_loop(0, peers, listed, 0, unroll=peers <= 8)


def own_kernel(
    payload, local_pairs_in, b_out, num_ref, den_ref, rows_ref, a_ref, s_ref, b_ref, local_pairs, sems, b_sems
):
    tiles = payload.shape[1]
    copies = fetch((local_pairs_in,), (local_pairs,), sems)
    planes = [payload[k] for k in range(4)]
    put_target(planes, rows_ref)

    def set_target(group, carry):
        for t in [group * 4 + i for i in range(4)]:
            rows = pl.ds(pl.multiple_of(t * depth, depth), depth)
            for half in range(rows_ref.shape[0]):
                block = rows_ref[half, rows, :].astype(bf16)
                for j in range(4):
                    b_ref[t, depth * j : depth * (j + 1), half * 128 : (half + 1) * 128] = block
        return carry

    lax.fori_loop(0, tiles // 4, set_target, 0)
    b_copies = fetch((b_ref.at[:, 0:depth, :],), (b_out,), b_sems)
    put_source(planes, rows_ref, 0)
    for copy in copies:
        copy.wait()

    def own(group, carry):
        for i, (a, s) in enumerate(turn_group(rows_ref, group)):
            t = group * 4 + i
            a_ref[t] = a
            s_ref[t] = s
            num, den = pair_sums(a, s, b_ref[t])
            num_ref[t] = num
            den_ref[t] = den
        return carry

    lax.fori_loop(0, tiles // 4, own, 0)

    def listed(step, carry):
        group = []
        for i in range(4):
            one = local_pairs[0, step * 4 + i]
            two = local_pairs[1, step * 4 + i]
            group += [(one, two), (two, one)]
        sums = [pair_sums(a_ref[src], s_ref[src], b_ref[dst]) for src, dst in group]
        for (src, dst), (num, den) in zip(group, sums):
            num_ref[dst] = num_ref[dst] + num
            den_ref[dst] = den_ref[dst] + den
        return carry

    lax.fori_loop(0, local_pairs.shape[1] // 4, listed, 0)
    for copy in b_copies:
        copy.wait()


def rest_kernel(
    peers,
    below_in,
    above_in,
    inbox_in,
    b_in,
    num_in,
    den_in,
    payload_in,
    history_in,
    corner_load_in,
    external_in,
    tile_sub_in,
    corner_map_in,
    send_tile_in,
    remote_pairs_in,
    remote_count_in,
    damage_ref,
    parts_ref,
    rows_ref,
    far_rows,
    sub_rows,
    map_rows,
    below,
    above,
    inbox,
    b_ref,
    num_ref,
    den_ref,
    own_strain,
    history,
    corner_load,
    external,
    tile_sub,
    corner_map,
    send_tile,
    remote_pairs,
    remote_count,
    far_tile,
    far_live,
    layer_sems,
    sum_sems,
    sems,
):
    tiles, points = history.shape
    count = lax.axis_size("sub")
    layer = lax.axis_index("sub")
    from_below, from_above = fetch((below_in, above_in), (below, above), layer_sems)
    sum_copies = fetch(
        [b_in] * 4 + [num_in, den_in],
        [b_ref.at[:, depth * j : depth * (j + 1), :] for j in range(4)] + [num_ref, den_ref],
        sum_sems,
    )
    halves = points // 128
    copies = fetch(
        [inbox_in.at[:, half * 128 : (half + 1) * 128] for half in range(halves)]
        + [
            payload_in.at[3],
            history_in,
            corner_load_in,
            external_in,
            tile_sub_in,
            corner_map_in,
            send_tile_in,
            remote_pairs_in,
            remote_count_in,
        ],
        [inbox.at[half] for half in range(halves)]
        + [own_strain, history, corner_load, external, tile_sub, corner_map, send_tile, remote_pairs, remote_count],
        sems,
    )

    def border(shift):
        def some(group, carry):
            sums = {}
            for i, (a, s) in enumerate(turn_group(rows_ref, group)):
                for place in (i, i + shift):
                    t = lax.rem(group * 4 + place + tiles, tiles)
                    num, den = pair_sums(a, s, b_ref[t])
                    if place in sums:
                        num, den = sums[place][1] + num, sums[place][2] + den
                    sums[place] = (t, num, den)
            for t, num, den in sums.values():
                num_ref[t] = num_ref[t] + num
                den_ref[t] = den_ref[t] + den
            return carry

        lax.fori_loop(0, tiles // 4, some, 0)

    from_below.wait()
    put_source([below[k] for k in range(4)], rows_ref, 0)
    for copy in sum_copies:
        copy.wait()

    @pl.when(layer > 0)
    def lower():
        border(-1)

    from_above.wait()

    @pl.when(layer < count - 1)
    def upper():
        put_source([above[k] for k in range(4)], rows_ref, 0)
        border(1)

    for copy in copies:
        copy.wait()
    for which in range(2):
        planes = [
            jnp.concatenate(
                [inbox[half, pl.ds(4 * which + k, peers, stride=8), :] for half in range(points // 128)], axis=1
            )
            for k in range(4)
        ]
        put_source(planes, far_rows, which * peers)

    def place(i, carry):
        h = remote_pairs[1, i]
        far_tile[h] = remote_pairs[0, i]
        far_live[h] = (i < remote_count[0]).astype(jnp.int32)
        far_tile[peers + i] = send_tile[i]
        far_live[peers + i] = 1
        return carry

    lax.fori_loop(0, peers, place, 0, unroll=peers <= 8)

    def far(group, carry):
        for i, (a, s) in enumerate(turn_group(far_rows, group)):
            t = far_tile[group * 4 + i]
            live = far_live[group * 4 + i].astype(f32)
            num, den = pair_sums(a, s, b_ref[t])
            num_ref[t] = num_ref[t] + num * live
            den_ref[t] = den_ref[t] + den * live
        return carry

    lax.fori_loop(0, 2 * peers // 4, far, 0)

    valid = (own_strain[...] > 0.0).astype(f32)
    num = jnp.sum(num_ref[...], axis=1) * valid
    den = jnp.sum(den_ref[...], axis=1) * valid
    strain_bar = num / (den + 1.0 - valid)
    kappa = jnp.maximum(strain_bar, history[...])
    damage = 1.0 - (keep_share + (1.0 - keep_share) * jnp.exp(-softening * (kappa - 1.0))) / kappa
    damage_ref[...] = damage
    intact = (1.0 - damage) * valid

    for t in range(tiles):
        sub_rows[t : t + 1, :] = jnp.full((1, 128), tile_sub[t], jnp.int32)
    subs, corners = corner_map.shape
    for m in range(subs):
        for c in range(corners):
            r = m * corners + c
            map_rows[r : r + 1, :] = jnp.full((1, 128), corner_map[m, c], jnp.int32)

    folded = corner_load[:, :, 0:128] * intact[None, :, 0:128]
    for half in range(1, points // 128):
        cut = slice(half * 128, (half + 1) * 128)
        folded = folded + corner_load[:, :, cut] * intact[None, :, cut]
    owner = sub_rows[...]
    sums = []
    for m in range(subs):
        chosen = jnp.where((owner == m)[None], folded, 0.0)
        sums.append(jnp.sum(jnp.sum(chosen, axis=1), axis=1, keepdims=True))
    sub_part = jnp.broadcast_to(jnp.concatenate(sums, axis=0), (subs * corners, 128))
    target = map_rows[...] - lax.broadcasted_iota(jnp.int32, (subs * corners, 128), 1)

    def scatter(j, carry):
        held = jnp.where(j == lax.axis_index("blk"), external[...], 0.0).reshape(1, 128)
        force = jnp.sum(jnp.where(target == j * 128, sub_part, 0.0), axis=0, keepdims=True)
        parts_ref[pl.ds(j, 1), :] = held - force
        return carry

    lax.fori_loop(0, peers, scatter, 0, unroll=peers <= 8)


def per_device(
    coords,
    strain,
    history,
    corner_load,
    tile_count,
    tile_sub,
    local_pairs,
    send_tile,
    remote_pairs,
    remote_count,
    corner_map,
    external,
):
    tiles, points = strain.shape
    halves = points // 128
    peers = lax.axis_size("blk")
    subs, corners = corner_map.shape
    params = pltpu.CompilerParams(vmem_limit_bytes=grant)
    block = 2 * points * points

    payload, outbox = pl.pallas_call(
        functools.partial(pack_kernel, peers),
        out_shape=(
            jax.ShapeDtypeStruct((4, tiles, points), f32),
            jax.ShapeDtypeStruct((peers * 8, points), f32),
        ),
        in_specs=[in_hbm] * 6,
        out_specs=(in_vmem, in_vmem),
        scratch_shapes=[pltpu.VMEM((tiles, points), f32)]
        + [pltpu.SMEM(v.shape, jnp.int32) for v in (tile_count, send_tile, remote_pairs, remote_count)]
        + [pltpu.SemaphoreType.DMA((6,))],
        compiler_params=params,
        name="pack",
    )(coords, strain, tile_count, send_tile, remote_pairs, remote_count)

    layers = lax.axis_size("sub")
    below = lax.ppermute(payload, "sub", [(i, i + 1) for i in range(layers - 1)])
    above = lax.ppermute(payload, "sub", [(i + 1, i) for i in range(layers - 1)])
    inbox = lax.all_to_all(outbox, "blk", split_axis=0, concat_axis=0, tiled=True)

    b_own, num, den = pl.pallas_call(
        own_kernel,
        out_shape=(
            jax.ShapeDtypeStruct((tiles, depth, points), bf16),
            jax.ShapeDtypeStruct((tiles, 8, points), f32),
            jax.ShapeDtypeStruct((tiles, 8, points), f32),
        ),
        in_specs=[in_vmem, in_hbm],
        out_specs=(in_hbm, in_vmem, in_vmem),
        scratch_shapes=[
            pltpu.VMEM((halves, tiles * depth, 128), f32),
            pltpu.VMEM((tiles, points, 4 * depth), bf16),
            pltpu.VMEM((tiles, points, 128), f32),
            pltpu.VMEM((tiles, 4 * depth, points), bf16),
            pltpu.SMEM(local_pairs.shape, jnp.int32),
            pltpu.SemaphoreType.DMA((1,)),
            pltpu.SemaphoreType.DMA((1,)),
        ],
        compiler_params=params,
        cost_estimate=pl.CostEstimate(
            flops=3 * tiles * block * depth, bytes_accessed=1 << 20, transcendentals=3 * tiles * points * points
        ),
        name="own",
    )(payload, local_pairs)

    damage, parts = pl.pallas_call(
        functools.partial(rest_kernel, peers),
        out_shape=(
            jax.ShapeDtypeStruct((tiles, points), f32),
            jax.ShapeDtypeStruct((peers, 128), f32),
        ),
        in_specs=[in_hbm] * 15,
        out_specs=(in_vmem,) * 2,
        scratch_shapes=[
            pltpu.VMEM((halves, tiles * depth, 128), f32),
            pltpu.VMEM((halves, 2 * peers * depth, 128), f32),
            pltpu.VMEM((tiles, 128), jnp.int32),
            pltpu.VMEM((subs * corners, 128), jnp.int32),
            pltpu.VMEM(payload.shape, f32),
            pltpu.VMEM(payload.shape, f32),
            pltpu.VMEM((halves, peers * 8, 128), f32),
            pltpu.VMEM((tiles, 4 * depth, points), bf16),
            pltpu.VMEM(num.shape, f32),
            pltpu.VMEM(den.shape, f32),
            pltpu.VMEM(strain.shape, f32),
            pltpu.VMEM(history.shape, f32),
            pltpu.VMEM(corner_load.shape, f32),
            pltpu.VMEM(external.shape, f32),
        ]
        + [pltpu.SMEM(v.shape, jnp.int32) for v in (tile_sub, corner_map, send_tile, remote_pairs, remote_count)]
        + [pltpu.SMEM((2 * peers,), jnp.int32)] * 2
        + [pltpu.SemaphoreType.DMA((n,)) for n in (2, 6, 9 + halves)],
        compiler_params=params,
        cost_estimate=pl.CostEstimate(
            flops=4 * tiles * block * depth, bytes_accessed=1 << 21, transcendentals=4 * tiles * points * points
        ),
        name="rest",
    )(
        below,
        above,
        inbox,
        b_own,
        num,
        den,
        payload,
        history,
        corner_load,
        external,
        tile_sub,
        corner_map,
        send_tile,
        remote_pairs,
        remote_count,
    )
    gathered = lax.all_to_all(parts, "blk", split_axis=0, concat_axis=0, tiled=True)
    return damage, jnp.sum(gathered, axis=0)


def solution(mesh):
    placed = (
        P(None, ("sub", "blk"), None),
        P(("sub", "blk"), None),
        P(("sub", "blk"), None),
        P(None, ("sub", "blk"), None),
        P(("sub", "blk")),
        P(("sub", "blk")),
        P(None, ("sub", "blk")),
        P(("sub", "blk")),
        P(None, ("sub", "blk")),
        P(("sub", "blk")),
        P(("sub", "blk"), None),
        P(("sub", "blk")),
    )
    return jax.shard_map(
        per_device,
        mesh=mesh,
        in_specs=placed,
        out_specs=(P(("sub", "blk"), None), P(("sub", "blk"))),
        check_vma=False,
    )
```

```python
import functools
import math

import jax
import jax.numpy as jnp
from jax import lax
from jax.experimental import pallas as pl
from jax.experimental.pallas import tpu as pltpu
from jax.sharding import PartitionSpec as P

gauss_rate = 4.0
keep_share = 0.05
softening = 0.5
coord_scale = math.sqrt(gauss_rate * math.log2(math.e))
far_off = 2048.0
depth = 32
pitch = depth + 1
grant = 24 * 1024 * 1024
whole_grant = 60 * 1024 * 1024

f32 = jnp.float32
bf16 = jnp.bfloat16
in_vmem = pl.BlockSpec(memory_space=pltpu.VMEM)
anywhere = pl.BlockSpec(memory_space=pl.ANY)


def pieces(value):
    high = value.astype(bf16).astype(f32)
    rest = value - high
    middle = rest.astype(bf16).astype(f32)
    low = (rest - middle).astype(bf16).astype(f32)
    return high, middle, low


def put_rows(rows_ref, base, rows):
    for r, row in enumerate(rows):
        tiles = row.shape[0]
        for half in range(row.shape[1] // 128):
            rows_ref[half, pl.ds(base * pitch + r, tiles, stride=pitch), :] = row[:, half * 128 : (half + 1) * 128]


def point_rows(planes):
    scaled = [p * coord_scale for p in planes[:3]]
    split = [pieces(s) for s in scaled]
    norm = scaled[0] * scaled[0] + scaled[1] * scaled[1] + scaled[2] * scaled[2]
    return split, norm


def put_source(planes, rows_ref, base):
    split, norm = point_rows(planes)
    ones = jnp.ones_like(norm)
    norm = norm + jnp.where(planes[3] > 0.0, 0.0, far_off)
    rows = []
    for high, middle, low in split:
        rows += [high, high, middle, high, low, middle]
    rows += list(pieces(-norm)) + [ones, ones, ones] + [planes[3]]
    rows += [jnp.zeros_like(norm)] * (depth - len(rows))
    put_rows(rows_ref, base, rows)


def put_target(planes, rows_ref):
    split, norm = point_rows(planes)
    ones = jnp.ones_like(norm)
    rows = []
    for high, middle, low in split:
        rows += [2.0 * v for v in (high, middle, high, low, high, middle)]
    rows += [ones, ones, ones] + list(pieces(-norm))
    rows += [jnp.zeros_like(norm)] * (depth - len(rows))
    put_rows(rows_ref, 0, rows)


def turn_group(rows_ref, group):
    turned = jnp.concatenate(
        [
            jnp.concatenate([rows_ref[half, pl.ds((group * 4 + j) * pitch, depth), :] for j in range(4)], axis=0).T
            for half in range(rows_ref.shape[0])
        ],
        axis=0,
    )
    left = turned.astype(bf16)
    column = lax.broadcasted_iota(jnp.int32, (1, 128), 1) // depth
    operands = []
    for j in range(4):
        mask = (column == j).astype(f32).astype(bf16)
        lane = depth * j + 24
        operands.append((left * mask, jnp.broadcast_to(turned[:, lane : lane + 1], turned.shape)))
    return operands


def pair_sums(a, s, b):
    points = a.shape[0]
    width = b.shape[1]
    weight = jnp.exp2(jnp.dot(a, b, preferred_element_type=f32))
    load = jnp.concatenate([s] * (width // 128), axis=1)
    den = jnp.sum(weight.reshape(points // 8, 8, width), axis=0)
    num = jnp.sum((weight * load).reshape(points // 8, 8, width), axis=0)
    return num, den


def fetch(sources, targets, sems):
    copies = [pltpu.make_async_copy(src, dst, sems.at[i]) for i, (src, dst) in enumerate(zip(sources, targets))]
    for copy in copies:
        copy.start()
    return copies


def pack_kernel(
    peers,
    coords,
    strain,
    tile_count_in,
    send_tile_in,
    remote_pairs_in,
    remote_count_in,
    payload,
    outbox,
    strain_here,
    tile_count,
    send_tile,
    remote_pairs,
    remote_count,
    sems,
):
    tiles, points = strain.shape
    copies = fetch(
        (coords, strain, tile_count_in, send_tile_in, remote_pairs_in, remote_count_in),
        (payload.at[0:3], strain_here, tile_count, send_tile, remote_pairs, remote_count),
        sems,
    )
    for copy in copies:
        copy.wait()
    lane = lax.broadcasted_iota(jnp.int32, (1, points), 1)
    for t in range(tiles):
        payload[3, t : t + 1, :] = jnp.where(lane < tile_count[t], strain_here[t : t + 1, :], 0.0)

    halves = points // 128

    def put(h, first, t, live):
        for k in range(4):
            row = payload[k, pl.ds(t, 1), :]
            if k == 3 and live is not None:
                row = row * live
            for half in range(halves):
                outbox[pl.ds((h * halves + half) * 8 + first + k, 1), :] = row[:, half * 128 : (half + 1) * 128]

    def sent(h, carry):
        put(h, 0, send_tile[h], None)
        return carry

    def listed(i, carry):
        put(remote_pairs[1, i], 4, remote_pairs[0, i], (i < remote_count[0]).astype(f32))
        return carry

    lax.fori_loop(0, peers, sent, 0, unroll=peers <= 8)
    lax.fori_loop(0, peers, listed, 0, unroll=peers <= 8)


def spread_rows(values):
    n = values.shape[1]
    wide = jnp.concatenate([values.astype(f32), jnp.zeros((1, 128 - n), f32)], axis=1)
    return jnp.broadcast_to(wide, (128, 128)).T[0:n]


def own_kernel(payload, local_pairs_in, b_ref, num_ref, den_ref, rows_ref, a_ref, s_ref, local_pairs, sems):
    tiles = payload.shape[1]
    copies = fetch((local_pairs_in,), (local_pairs,), sems)
    planes = [payload[k] for k in range(4)]
    put_target(planes, rows_ref)

    def set_target(group, carry):
        for t in [group * 4 + i for i in range(4)]:
            rows = pl.ds(t * pitch, depth)
            for half in range(rows_ref.shape[0]):
                block = rows_ref[half, rows, :].astype(bf16)
                for j in range(4):
                    b_ref[t, depth * j : depth * (j + 1), half * 128 : (half + 1) * 128] = block
        return carry

    lax.fori_loop(0, tiles // 4, set_target, 0)
    put_source(planes, rows_ref, 0)
    for copy in copies:
        copy.wait()

    def own(group, carry):
        for i, (a, s) in enumerate(turn_group(rows_ref, group)):
            t = group * 4 + i
            a_ref[t] = a
            s_ref[t] = s
            num, den = pair_sums(a, s, b_ref[t])
            num_ref[t] = num
            den_ref[t] = den
        return carry

    lax.fori_loop(0, tiles // 4, own, 0)

    def listed(step, carry):
        group = []
        for i in range(4):
            one = local_pairs[0, step * 4 + i]
            two = local_pairs[1, step * 4 + i]
            group += [(one, two), (two, one)]
        sums = [pair_sums(a_ref[src], s_ref[src], b_ref[dst]) for src, dst in group]
        for (src, dst), (num, den) in zip(group, sums):
            num_ref[dst] = num_ref[dst] + num
            den_ref[dst] = den_ref[dst] + den
        return carry

    lax.fori_loop(0, local_pairs.shape[1] // 4, listed, 0)


def rest_kernel(
    peers,
    below,
    above,
    inbox,
    b_ref,
    num_in,
    den_in,
    payload,
    history,
    corner_load,
    external,
    tile_sub,
    corner_map,
    send_tile_in,
    remote_pairs_in,
    remote_count_in,
    damage_ref,
    parts_ref,
    num_ref,
    den_ref,
    rows_ref,
    far_rows,
    last_a,
    last_s,
    send_tile,
    remote_pairs,
    remote_count,
    far_tile,
    far_live,
    sems,
):
    tiles, points = history.shape
    halves = points // 128
    groups = tiles // 4
    count = lax.axis_size("sub")
    layer = lax.axis_index("sub")
    copies = fetch(
        (send_tile_in, remote_pairs_in, remote_count_in),
        (send_tile, remote_pairs, remote_count),
        sems,
    )

    def border(shift):
        def turned(step):
            group = step if shift < 0 else groups - 1 - step
            return group, turn_group(rows_ref, group)

        edge = 3 if shift < 0 else 0

        def keep(operands):
            last_a[...] = operands[edge][0]
            last_s[...] = operands[edge][1]

        keep(turned(groups - 1)[1])

        def some(step, carry):
            group, operands = turned(step)
            outer = (last_a[...], last_s[...])
            sums = []
            for i in range(4):
                a, s = operands[i]
                more_a, more_s = operands[i + shift] if 0 <= i + shift < 4 else outer
                sums.append(
                    pair_sums(
                        jnp.concatenate([a, more_a], axis=0),
                        jnp.concatenate([s, more_s], axis=0),
                        b_ref[group * 4 + i],
                    )
                )
            for i, (num, den) in enumerate(sums):
                t = group * 4 + i
                num_ref[t] = num_ref[t] + num
                den_ref[t] = den_ref[t] + den
            keep(operands)
            return carry

        lax.fori_loop(0, groups, some, 0)

    @pl.when(layer > 0)
    def lower():
        put_source([below[k] for k in range(4)], rows_ref, 0)
        border(1)

    @pl.when(layer < count - 1)
    def upper():
        put_source([above[k] for k in range(4)], rows_ref, 0)
        border(-1)

    for copy in copies:
        copy.wait()
    for which in range(2):
        planes = [
            jnp.concatenate(
                [inbox[pl.ds(half * 8 + 4 * which + k, peers, stride=8 * halves), :] for half in range(halves)], axis=1
            )
            for k in range(4)
        ]
        put_source(planes, far_rows, which * peers)

    def place(i, carry):
        h = remote_pairs[1, i]
        far_tile[h] = remote_pairs[0, i]
        far_live[h] = (i < remote_count[0]).astype(jnp.int32)
        far_tile[peers + i] = send_tile[i]
        far_live[peers + i] = 1
        return carry

    lax.fori_loop(0, peers, place, 0, unroll=peers <= 8)

    def far(group, carry):
        for i, (a, s) in enumerate(turn_group(far_rows, group)):
            t = far_tile[group * 4 + i]
            live = far_live[group * 4 + i].astype(f32)
            num, den = pair_sums(a, s, b_ref[t])
            num_ref[t] = num_ref[t] + num * live
            den_ref[t] = den_ref[t] + den * live
        return carry

    lax.fori_loop(0, 2 * peers // 4, far, 0)

    valid = (payload[3] > 0.0).astype(f32)
    num = jnp.sum(num_ref[...], axis=1) * valid
    den = jnp.sum(den_ref[...], axis=1) * valid
    strain_bar = num / (den + 1.0 - valid)
    kappa = jnp.maximum(strain_bar, history[...])
    damage = 1.0 - (keep_share + (1.0 - keep_share) * jnp.exp(-softening * (kappa - 1.0))) / kappa
    damage_ref[...] = damage
    intact = (1.0 - damage) * valid

    folded = corner_load[:, :, 0:128] * intact[None, :, 0:128]
    for half in range(1, points // 128):
        cut = slice(half * 128, (half + 1) * 128)
        folded = folded + corner_load[:, :, cut] * intact[None, :, cut]
    owner = spread_rows(tile_sub[...].reshape(1, tiles))
    subs, corners = corner_map.shape
    map_rows = spread_rows(jnp.concatenate([corner_map[m : m + 1, :] for m in range(subs)], axis=1))
    sums = []
    for m in range(subs):
        chosen = jnp.where((owner == float(m))[None], folded, 0.0)
        sums.append(jnp.sum(jnp.sum(chosen, axis=1), axis=1, keepdims=True))
    sub_part = jnp.broadcast_to(jnp.concatenate(sums, axis=0), (subs * corners, 128))
    target = map_rows.astype(jnp.int32) - lax.broadcasted_iota(jnp.int32, (subs * corners, 128), 1)

    def scatter(j, carry):
        held = jnp.where(j == lax.axis_index("blk"), external[...], 0.0).reshape(1, 128)
        force = jnp.sum(jnp.where(target == j * 128, sub_part, 0.0), axis=0, keepdims=True)
        parts_ref[pl.ds(j, 1), :] = held - force
        return carry

    lax.fori_loop(0, peers, scatter, 0, unroll=peers <= 8)


def per_device(
    coords,
    strain,
    history,
    corner_load,
    tile_count,
    tile_sub,
    local_pairs,
    send_tile,
    remote_pairs,
    remote_count,
    corner_map,
    external,
):
    tiles, points = strain.shape
    halves = points // 128
    peers = lax.axis_size("blk")
    params = pltpu.CompilerParams(vmem_limit_bytes=grant)
    whole_params = pltpu.CompilerParams(vmem_limit_bytes=whole_grant)
    block = 2 * points * points

    payload, outbox = pl.pallas_call(
        functools.partial(pack_kernel, peers),
        out_shape=(
            jax.ShapeDtypeStruct((4, tiles, points), f32),
            jax.ShapeDtypeStruct((peers * halves * 8, 128), f32),
        ),
        in_specs=[anywhere] * 6,
        out_specs=(in_vmem, in_vmem),
        scratch_shapes=[pltpu.VMEM((tiles, points), f32)]
        + [pltpu.SMEM(v.shape, jnp.int32) for v in (tile_count, send_tile, remote_pairs, remote_count)]
        + [pltpu.SemaphoreType.DMA((6,))],
        compiler_params=whole_params,
        name="pack",
    )(coords, strain, tile_count, send_tile, remote_pairs, remote_count)

    layers = lax.axis_size("sub")
    below = lax.ppermute(payload, "sub", [(i, i + 1) for i in range(layers - 1)])
    above = lax.ppermute(payload, "sub", [(i + 1, i) for i in range(layers - 1)])
    inbox = lax.all_to_all(outbox, "blk", split_axis=0, concat_axis=0, tiled=True)

    b_own, num, den = pl.pallas_call(
        own_kernel,
        out_shape=(
            jax.ShapeDtypeStruct((tiles, 4 * depth, points), bf16),
            jax.ShapeDtypeStruct((tiles, 8, points), f32),
            jax.ShapeDtypeStruct((tiles, 8, points), f32),
        ),
        in_specs=[in_vmem, anywhere],
        out_specs=(in_vmem,) * 3,
        scratch_shapes=[
            pltpu.VMEM((halves, tiles * pitch, 128), f32),
            pltpu.VMEM((tiles, points, 4 * depth), bf16),
            pltpu.VMEM((tiles, points, 128), f32),
            pltpu.SMEM(local_pairs.shape, jnp.int32),
            pltpu.SemaphoreType.DMA((1,)),
        ],
        compiler_params=params,
        cost_estimate=pl.CostEstimate(
            flops=3 * tiles * block * depth, bytes_accessed=1 << 20, transcendentals=3 * tiles * points * points
        ),
        name="own",
    )(payload, local_pairs)

    damage, parts, num, den = pl.pallas_call(
        functools.partial(rest_kernel, peers),
        out_shape=(
            jax.ShapeDtypeStruct((tiles, points), f32),
            jax.ShapeDtypeStruct((peers, 128), f32),
            jax.ShapeDtypeStruct(num.shape, f32),
            jax.ShapeDtypeStruct(den.shape, f32),
        ),
        in_specs=[in_vmem] * 12 + [anywhere] * 3,
        out_specs=(in_vmem,) * 4,
        input_output_aliases={4: 2, 5: 3},
        scratch_shapes=[
            pltpu.VMEM((halves, tiles * pitch, 128), f32),
            pltpu.VMEM((halves, 2 * peers * pitch, 128), f32),
            pltpu.VMEM((points, 4 * depth), bf16),
            pltpu.VMEM((points, 128), f32),
        ]
        + [pltpu.SMEM(v.shape, jnp.int32) for v in (send_tile, remote_pairs, remote_count)]
        + [pltpu.SMEM((2 * peers,), jnp.int32)] * 2
        + [pltpu.SemaphoreType.DMA((3,))],
        compiler_params=params,
        cost_estimate=pl.CostEstimate(
            flops=4 * tiles * block * depth, bytes_accessed=1 << 21, transcendentals=4 * tiles * points * points
        ),
        name="rest",
    )(
        below,
        above,
        inbox,
        b_own,
        num,
        den,
        payload,
        history,
        corner_load,
        external,
        tile_sub,
        corner_map,
        send_tile,
        remote_pairs,
        remote_count,
    )
    gathered = lax.all_to_all(parts, "blk", split_axis=0, concat_axis=0, tiled=True)
    return damage, jnp.sum(gathered, axis=0)


def solution(mesh):
    placed = (
        P(None, ("sub", "blk"), None),
        P(("sub", "blk"), None),
        P(("sub", "blk"), None),
        P(None, ("sub", "blk"), None),
        P(("sub", "blk")),
        P(("sub", "blk")),
        P(None, ("sub", "blk")),
        P(("sub", "blk")),
        P(None, ("sub", "blk")),
        P(("sub", "blk")),
        P(("sub", "blk"), None),
        P(("sub", "blk")),
    )
    return jax.shard_map(
        per_device,
        mesh=mesh,
        in_specs=placed,
        out_specs=(P(("sub", "blk"), None), P(("sub", "blk"))),
        check_vma=False,
    )
```

```python
import functools
import math

import jax
import jax.numpy as jnp
from jax import lax
from jax.experimental import pallas as pl
from jax.experimental.pallas import tpu as pltpu
from jax.sharding import PartitionSpec as P

gauss_rate = 4.0
keep_share = 0.05
softening = 0.5
coord_scale = math.sqrt(gauss_rate * math.log2(math.e))
far_off = 2048.0
depth = 32
pitch = depth + 1
grant = 24 * 1024 * 1024
whole_grant = 60 * 1024 * 1024

f32 = jnp.float32
bf16 = jnp.bfloat16
in_vmem = pl.BlockSpec(memory_space=pltpu.VMEM)
anywhere = pl.BlockSpec(memory_space=pl.ANY)


def pieces(value):
    high = value.astype(bf16).astype(f32)
    rest = value - high
    middle = rest.astype(bf16).astype(f32)
    low = (rest - middle).astype(bf16).astype(f32)
    return high, middle, low


def put_rows(rows_ref, base, rows):
    for r, row in enumerate(rows):
        tiles = row.shape[0]
        for half in range(row.shape[1] // 128):
            rows_ref[half, pl.ds(base * pitch + r, tiles, stride=pitch), :] = row[:, half * 128 : (half + 1) * 128]


def point_rows(planes):
    scaled = [p * coord_scale for p in planes[:3]]
    split = [pieces(s) for s in scaled]
    norm = scaled[0] * scaled[0] + scaled[1] * scaled[1] + scaled[2] * scaled[2]
    return split, norm + jnp.where(planes[3] > 0.0, 0.0, far_off)


def put_source(planes, rows_ref, base):
    split, norm = point_rows(planes)
    ones = jnp.ones_like(norm)
    rows = []
    for high, middle, low in split:
        rows += [high, high, middle, high, low, middle]
    rows += list(pieces(-norm)) + [ones, ones, ones] + [planes[3]]
    rows += [jnp.zeros_like(norm)] * (depth - len(rows))
    put_rows(rows_ref, base, rows)


def put_target(planes, rows_ref):
    split, norm = point_rows(planes)
    ones = jnp.ones_like(norm)
    rows = []
    for high, middle, low in split:
        rows += [2.0 * v for v in (high, middle, high, low, high, middle)]
    rows += [ones, ones, ones] + list(pieces(-norm))
    rows += [jnp.zeros_like(norm)] * (depth - len(rows))
    put_rows(rows_ref, 0, rows)


def turn_group(rows_ref, group):
    turned = jnp.concatenate(
        [
            jnp.concatenate([rows_ref[half, pl.ds((group * 4 + j) * pitch, depth), :] for j in range(4)], axis=0).T
            for half in range(rows_ref.shape[0])
        ],
        axis=0,
    )
    left = turned.astype(bf16)
    column = lax.broadcasted_iota(jnp.int32, (1, 128), 1) // depth
    operands = []
    for j in range(4):
        mask = (column == j).astype(f32).astype(bf16)
        lane = depth * j + 24
        operands.append((left * mask, jnp.broadcast_to(turned[:, lane : lane + 1], turned.shape)))
    return operands


def fold(x):
    return jnp.sum(x.reshape(x.shape[0] // 8, 8, x.shape[1]), axis=0)


def column_sums(weight, s):
    load = jnp.concatenate([s] * (weight.shape[1] // 128), axis=1)
    return fold(weight * load), fold(weight)


def pair_sums(a, s, b):
    return column_sums(jnp.exp2(jnp.dot(a, b, preferred_element_type=f32)), s)


def both_sums(a, s, b, s_row):
    weight = jnp.exp2(jnp.dot(a, b, preferred_element_type=f32))
    cuts = [slice(lo, lo + 128) for lo in range(0, weight.shape[1], 128)]
    den_row = sum(weight[:, cut] for cut in cuts)
    num_row = sum(weight[:, cut] * s_row[:, cut] for cut in cuts)
    turned = [jnp.concatenate([fold(x[cut].T) for cut in cuts], axis=1) for x in (num_row, den_row)]
    return column_sums(weight, s), turned


def fetch(sources, targets, sems):
    copies = [pltpu.make_async_copy(src, dst, sems.at[i]) for i, (src, dst) in enumerate(zip(sources, targets))]
    for copy in copies:
        copy.start()
    return copies


def pack_kernel(
    peers,
    coords,
    strain,
    tile_count_in,
    send_tile_in,
    remote_pairs_in,
    remote_count_in,
    local_pairs_in,
    payload,
    outbox,
    strain_here,
    tile_count,
    send_tile,
    remote_pairs,
    remote_count,
    local_pairs,
    sems,
):
    tiles, points = strain.shape
    copies = fetch(
        (coords, strain, tile_count_in, send_tile_in, remote_pairs_in, remote_count_in, local_pairs_in),
        (payload.at[0:3], strain_here, tile_count, send_tile, remote_pairs, remote_count, local_pairs),
        sems,
    )
    payload[4] = jnp.zeros((tiles, points), f32)
    for copy in copies:
        copy.wait()
    payload[4, 0:2, 0 : local_pairs.shape[1]] = local_pairs[...].astype(f32)
    lane = lax.broadcasted_iota(jnp.int32, (1, points), 1)
    for t in range(tiles):
        payload[3, t : t + 1, :] = jnp.where(lane < tile_count[t], strain_here[t : t + 1, :], 0.0)

    halves = points // 128

    def put(h, first, t, live):
        for k in range(4):
            row = payload[k, pl.ds(t, 1), :]
            if k == 3 and live is not None:
                row = row * live
            for half in range(halves):
                outbox[pl.ds((h * halves + half) * 8 + first + k, 1), :] = row[:, half * 128 : (half + 1) * 128]

    def sent(h, carry):
        put(h, 0, send_tile[h], None)
        return carry

    def listed(i, carry):
        put(remote_pairs[1, i], 4, remote_pairs[0, i], (i < remote_count[0]).astype(f32))
        return carry

    lax.fori_loop(0, peers, sent, 0, unroll=peers <= 8)
    lax.fori_loop(0, peers, listed, 0, unroll=peers <= 8)


def spread_rows(values):
    n = values.shape[1]
    wide = jnp.concatenate([values.astype(f32), jnp.zeros((1, 128 - n), f32)], axis=1)
    return jnp.broadcast_to(wide, (128, 128)).T[0:n]


def own_kernel(pairs, payload, b_ref, num_ref, den_ref, rows_ref, a_ref, s_ref, local_pairs, sems):
    tiles = payload.shape[1]
    copies = fetch((payload.at[4, 0:8, 0:128],), (local_pairs,), sems)
    planes = [payload[k] for k in range(4)]
    put_target(planes, rows_ref)

    def set_target(group, carry):
        for t in [group * 4 + i for i in range(4)]:
            rows = pl.ds(t * pitch, depth)
            for half in range(rows_ref.shape[0]):
                block = rows_ref[half, rows, :].astype(bf16)
                for j in range(4):
                    b_ref[t, depth * j : depth * (j + 1), half * 128 : (half + 1) * 128] = block
        return carry

    lax.fori_loop(0, tiles // 4, set_target, 0)
    put_source(planes, rows_ref, 0)
    for copy in copies:
        copy.wait()

    def own(group, carry):
        for i, (a, s) in enumerate(turn_group(rows_ref, group)):
            t = group * 4 + i
            a_ref[t] = a
            s_ref[t] = s
            num, den = pair_sums(a, s, b_ref[t])
            num_ref[t] = num
            den_ref[t] = den
        return carry

    lax.fori_loop(0, tiles // 4, own, 0)

    def listed(step, carry):
        group = []
        for i in range(4):
            one = local_pairs[0, step * 4 + i].astype(jnp.int32)
            two = local_pairs[1, step * 4 + i].astype(jnp.int32)
            group.append((one, two))
        sums = [both_sums(a_ref[one], s_ref[one], b_ref[two], payload[3, pl.ds(two, 1), :]) for one, two in group]
        for (one, two), (for_two, for_one) in zip(group, sums):
            for t, (num, den) in ((two, for_two), (one, for_one)):
                num_ref[t] = num_ref[t] + num
                den_ref[t] = den_ref[t] + den
        return carry

    lax.fori_loop(0, pairs // 4, listed, 0)


def rest_kernel(
    peers,
    below,
    above,
    inbox,
    b_ref,
    num_in,
    den_in,
    payload,
    history,
    corner_load,
    external,
    tile_sub,
    corner_map,
    send_tile_in,
    remote_pairs_in,
    remote_count_in,
    damage_ref,
    parts_ref,
    rows_ref,
    far_rows,
    num_ref,
    den_ref,
    send_tile,
    remote_pairs,
    remote_count,
    far_tile,
    far_live,
    sems,
):
    tiles, points = history.shape
    halves = points // 128
    groups = tiles // 4
    count = lax.axis_size("sub")
    layer = lax.axis_index("sub")
    copies = fetch(
        (send_tile_in, remote_pairs_in, remote_count_in),
        (send_tile, remote_pairs, remote_count),
        sems,
    )

    num_ref[...] = num_in[...]
    den_ref[...] = den_in[...]

    def border(shift):
        def some(group, carry):
            sums = {}
            for i, (a, s) in enumerate(turn_group(rows_ref, group)):
                places = (i, i + shift)
                targets = [lax.rem(group * 4 + place + tiles, tiles) for place in places]
                num, den = pair_sums(a, s, jnp.concatenate([b_ref[t] for t in targets], axis=1))
                for j, (place, t) in enumerate(zip(places, targets)):
                    cut = slice(j * points, (j + 1) * points)
                    held = sums.get(place, (t, 0.0, 0.0))
                    sums[place] = (t, held[1] + num[:, cut], held[2] + den[:, cut])
            for t, num, den in sums.values():
                num_ref[t] = num_ref[t] + num
                den_ref[t] = den_ref[t] + den
            return carry

        lax.fori_loop(0, groups, some, 0)

    @pl.when(layer > 0)
    def lower():
        put_source([below[k] for k in range(4)], rows_ref, 0)
        border(-1)

    @pl.when(layer < count - 1)
    def upper():
        put_source([above[k] for k in range(4)], rows_ref, 0)
        border(1)

    for copy in copies:
        copy.wait()
    for which in range(2):
        planes = [
            jnp.concatenate(
                [inbox[pl.ds(half * 8 + 4 * which + k, peers, stride=8 * halves), :] for half in range(halves)], axis=1
            )
            for k in range(4)
        ]
        put_source(planes, far_rows, which * peers)

    def place(i, carry):
        h = remote_pairs[1, i]
        far_tile[h] = remote_pairs[0, i]
        far_live[h] = (i < remote_count[0]).astype(jnp.int32)
        far_tile[peers + i] = send_tile[i]
        far_live[peers + i] = 1
        return carry

    lax.fori_loop(0, peers, place, 0, unroll=peers <= 8)

    def far(group, carry):
        for i, (a, s) in enumerate(turn_group(far_rows, group)):
            t = far_tile[group * 4 + i]
            live = far_live[group * 4 + i].astype(f32)
            num, den = pair_sums(a, s, b_ref[t])
            num_ref[t] = num_ref[t] + num * live
            den_ref[t] = den_ref[t] + den * live
        return carry

    lax.fori_loop(0, 2 * peers // 4, far, 0)

    valid = (payload[3] > 0.0).astype(f32)
    num = jnp.sum(num_ref[...], axis=1) * valid
    den = jnp.sum(den_ref[...], axis=1) * valid
    strain_bar = num / (den + 1.0 - valid)
    kappa = jnp.maximum(strain_bar, history[...])
    damage = 1.0 - (keep_share + (1.0 - keep_share) * jnp.exp(-softening * (kappa - 1.0))) / kappa
    damage_ref[...] = damage
    intact = (1.0 - damage) * valid

    folded = corner_load[:, :, 0:128] * intact[None, :, 0:128]
    for half in range(1, points // 128):
        cut = slice(half * 128, (half + 1) * 128)
        folded = folded + corner_load[:, :, cut] * intact[None, :, cut]
    owner = spread_rows(tile_sub[...].reshape(1, tiles))
    subs, corners = corner_map.shape
    map_rows = spread_rows(jnp.concatenate([corner_map[m : m + 1, :] for m in range(subs)], axis=1))
    sums = []
    for m in range(subs):
        chosen = jnp.where((owner == float(m))[None], folded, 0.0)
        sums.append(jnp.sum(jnp.sum(chosen, axis=1), axis=1, keepdims=True))
    sub_part = jnp.broadcast_to(jnp.concatenate(sums, axis=0), (subs * corners, 128))
    target = map_rows.astype(jnp.int32) - lax.broadcasted_iota(jnp.int32, (subs * corners, 128), 1)

    def scatter(j, carry):
        held = jnp.where(j == lax.axis_index("blk"), external[...], 0.0).reshape(1, 128)
        force = jnp.sum(jnp.where(target == j * 128, sub_part, 0.0), axis=0, keepdims=True)
        parts_ref[pl.ds(j, 1), :] = held - force
        return carry

    lax.fori_loop(0, peers, scatter, 0, unroll=peers <= 8)


def per_device(
    coords,
    strain,
    history,
    corner_load,
    tile_count,
    tile_sub,
    local_pairs,
    send_tile,
    remote_pairs,
    remote_count,
    corner_map,
    external,
):
    tiles, points = strain.shape
    halves = points // 128
    peers = lax.axis_size("blk")
    params = pltpu.CompilerParams(vmem_limit_bytes=grant)
    whole_params = pltpu.CompilerParams(vmem_limit_bytes=whole_grant)
    block = 2 * points * points

    payload, outbox = pl.pallas_call(
        functools.partial(pack_kernel, peers),
        out_shape=(
            jax.ShapeDtypeStruct((5, tiles, points), f32),
            jax.ShapeDtypeStruct((peers * halves * 8, 128), f32),
        ),
        in_specs=[anywhere] * 7,
        out_specs=(in_vmem, in_vmem),
        scratch_shapes=[pltpu.VMEM((tiles, points), f32)]
        + [pltpu.SMEM(v.shape, jnp.int32) for v in (tile_count, send_tile, remote_pairs, remote_count)]
        + [pltpu.VMEM(local_pairs.shape, jnp.int32), pltpu.SemaphoreType.DMA((7,))],
        compiler_params=whole_params,
        name="pack",
    )(coords, strain, tile_count, send_tile, remote_pairs, remote_count, local_pairs)

    layers = lax.axis_size("sub")
    below = lax.ppermute(payload, "sub", [(i, i + 1) for i in range(layers - 1)])
    above = lax.ppermute(payload, "sub", [(i + 1, i) for i in range(layers - 1)])
    inbox = lax.all_to_all(outbox, "blk", split_axis=0, concat_axis=0, tiled=True)

    b_own, num, den = pl.pallas_call(
        functools.partial(own_kernel, local_pairs.shape[1]),
        out_shape=(
            jax.ShapeDtypeStruct((tiles, 4 * depth, points), bf16),
            jax.ShapeDtypeStruct((tiles, 8, points), f32),
            jax.ShapeDtypeStruct((tiles, 8, points), f32),
        ),
        in_specs=[in_vmem],
        out_specs=(in_vmem,) * 3,
        scratch_shapes=[
            pltpu.VMEM((halves, tiles * pitch, 128), f32),
            pltpu.VMEM((tiles, points, 4 * depth), bf16),
            pltpu.VMEM((tiles, points, 128), f32),
            pltpu.SMEM((8, 128), f32),
            pltpu.SemaphoreType.DMA((1,)),
        ],
        compiler_params=params,
        cost_estimate=pl.CostEstimate(
            flops=3 * tiles * block * depth, bytes_accessed=1 << 20, transcendentals=3 * tiles * points * points
        ),
        name="own",
    )(payload)

    damage, parts = pl.pallas_call(
        functools.partial(rest_kernel, peers),
        out_shape=(
            jax.ShapeDtypeStruct((tiles, points), f32),
            jax.ShapeDtypeStruct((peers, 128), f32),
        ),
        in_specs=[in_vmem] * 12 + [anywhere] * 3,
        out_specs=(in_vmem,) * 2,
        scratch_shapes=[
            pltpu.VMEM((halves, tiles * pitch, 128), f32),
            pltpu.VMEM((halves, 2 * peers * pitch, 128), f32),
            pltpu.VMEM(num.shape, f32),
            pltpu.VMEM(den.shape, f32),
        ]
        + [pltpu.SMEM(v.shape, jnp.int32) for v in (send_tile, remote_pairs, remote_count)]
        + [pltpu.SMEM((2 * peers,), jnp.int32)] * 2
        + [pltpu.SemaphoreType.DMA((3,))],
        compiler_params=params,
        cost_estimate=pl.CostEstimate(
            flops=4 * tiles * block * depth, bytes_accessed=1 << 21, transcendentals=4 * tiles * points * points
        ),
        name="rest",
    )(
        below,
        above,
        inbox,
        b_own,
        num,
        den,
        payload,
        history,
        corner_load,
        external,
        tile_sub,
        corner_map,
        send_tile,
        remote_pairs,
        remote_count,
    )
    gathered = lax.all_to_all(parts, "blk", split_axis=0, concat_axis=0, tiled=True)
    return damage, jnp.sum(gathered, axis=0)


def solution(mesh):
    placed = (
        P(None, ("sub", "blk"), None),
        P(("sub", "blk"), None),
        P(("sub", "blk"), None),
        P(None, ("sub", "blk"), None),
        P(("sub", "blk")),
        P(("sub", "blk")),
        P(None, ("sub", "blk")),
        P(("sub", "blk")),
        P(None, ("sub", "blk")),
        P(("sub", "blk")),
        P(("sub", "blk"), None),
        P(("sub", "blk")),
    )
    return jax.shard_map(
        per_device,
        mesh=mesh,
        in_specs=placed,
        out_specs=(P(("sub", "blk"), None), P(("sub", "blk"))),
        check_vma=False,
    )
```

```python
import functools
import math

import jax
import jax.numpy as jnp
from jax import lax
from jax.experimental import pallas as pl
from jax.experimental.pallas import tpu as pltpu
from jax.sharding import PartitionSpec as P

gauss_rate = 4.0
keep_share = 0.05
softening = 0.5
coord_scale = math.sqrt(gauss_rate)
far_off = 2048.0
depth = 32
pitch = depth + 1
grant = 48 * 1024 * 1024
whole_grant = 60 * 1024 * 1024

f32 = jnp.float32
bf16 = jnp.bfloat16
in_vmem = pl.BlockSpec(memory_space=pltpu.VMEM)
anywhere = pl.BlockSpec(memory_space=pl.ANY)


def pieces(value):
    high = value.astype(bf16).astype(f32)
    rest = value - high
    middle = rest.astype(bf16).astype(f32)
    low = (rest - middle).astype(bf16).astype(f32)
    return high, middle, low


def put_rows(rows_ref, base, rows):
    for r, row in enumerate(rows):
        tiles = row.shape[0]
        for half in range(row.shape[1] // 128):
            rows_ref[half, pl.ds(base * pitch + r, tiles, stride=pitch), :] = row[:, half * 128 : (half + 1) * 128]


def point_rows(planes):
    scaled = [p * coord_scale for p in planes[:3]]
    split = [pieces(s) for s in scaled]
    norm = scaled[0] * scaled[0] + scaled[1] * scaled[1] + scaled[2] * scaled[2]
    return split, norm + jnp.where(planes[3] > 0.0, 0.0, far_off)


def put_source(planes, rows_ref, base):
    split, norm = point_rows(planes)
    ones = jnp.ones_like(norm)
    rows = []
    for high, middle, low in split:
        rows += [high, high, middle, high, low, middle]
    rows += list(pieces(-norm)) + [ones, ones, ones] + [planes[3]]
    rows += [jnp.zeros_like(norm)] * (depth - len(rows))
    put_rows(rows_ref, base, rows)


def put_target(planes, rows_ref):
    split, norm = point_rows(planes)
    ones = jnp.ones_like(norm)
    rows = []
    for high, middle, low in split:
        rows += [2.0 * v for v in (high, middle, high, low, high, middle)]
    rows += [ones, ones, ones] + list(pieces(-norm))
    rows += [jnp.zeros_like(norm)] * (depth - len(rows))
    put_rows(rows_ref, 0, rows)


def turn_group(rows_ref, group):
    turned = jnp.concatenate(
        [
            jnp.concatenate([rows_ref[half, pl.ds((group * 4 + j) * pitch, depth), :] for j in range(4)], axis=0).T
            for half in range(rows_ref.shape[0])
        ],
        axis=0,
    )
    left = turned.astype(bf16)
    column = lax.broadcasted_iota(jnp.int32, (1, 128), 1) // depth
    operands = []
    for j in range(4):
        mask = (column == j).astype(f32).astype(bf16)
        lane = depth * j + 24
        operands.append((left * mask, jnp.broadcast_to(turned[:, lane : lane + 1], turned.shape)))
    return operands


def fold(x):
    return jnp.sum(x.reshape(x.shape[0] // 8, 8, x.shape[1]), axis=0)


def column_sums(weight, s):
    load = jnp.concatenate([s] * (weight.shape[1] // 128), axis=1)
    return fold(weight * load), fold(weight)


def pair_sums(a, s, b, step):
    num, den = 0.0, 0.0
    for lo in range(0, a.shape[0], step):
        weight = jnp.exp(jnp.dot(a[lo : lo + step], b, preferred_element_type=f32))
        more_num, more_den = column_sums(weight, s[lo : lo + step])
        num, den = num + more_num, den + more_den
    return num, den


def fetch(sources, targets, sems):
    copies = [pltpu.make_async_copy(src, dst, sems.at[i]) for i, (src, dst) in enumerate(zip(sources, targets))]
    for copy in copies:
        copy.start()
    return copies


def pack_kernel(
    peers,
    coords,
    strain,
    tile_count_in,
    send_tile_in,
    remote_pairs_in,
    remote_count_in,
    local_pairs_in,
    payload,
    outbox,
    strain_here,
    tile_count,
    send_tile,
    remote_pairs,
    remote_count,
    local_pairs,
    sems,
):
    tiles, points = strain.shape
    copies = fetch(
        (coords, strain, tile_count_in, send_tile_in, remote_pairs_in, remote_count_in, local_pairs_in),
        (payload.at[0:3], strain_here, tile_count, send_tile, remote_pairs, remote_count, local_pairs),
        sems,
    )
    payload[4] = jnp.zeros((tiles, points), f32)
    for copy in copies:
        copy.wait()
    payload[4, 0:2, 0 : local_pairs.shape[1]] = local_pairs[...].astype(f32)
    lane = lax.broadcasted_iota(jnp.int32, (1, points), 1)
    for t in range(tiles):
        payload[3, t : t + 1, :] = jnp.where(lane < tile_count[t], strain_here[t : t + 1, :], 0.0)

    halves = points // 128

    def put(h, first, t, live):
        for k in range(4):
            row = payload[k, pl.ds(t, 1), :]
            if k == 3 and live is not None:
                row = row * live
            for half in range(halves):
                outbox[pl.ds((h * halves + half) * 8 + first + k, 1), :] = row[:, half * 128 : (half + 1) * 128]

    def sent(h, carry):
        put(h, 0, send_tile[h], None)
        return carry

    def listed(i, carry):
        put(remote_pairs[1, i], 4, remote_pairs[0, i], (i < remote_count[0]).astype(f32))
        return carry

    lax.fori_loop(0, peers, sent, 0, unroll=peers <= 8)
    lax.fori_loop(0, peers, listed, 0, unroll=peers <= 8)


def spread_rows(values):
    n = values.shape[1]
    wide = jnp.concatenate([values.astype(f32), jnp.zeros((1, 128 - n), f32)], axis=1)
    return jnp.broadcast_to(wide, (128, 128)).T[0:n]


def own_kernel(pairs, payload, b_ref, sums_ref, rows_ref, a_ref, s_ref, local_pairs, sems):
    tiles = payload.shape[1]
    copies = fetch((payload.at[4, 0:8, 0:128],), (local_pairs,), sems)
    planes = [payload[k] for k in range(4)]
    put_target(planes, rows_ref)

    def set_target(group, carry):
        for t in [group * 4 + i for i in range(4)]:
            rows = pl.ds(t * pitch, depth)
            for half in range(rows_ref.shape[0]):
                block = rows_ref[half, rows, :].astype(bf16)
                for j in range(4):
                    b_ref[t, depth * j : depth * (j + 1), half * 128 : (half + 1) * 128] = block
        return carry

    lax.fori_loop(0, tiles // 4, set_target, 0)
    put_source(planes, rows_ref, 0)
    for copy in copies:
        copy.wait()

    def own(group, carry):
        for i, (a, s) in enumerate(turn_group(rows_ref, group)):
            t = group * 4 + i
            a_ref[t] = a
            s_ref[t] = s
            num, den = pair_sums(a, s, b_ref[t], 64)
            sums_ref[0, t] = num
            sums_ref[1, t] = den
        return carry

    lax.fori_loop(0, tiles // 4, own, 0)

    def listed(step, carry):
        group = []
        for i in range(4):
            one = local_pairs[0, step * 4 + i].astype(jnp.int32)
            two = local_pairs[1, step * 4 + i].astype(jnp.int32)
            group += [(one, two), (two, one)]
        sums = [pair_sums(a_ref[src], s_ref[src], b_ref[dst], 64) for src, dst in group]
        for (src, dst), (num, den) in zip(group, sums):
            sums_ref[0, dst] = sums_ref[0, dst] + num
            sums_ref[1, dst] = sums_ref[1, dst] + den
        return carry

    lax.fori_loop(0, pairs // 4, listed, 0)


def rest_kernel(
    peers,
    below,
    above,
    inbox,
    b_ref,
    sums_in,
    payload,
    history,
    corner_load,
    external,
    tile_sub,
    corner_map,
    send_tile_in,
    remote_pairs_in,
    remote_count_in,
    damage_ref,
    parts_ref,
    rows_ref,
    far_rows,
    sums_ref,
    send_tile,
    remote_pairs,
    remote_count,
    far_tile,
    far_live,
    sems,
):
    tiles, points = history.shape
    halves = points // 128
    groups = tiles // 4
    count = lax.axis_size("sub")
    layer = lax.axis_index("sub")
    copies = fetch(
        (send_tile_in, remote_pairs_in, remote_count_in),
        (send_tile, remote_pairs, remote_count),
        sems,
    )

    sums_ref[...] = sums_in[...]

    def border(shift):
        def some(group, carry):
            sums = {}
            for i, (a, s) in enumerate(turn_group(rows_ref, group)):
                places = (i, i + shift)
                targets = [lax.rem(group * 4 + place + tiles, tiles) for place in places]
                num, den = pair_sums(a, s, jnp.concatenate([b_ref[t] for t in targets], axis=1), points)
                for j, (place, t) in enumerate(zip(places, targets)):
                    cut = slice(j * points, (j + 1) * points)
                    held = sums.get(place, (t, 0.0, 0.0))
                    sums[place] = (t, held[1] + num[:, cut], held[2] + den[:, cut])
            for t, num, den in sums.values():
                sums_ref[0, t] = sums_ref[0, t] + num
                sums_ref[1, t] = sums_ref[1, t] + den
            return carry

        lax.fori_loop(0, groups, some, 0)

    @pl.when(layer > 0)
    def lower():
        put_source([below[k] for k in range(4)], rows_ref, 0)
        border(-1)

    @pl.when(layer < count - 1)
    def upper():
        put_source([above[k] for k in range(4)], rows_ref, 0)
        border(1)

    for copy in copies:
        copy.wait()
    for which in range(2):
        planes = [
            jnp.concatenate(
                [inbox[pl.ds(half * 8 + 4 * which + k, peers, stride=8 * halves), :] for half in range(halves)], axis=1
            )
            for k in range(4)
        ]
        put_source(planes, far_rows, which * peers)

    def place(i, carry):
        h = remote_pairs[1, i]
        far_tile[h] = remote_pairs[0, i]
        far_live[h] = (i < remote_count[0]).astype(jnp.int32)
        far_tile[peers + i] = send_tile[i]
        far_live[peers + i] = 1
        return carry

    lax.fori_loop(0, peers, place, 0, unroll=peers <= 8)

    def far(group, carry):
        for i, (a, s) in enumerate(turn_group(far_rows, group)):
            t = far_tile[group * 4 + i]
            live = far_live[group * 4 + i].astype(f32)
            num, den = pair_sums(a, s, b_ref[t], points)
            sums_ref[0, t] = sums_ref[0, t] + num * live
            sums_ref[1, t] = sums_ref[1, t] + den * live
        return carry

    lax.fori_loop(0, 2 * peers // 4, far, 0)

    valid = (payload[3] > 0.0).astype(f32)
    num, den = jnp.sum(sums_ref[...], axis=2)
    strain_bar = num / (den + 1.0 - valid)
    kappa = jnp.maximum(strain_bar, history[...])
    damage = 1.0 - (keep_share + (1.0 - keep_share) * jnp.exp(-softening * (kappa - 1.0))) / kappa
    damage_ref[...] = damage
    intact = (1.0 - damage) * valid

    folded = corner_load[:, :, 0:128] * intact[None, :, 0:128]
    for half in range(1, points // 128):
        cut = slice(half * 128, (half + 1) * 128)
        folded = folded + corner_load[:, :, cut] * intact[None, :, cut]
    owner = spread_rows(tile_sub[...].reshape(1, tiles))
    subs, corners = corner_map.shape
    map_rows = spread_rows(jnp.concatenate([corner_map[m : m + 1, :] for m in range(subs)], axis=1))
    sums = []
    for m in range(subs):
        chosen = jnp.where((owner == float(m))[None], folded, 0.0)
        sums.append(jnp.sum(jnp.sum(chosen, axis=1), axis=1, keepdims=True))
    sub_part = jnp.broadcast_to(jnp.concatenate(sums, axis=0), (subs * corners, 128))
    target = map_rows.astype(jnp.int32) - lax.broadcasted_iota(jnp.int32, (subs * corners, 128), 1)

    def scatter(j, carry):
        held = jnp.where(j == lax.axis_index("blk"), external[...], 0.0).reshape(1, 128)
        force = jnp.sum(jnp.where(target == j * 128, sub_part, 0.0), axis=0, keepdims=True)
        parts_ref[pl.ds(j, 1), :] = held - force
        return carry

    lax.fori_loop(0, peers, scatter, 0, unroll=peers <= 8)


def per_device(
    coords,
    strain,
    history,
    corner_load,
    tile_count,
    tile_sub,
    local_pairs,
    send_tile,
    remote_pairs,
    remote_count,
    corner_map,
    external,
):
    tiles, points = strain.shape
    halves = points // 128
    peers = lax.axis_size("blk")
    params = pltpu.CompilerParams(vmem_limit_bytes=grant)
    whole_params = pltpu.CompilerParams(vmem_limit_bytes=whole_grant)
    block = 2 * points * points

    payload, outbox = pl.pallas_call(
        functools.partial(pack_kernel, peers),
        out_shape=(
            jax.ShapeDtypeStruct((5, tiles, points), f32),
            jax.ShapeDtypeStruct((peers * halves * 8, 128), f32),
        ),
        in_specs=[anywhere] * 7,
        out_specs=(in_vmem, in_vmem),
        scratch_shapes=[pltpu.VMEM((tiles, points), f32)]
        + [pltpu.SMEM(v.shape, jnp.int32) for v in (tile_count, send_tile, remote_pairs, remote_count)]
        + [pltpu.VMEM(local_pairs.shape, jnp.int32), pltpu.SemaphoreType.DMA((7,))],
        compiler_params=whole_params,
        name="pack",
    )(coords, strain, tile_count, send_tile, remote_pairs, remote_count, local_pairs)

    layers = lax.axis_size("sub")
    below = lax.ppermute(payload, "sub", [(i, i + 1) for i in range(layers - 1)])
    above = lax.ppermute(payload, "sub", [(i + 1, i) for i in range(layers - 1)])
    inbox = lax.all_to_all(outbox, "blk", split_axis=0, concat_axis=0, tiled=True)

    b_own, sums = pl.pallas_call(
        functools.partial(own_kernel, local_pairs.shape[1]),
        out_shape=(
            jax.ShapeDtypeStruct((tiles, 4 * depth, points), bf16),
            jax.ShapeDtypeStruct((2, tiles, 8, points), f32),
        ),
        in_specs=[in_vmem],
        out_specs=(in_vmem,) * 2,
        scratch_shapes=[
            pltpu.VMEM((halves, tiles * pitch, 128), f32),
            pltpu.VMEM((tiles, points, 4 * depth), bf16),
            pltpu.VMEM((tiles, points, 128), f32),
            pltpu.SMEM((8, 128), f32),
            pltpu.SemaphoreType.DMA((1,)),
        ],
        compiler_params=params,
        cost_estimate=pl.CostEstimate(
            flops=3 * tiles * block * depth, bytes_accessed=1 << 20, transcendentals=3 * tiles * points * points
        ),
        name="own",
    )(payload)

    damage, parts = pl.pallas_call(
        functools.partial(rest_kernel, peers),
        out_shape=(
            jax.ShapeDtypeStruct((tiles, points), f32),
            jax.ShapeDtypeStruct((peers, 128), f32),
        ),
        in_specs=[in_vmem] * 11 + [anywhere] * 3,
        out_specs=(in_vmem,) * 2,
        scratch_shapes=[
            pltpu.VMEM((halves, tiles * pitch, 128), f32),
            pltpu.VMEM((halves, 2 * peers * pitch, 128), f32),
            pltpu.VMEM(sums.shape, f32),
        ]
        + [pltpu.SMEM(v.shape, jnp.int32) for v in (send_tile, remote_pairs, remote_count)]
        + [pltpu.SMEM((2 * peers,), jnp.int32)] * 2
        + [pltpu.SemaphoreType.DMA((3,))],
        compiler_params=params,
        cost_estimate=pl.CostEstimate(
            flops=4 * tiles * block * depth, bytes_accessed=1 << 21, transcendentals=4 * tiles * points * points
        ),
        name="rest",
    )(
        below,
        above,
        inbox,
        b_own,
        sums,
        payload,
        history,
        corner_load,
        external,
        tile_sub,
        corner_map,
        send_tile,
        remote_pairs,
        remote_count,
    )
    gathered = lax.all_to_all(parts, "blk", split_axis=0, concat_axis=0, tiled=True)
    return damage, jnp.sum(gathered, axis=0)


def solution(mesh):
    placed = (
        P(None, ("sub", "blk"), None),
        P(("sub", "blk"), None),
        P(("sub", "blk"), None),
        P(None, ("sub", "blk"), None),
        P(("sub", "blk")),
        P(("sub", "blk")),
        P(None, ("sub", "blk")),
        P(("sub", "blk")),
        P(None, ("sub", "blk")),
        P(("sub", "blk")),
        P(("sub", "blk"), None),
        P(("sub", "blk")),
    )
    return jax.shard_map(
        per_device,
        mesh=mesh,
        in_specs=placed,
        out_specs=(P(("sub", "blk"), None), P(("sub", "blk"))),
        check_vma=False,
    )
```

```python
import functools
import math

import jax
import jax.numpy as jnp
from jax import lax
from jax.experimental import pallas as pl
from jax.experimental.pallas import tpu as pltpu
from jax.sharding import PartitionSpec as P

gauss_rate = 4.0
keep_share = 0.05
softening = 0.5
coord_scale = math.sqrt(gauss_rate * math.log2(math.e))
far_off = 2048.0
depth = 32
pitch = depth + 1
grant = 24 * 1024 * 1024
whole_grant = 60 * 1024 * 1024

f32 = jnp.float32
bf16 = jnp.bfloat16
in_vmem = pl.BlockSpec(memory_space=pltpu.VMEM)
anywhere = pl.BlockSpec(memory_space=pl.ANY)


def pieces(value):
    high = value.astype(bf16).astype(f32)
    rest = value - high
    middle = rest.astype(bf16).astype(f32)
    low = (rest - middle).astype(bf16).astype(f32)
    return high, middle, low


def put_rows(rows_ref, base, rows):
    for r, row in enumerate(rows):
        tiles = row.shape[0]
        for half in range(row.shape[1] // 128):
            rows_ref[half, pl.ds(base * pitch + r, tiles, stride=pitch), :] = row[:, half * 128 : (half + 1) * 128]


def point_rows(planes):
    scaled = [p * coord_scale for p in planes[:3]]
    split = [pieces(s) for s in scaled]
    norm = scaled[0] * scaled[0] + scaled[1] * scaled[1] + scaled[2] * scaled[2]
    return split, norm + jnp.where(planes[3] > 0.0, 0.0, far_off)


def put_source(planes, rows_ref, base):
    split, norm = point_rows(planes)
    ones = jnp.ones_like(norm)
    rows = []
    for high, middle, low in split:
        rows += [high, high, middle, high, low, middle]
    rows += list(pieces(-norm)) + [ones, ones, ones] + [planes[3]]
    rows += [jnp.zeros_like(norm)] * (depth - len(rows))
    put_rows(rows_ref, base, rows)


def put_target(planes, rows_ref):
    split, norm = point_rows(planes)
    ones = jnp.ones_like(norm)
    rows = []
    for high, middle, low in split:
        rows += [2.0 * v for v in (high, middle, high, low, high, middle)]
    rows += [ones, ones, ones] + list(pieces(-norm))
    rows += [jnp.zeros_like(norm)] * (depth - len(rows))
    put_rows(rows_ref, 0, rows)


def turn_group(rows_ref, group):
    turned = jnp.concatenate(
        [
            jnp.concatenate([rows_ref[half, pl.ds((group * 4 + j) * pitch, depth), :] for j in range(4)], axis=0).T
            for half in range(rows_ref.shape[0])
        ],
        axis=0,
    )
    left = turned.astype(bf16)
    column = lax.broadcasted_iota(jnp.int32, (1, 128), 1) // depth
    operands = []
    for j in range(4):
        mask = (column == j).astype(f32).astype(bf16)
        lane = depth * j + 24
        operands.append((left * mask, jnp.broadcast_to(turned[:, lane : lane + 1], turned.shape)))
    return operands


def fold(x):
    return jnp.sum(x.reshape(x.shape[0] // 8, 8, x.shape[1]), axis=0)


def column_sums(weight, s):
    load = jnp.concatenate([s] * (weight.shape[1] // 128), axis=1)
    return fold(weight * load), fold(weight)


def add_pair(sums_ref, t, a, s, b, live=None):
    weight = jnp.exp2(jnp.dot(a, b, preferred_element_type=f32))
    num, den = column_sums(weight, s)
    if live is not None:
        num, den = num * live, den * live
    sums_ref[0, t] = sums_ref[0, t] + num
    sums_ref[1, t] = sums_ref[1, t] + den


def repeat_target(compact, b_ref):
    def some_tiles(step, carry):
        for t in [step * 4 + i for i in range(4)]:
            block = compact[t]
            for j in range(4):
                b_ref[t, depth * j : depth * (j + 1), :] = block
        return carry

    lax.fori_loop(0, compact.shape[0] // 4, some_tiles, 0)


def fetch(sources, targets, sems):
    copies = [pltpu.make_async_copy(src, dst, sems.at[i]) for i, (src, dst) in enumerate(zip(sources, targets))]
    for copy in copies:
        copy.start()
    return copies


def pack_kernel(
    peers,
    coords,
    strain,
    tile_count_in,
    send_tile_in,
    remote_pairs_in,
    remote_count_in,
    local_pairs_in,
    payload,
    outbox,
    strain_here,
    tile_count,
    send_tile,
    remote_pairs,
    remote_count,
    local_pairs,
    sems,
):
    tiles, points = strain.shape
    copies = fetch(
        (coords, strain, tile_count_in, send_tile_in, remote_pairs_in, remote_count_in, local_pairs_in),
        (payload.at[0:3], strain_here, tile_count, send_tile, remote_pairs, remote_count, local_pairs),
        sems,
    )
    payload[4] = jnp.zeros((tiles, points), f32)
    for copy in copies:
        copy.wait()
    payload[4, 0:2, 0 : local_pairs.shape[1]] = local_pairs[...].astype(f32)
    lane = lax.broadcasted_iota(jnp.int32, (1, points), 1)
    for t in range(tiles):
        payload[3, t : t + 1, :] = jnp.where(lane < tile_count[t], strain_here[t : t + 1, :], 0.0)

    halves = points // 128

    def put(h, first, t, live):
        for k in range(4):
            row = payload[k, pl.ds(t, 1), :]
            if k == 3 and live is not None:
                row = row * live
            for half in range(halves):
                outbox[pl.ds((h * halves + half) * 8 + first + k, 1), :] = row[:, half * 128 : (half + 1) * 128]

    def sent(h, carry):
        put(h, 0, send_tile[h], None)
        return carry

    def listed(i, carry):
        put(remote_pairs[1, i], 4, remote_pairs[0, i], (i < remote_count[0]).astype(f32))
        return carry

    lax.fori_loop(0, peers, sent, 0, unroll=peers <= 8)
    lax.fori_loop(0, peers, listed, 0, unroll=peers <= 8)


def spread_rows(values):
    n = values.shape[1]
    wide = jnp.concatenate([values.astype(f32), jnp.zeros((1, 128 - n), f32)], axis=1)
    return jnp.broadcast_to(wide, (128, 128)).T[0:n]


def own_kernel(pairs, payload, b_out, sums_ref, rows_ref, a_ref, s_ref, b_ref, local_pairs, sems):
    tiles = payload.shape[1]
    copies = fetch((payload.at[4, 0:8, 0:128],), (local_pairs,), sems)
    planes = [payload[k] for k in range(4)]
    put_target(planes, rows_ref)

    def set_target(group, carry):
        for t in [group * 4 + i for i in range(4)]:
            rows = pl.ds(t * pitch, depth)
            for half in range(rows_ref.shape[0]):
                b_out[t, :, half * 128 : (half + 1) * 128] = rows_ref[half, rows, :].astype(bf16)
        return carry

    lax.fori_loop(0, tiles // 4, set_target, 0)
    repeat_target(b_out, b_ref)
    put_source(planes, rows_ref, 0)
    sums_ref[...] = jnp.zeros_like(sums_ref)
    for copy in copies:
        copy.wait()

    def own(step, carry):
        for group in (2 * step, 2 * step + 1):
            for i, (a, s) in enumerate(turn_group(rows_ref, group)):
                t = group * 4 + i
                a_ref[t] = a
                s_ref[t] = s
                add_pair(sums_ref, t, a, s, b_ref[t])
        return carry

    lax.fori_loop(0, tiles // 8, own, 0)

    def listed(step, carry):
        for i in range(8):
            one = local_pairs[0, step * 8 + i].astype(jnp.int32)
            two = local_pairs[1, step * 8 + i].astype(jnp.int32)
            add_pair(sums_ref, two, a_ref[one], s_ref[one], b_ref[two])
            add_pair(sums_ref, one, a_ref[two], s_ref[two], b_ref[one])
        return carry

    lax.fori_loop(0, pairs // 8, listed, 0)


def rest_kernel(
    peers,
    below,
    above,
    inbox,
    b_in,
    sums_in,
    payload,
    history,
    corner_load,
    external,
    tile_sub,
    corner_map,
    send_tile_in,
    remote_pairs_in,
    remote_count_in,
    damage_ref,
    parts_ref,
    rows_ref,
    far_rows,
    b_ref,
    sums_ref,
    send_tile,
    remote_pairs,
    remote_count,
    far_tile,
    far_live,
    sems,
):
    tiles, points = history.shape
    halves = points // 128
    groups = tiles // 4
    count = lax.axis_size("sub")
    layer = lax.axis_index("sub")
    copies = fetch(
        (send_tile_in, remote_pairs_in, remote_count_in),
        (send_tile, remote_pairs, remote_count),
        sems,
    )

    sums_ref[...] = sums_in[...]
    repeat_target(b_in, b_ref)

    def border(shift):
        def some(step, carry):
            for group in (2 * step, 2 * step + 1):
                for i, (a, s) in enumerate(turn_group(rows_ref, group)):
                    for place in (i, i + shift):
                        t = lax.rem(group * 4 + place + tiles, tiles)
                        add_pair(sums_ref, t, a, s, b_ref[t])
            return carry

        lax.fori_loop(0, groups // 2, some, 0)

    @pl.when(layer > 0)
    def lower():
        put_source([below[k] for k in range(4)], rows_ref, 0)
        border(-1)

    @pl.when(layer < count - 1)
    def upper():
        put_source([above[k] for k in range(4)], rows_ref, 0)
        border(1)

    for copy in copies:
        copy.wait()
    for which in range(2):
        planes = [
            jnp.concatenate(
                [inbox[pl.ds(half * 8 + 4 * which + k, peers, stride=8 * halves), :] for half in range(halves)], axis=1
            )
            for k in range(4)
        ]
        put_source(planes, far_rows, which * peers)

    def place(i, carry):
        h = remote_pairs[1, i]
        far_tile[h] = remote_pairs[0, i]
        far_live[h] = (i < remote_count[0]).astype(jnp.int32)
        far_tile[peers + i] = send_tile[i]
        far_live[peers + i] = 1
        return carry

    lax.fori_loop(0, peers, place, 0, unroll=peers <= 8)

    def far(step, carry):
        for group in (2 * step, 2 * step + 1):
            for i, (a, s) in enumerate(turn_group(far_rows, group)):
                t = far_tile[group * 4 + i]
                add_pair(sums_ref, t, a, s, b_ref[t], far_live[group * 4 + i].astype(f32))
        return carry

    lax.fori_loop(0, 2 * peers // 8, far, 0)

    valid = (payload[3] > 0.0).astype(f32)
    num, den = jnp.sum(sums_ref[...], axis=2)
    strain_bar = num / (den + 1.0 - valid)
    kappa = jnp.maximum(strain_bar, history[...])
    damage = 1.0 - (keep_share + (1.0 - keep_share) * jnp.exp(-softening * (kappa - 1.0))) / kappa
    damage_ref[...] = damage
    intact = (1.0 - damage) * valid

    folded = corner_load[:, :, 0:128] * intact[None, :, 0:128]
    for half in range(1, points // 128):
        cut = slice(half * 128, (half + 1) * 128)
        folded = folded + corner_load[:, :, cut] * intact[None, :, cut]
    owner = spread_rows(tile_sub[...].reshape(1, tiles))
    subs, corners = corner_map.shape
    map_rows = spread_rows(jnp.concatenate([corner_map[m : m + 1, :] for m in range(subs)], axis=1))
    sums = []
    for m in range(subs):
        chosen = jnp.where((owner == float(m))[None], folded, 0.0)
        sums.append(jnp.sum(jnp.sum(chosen, axis=1), axis=1, keepdims=True))
    sub_part = jnp.broadcast_to(jnp.concatenate(sums, axis=0), (subs * corners, 128))
    target = map_rows.astype(jnp.int32) - lax.broadcasted_iota(jnp.int32, (subs * corners, 128), 1)

    def scatter(j, carry):
        held = jnp.where(j == lax.axis_index("blk"), external[...], 0.0).reshape(1, 128)
        force = jnp.sum(jnp.where(target == j * 128, sub_part, 0.0), axis=0, keepdims=True)
        parts_ref[pl.ds(j, 1), :] = held - force
        return carry

    lax.fori_loop(0, peers, scatter, 0, unroll=peers <= 8)


def per_device(
    coords,
    strain,
    history,
    corner_load,
    tile_count,
    tile_sub,
    local_pairs,
    send_tile,
    remote_pairs,
    remote_count,
    corner_map,
    external,
):
    tiles, points = strain.shape
    halves = points // 128
    peers = lax.axis_size("blk")
    params = pltpu.CompilerParams(vmem_limit_bytes=grant)
    whole_params = pltpu.CompilerParams(vmem_limit_bytes=whole_grant)
    block = 2 * points * points

    payload, outbox = pl.pallas_call(
        functools.partial(pack_kernel, peers),
        out_shape=(
            jax.ShapeDtypeStruct((5, tiles, points), f32),
            jax.ShapeDtypeStruct((peers * halves * 8, 128), f32),
        ),
        in_specs=[anywhere] * 7,
        out_specs=(in_vmem, in_vmem),
        scratch_shapes=[pltpu.VMEM((tiles, points), f32)]
        + [pltpu.SMEM(v.shape, jnp.int32) for v in (tile_count, send_tile, remote_pairs, remote_count)]
        + [pltpu.VMEM(local_pairs.shape, jnp.int32), pltpu.SemaphoreType.DMA((7,))],
        compiler_params=whole_params,
        name="pack",
    )(coords, strain, tile_count, send_tile, remote_pairs, remote_count, local_pairs)

    layers = lax.axis_size("sub")
    below = lax.ppermute(payload, "sub", [(i, i + 1) for i in range(layers - 1)])
    above = lax.ppermute(payload, "sub", [(i + 1, i) for i in range(layers - 1)])
    inbox = lax.all_to_all(outbox, "blk", split_axis=0, concat_axis=0, tiled=True)

    b_own, sums = pl.pallas_call(
        functools.partial(own_kernel, local_pairs.shape[1]),
        out_shape=(
            jax.ShapeDtypeStruct((tiles, depth, points), bf16),
            jax.ShapeDtypeStruct((2, tiles, 8, points), f32),
        ),
        in_specs=[in_vmem],
        out_specs=(in_vmem,) * 2,
        scratch_shapes=[
            pltpu.VMEM((halves, tiles * pitch, 128), f32),
            pltpu.VMEM((tiles, points, 4 * depth), bf16),
            pltpu.VMEM((tiles, points, 128), f32),
            pltpu.VMEM((tiles, 4 * depth, points), bf16),
            pltpu.SMEM((8, 128), f32),
            pltpu.SemaphoreType.DMA((1,)),
        ],
        compiler_params=params,
        cost_estimate=pl.CostEstimate(
            flops=3 * tiles * block * depth, bytes_accessed=1 << 20, transcendentals=3 * tiles * points * points
        ),
        name="own",
    )(payload)

    damage, parts = pl.pallas_call(
        functools.partial(rest_kernel, peers),
        out_shape=(
            jax.ShapeDtypeStruct((tiles, points), f32),
            jax.ShapeDtypeStruct((peers, 128), f32),
        ),
        in_specs=[in_vmem] * 11 + [anywhere] * 3,
        out_specs=(in_vmem,) * 2,
        scratch_shapes=[
            pltpu.VMEM((halves, tiles * pitch, 128), f32),
            pltpu.VMEM((halves, 2 * peers * pitch, 128), f32),
            pltpu.VMEM((tiles, 4 * depth, points), bf16),
            pltpu.VMEM(sums.shape, f32),
        ]
        + [pltpu.SMEM(v.shape, jnp.int32) for v in (send_tile, remote_pairs, remote_count)]
        + [pltpu.SMEM((2 * peers,), jnp.int32)] * 2
        + [pltpu.SemaphoreType.DMA((3,))],
        compiler_params=params,
        cost_estimate=pl.CostEstimate(
            flops=4 * tiles * block * depth, bytes_accessed=1 << 21, transcendentals=4 * tiles * points * points
        ),
        name="rest",
    )(
        below,
        above,
        inbox,
        b_own,
        sums,
        payload,
        history,
        corner_load,
        external,
        tile_sub,
        corner_map,
        send_tile,
        remote_pairs,
        remote_count,
    )
    gathered = lax.all_to_all(parts, "blk", split_axis=0, concat_axis=0, tiled=True)
    return damage, jnp.sum(gathered, axis=0)


def solution(mesh):
    placed = (
        P(None, ("sub", "blk"), None),
        P(("sub", "blk"), None),
        P(("sub", "blk"), None),
        P(None, ("sub", "blk"), None),
        P(("sub", "blk")),
        P(("sub", "blk")),
        P(None, ("sub", "blk")),
        P(("sub", "blk")),
        P(None, ("sub", "blk")),
        P(("sub", "blk")),
        P(("sub", "blk"), None),
        P(("sub", "blk")),
    )
    return jax.shard_map(
        per_device,
        mesh=mesh,
        in_specs=placed,
        out_specs=(P(("sub", "blk"), None), P(("sub", "blk"))),
        check_vma=False,
    )
```

```python
import functools
import math

import jax
import jax.numpy as jnp
from jax import lax
from jax.experimental import pallas as pl
from jax.experimental.pallas import tpu as pltpu
from jax.sharding import PartitionSpec as P

gauss_rate = 4.0
keep_share = 0.05
softening = 0.5
coord_scale = math.sqrt(gauss_rate * math.log2(math.e))
far_off = 2048.0
depth = 32
pitch = depth + 1
grant = 24 * 1024 * 1024

f32 = jnp.float32
bf16 = jnp.bfloat16
in_vmem = pl.BlockSpec(memory_space=pltpu.VMEM)
anywhere = pl.BlockSpec(memory_space=pl.ANY)


def in_hbm(value):
    return value if value.size == 1 else pltpu.with_memory_space_constraint(value, pltpu.HBM)


def pieces(value):
    high = value.astype(bf16).astype(f32)
    rest = value - high
    middle = rest.astype(bf16).astype(f32)
    low = (rest - middle).astype(bf16).astype(f32)
    return high, middle, low


def put_rows(rows_ref, base, rows):
    for r, row in enumerate(rows):
        tiles = row.shape[0]
        for half in range(row.shape[1] // 128):
            rows_ref[half, pl.ds(base * pitch + r, tiles, stride=pitch), :] = row[:, half * 128 : (half + 1) * 128]


def point_rows(planes):
    scaled = [p * coord_scale for p in planes[:3]]
    split = [pieces(s) for s in scaled]
    norm = scaled[0] * scaled[0] + scaled[1] * scaled[1] + scaled[2] * scaled[2]
    return split, norm + jnp.where(planes[3] > 0.0, 0.0, far_off)


def put_source(planes, rows_ref, base):
    split, norm = point_rows(planes)
    ones = jnp.ones_like(norm)
    rows = []
    for high, middle, low in split:
        rows += [high, high, middle, high, low, middle]
    rows += list(pieces(-norm)) + [ones, ones, ones] + [planes[3]]
    rows += [jnp.zeros_like(norm)] * (depth - len(rows))
    put_rows(rows_ref, base, rows)


def put_target(planes, rows_ref):
    split, norm = point_rows(planes)
    ones = jnp.ones_like(norm)
    rows = []
    for high, middle, low in split:
        rows += [2.0 * v for v in (high, middle, high, low, high, middle)]
    rows += [ones, ones, ones] + list(pieces(-norm))
    rows += [jnp.zeros_like(norm)] * (depth - len(rows))
    put_rows(rows_ref, 0, rows)


def turn_group(rows_ref, group):
    turned = jnp.concatenate(
        [
            jnp.concatenate([rows_ref[half, pl.ds((group * 4 + j) * pitch, depth), :] for j in range(4)], axis=0).T
            for half in range(rows_ref.shape[0])
        ],
        axis=0,
    )
    left = turned.astype(bf16)
    column = lax.broadcasted_iota(jnp.int32, (1, 128), 1) // depth
    operands = []
    for j in range(4):
        mask = (column == j).astype(f32).astype(bf16)
        lane = depth * j + 24
        operands.append((left * mask, jnp.broadcast_to(turned[:, lane : lane + 1], turned.shape)))
    return operands


def fold(x):
    return jnp.sum(x.reshape(x.shape[0] // 8, 8, x.shape[1]), axis=0)


def column_sums(weight, s):
    load = jnp.concatenate([s] * (weight.shape[1] // 128), axis=1)
    return fold(weight * load), fold(weight)


def add_pair(sums_ref, t, a, s, b, live=None):
    weight = jnp.exp2(jnp.dot(a, b, preferred_element_type=f32))
    num, den = column_sums(weight, s)
    if live is not None:
        num, den = num * live, den * live
    sums_ref[0, t] = sums_ref[0, t] + num
    sums_ref[1, t] = sums_ref[1, t] + den


def repeat_target(compact, b_ref):
    def some_tiles(step, carry):
        for t in [step * 4 + i for i in range(4)]:
            block = compact[t]
            for j in range(4):
                b_ref[t, depth * j : depth * (j + 1), :] = block
        return carry

    lax.fori_loop(0, compact.shape[0] // 4, some_tiles, 0)


def fetch(sources, targets, sems):
    copies = [pltpu.make_async_copy(src, dst, sems.at[i]) for i, (src, dst) in enumerate(zip(sources, targets))]
    for copy in copies:
        copy.start()
    return copies


def pack_kernel(
    peers,
    coords,
    strain,
    tile_count_in,
    send_tile_in,
    remote_pairs_in,
    remote_count_in,
    local_pairs_in,
    payload,
    outbox,
    strain_here,
    tile_count,
    send_tile,
    remote_pairs,
    remote_count,
    local_pairs,
    sems,
):
    tiles, points = strain.shape
    copies = fetch(
        (coords, strain, tile_count_in, send_tile_in, remote_pairs_in, remote_count_in, local_pairs_in),
        (payload.at[0:3], strain_here, tile_count, send_tile, remote_pairs, remote_count, local_pairs),
        sems,
    )
    payload[4] = jnp.zeros((tiles, points), f32)
    for copy in copies:
        copy.wait()
    payload[4, 0:2, 0 : local_pairs.shape[1]] = local_pairs[...].astype(f32)
    lane = lax.broadcasted_iota(jnp.int32, (1, points), 1)
    for t in range(tiles):
        payload[3, t : t + 1, :] = jnp.where(lane < tile_count[t], strain_here[t : t + 1, :], 0.0)

    halves = points // 128

    def put(h, first, t, live):
        for k in range(4):
            row = payload[k, pl.ds(t, 1), :]
            if k == 3 and live is not None:
                row = row * live
            for half in range(halves):
                outbox[pl.ds((h * halves + half) * 8 + first + k, 1), :] = row[:, half * 128 : (half + 1) * 128]

    def sent(h, carry):
        put(h, 0, send_tile[h], None)
        return carry

    def listed(i, carry):
        put(remote_pairs[1, i], 4, remote_pairs[0, i], (i < remote_count[0]).astype(f32))
        return carry

    lax.fori_loop(0, peers, sent, 0, unroll=peers <= 8)
    lax.fori_loop(0, peers, listed, 0, unroll=peers <= 8)


def spread_rows(values):
    n = values.shape[1]
    wide = jnp.concatenate([values.astype(f32), jnp.zeros((1, 128 - n), f32)], axis=1)
    return jnp.broadcast_to(wide, (128, 128)).T[0:n]


def own_kernel(pairs, payload, b_out, sums_ref, rows_ref, a_ref, s_ref, b_ref, local_pairs, sems):
    tiles = payload.shape[1]
    copies = fetch((payload.at[4, 0:8, 0:128],), (local_pairs,), sems)
    planes = [payload[k] for k in range(4)]
    put_target(planes, rows_ref)

    def set_target(group, carry):
        for t in [group * 4 + i for i in range(4)]:
            rows = pl.ds(t * pitch, depth)
            for half in range(rows_ref.shape[0]):
                b_out[t, :, half * 128 : (half + 1) * 128] = rows_ref[half, rows, :].astype(bf16)
        return carry

    lax.fori_loop(0, tiles // 4, set_target, 0)
    repeat_target(b_out, b_ref)
    put_source(planes, rows_ref, 0)
    sums_ref[...] = jnp.zeros_like(sums_ref)
    for copy in copies:
        copy.wait()

    def own(step, carry):
        for group in [4 * step + g for g in range(4)]:
            for i, (a, s) in enumerate(turn_group(rows_ref, group)):
                t = group * 4 + i
                a_ref[t] = a
                s_ref[t] = s
                add_pair(sums_ref, t, a, s, b_ref[t])
        return carry

    lax.fori_loop(0, tiles // 16, own, 0)

    def listed(step, carry):
        for i in range(16):
            one = local_pairs[0, step * 16 + i].astype(jnp.int32)
            two = local_pairs[1, step * 16 + i].astype(jnp.int32)
            add_pair(sums_ref, two, a_ref[one], s_ref[one], b_ref[two])
            add_pair(sums_ref, one, a_ref[two], s_ref[two], b_ref[one])
        return carry

    lax.fori_loop(0, pairs // 16, listed, 0)


def rest_kernel(
    peers,
    below,
    above,
    inbox,
    b_in,
    sums_in,
    payload,
    history_in,
    corner_load_in,
    external_in,
    tile_sub_in,
    corner_map_in,
    send_tile_in,
    remote_pairs_in,
    remote_count_in,
    damage_out,
    parts_ref,
    damage_ref,
    history,
    corner_load,
    external,
    tile_sub,
    corner_map,
    rows_ref,
    far_rows,
    b_ref,
    sums_ref,
    send_tile,
    remote_pairs,
    remote_count,
    far_tile,
    far_live,
    sems,
):
    tiles, points = history.shape
    halves = points // 128
    groups = tiles // 4
    count = lax.axis_size("sub")
    layer = lax.axis_index("sub")
    copies = fetch(
        (
            send_tile_in,
            remote_pairs_in,
            remote_count_in,
            history_in,
            corner_load_in,
            external_in,
            tile_sub_in,
            corner_map_in,
        ),
        (send_tile, remote_pairs, remote_count, history, corner_load, external, tile_sub, corner_map),
        sems.at[0:8],
    )

    sums_ref[...] = sums_in[...]
    repeat_target(b_in, b_ref)

    def border(shift):
        def some(step, carry):
            for group in [4 * step + g for g in range(4)]:
                for i, (a, s) in enumerate(turn_group(rows_ref, group)):
                    for place in (i, i + shift):
                        t = lax.rem(group * 4 + place + tiles, tiles)
                        add_pair(sums_ref, t, a, s, b_ref[t])
            return carry

        lax.fori_loop(0, groups // 4, some, 0)

    @pl.when(layer > 0)
    def lower():
        put_source([below[k] for k in range(4)], rows_ref, 0)
        border(-1)

    @pl.when(layer < count - 1)
    def upper():
        put_source([above[k] for k in range(4)], rows_ref, 0)
        border(1)

    for copy in copies:
        copy.wait()
    for which in range(2):
        planes = [
            jnp.concatenate(
                [inbox[pl.ds(half * 8 + 4 * which + k, peers, stride=8 * halves), :] for half in range(halves)], axis=1
            )
            for k in range(4)
        ]
        put_source(planes, far_rows, which * peers)

    def place(i, carry):
        h = remote_pairs[1, i]
        far_tile[h] = remote_pairs[0, i]
        far_live[h] = (i < remote_count[0]).astype(jnp.int32)
        far_tile[peers + i] = send_tile[i]
        far_live[peers + i] = 1
        return carry

    lax.fori_loop(0, peers, place, 0, unroll=peers <= 8)

    def far(step, carry):
        for group in (2 * step, 2 * step + 1):
            for i, (a, s) in enumerate(turn_group(far_rows, group)):
                t = far_tile[group * 4 + i]
                add_pair(sums_ref, t, a, s, b_ref[t], far_live[group * 4 + i].astype(f32))
        return carry

    lax.fori_loop(0, 2 * peers // 8, far, 0)

    valid = (payload[3] > 0.0).astype(f32)
    num, den = jnp.sum(sums_ref[...], axis=2)
    strain_bar = num / (den + 1.0 - valid)
    kappa = jnp.maximum(strain_bar, history[...])
    damage = 1.0 - (keep_share + (1.0 - keep_share) * jnp.exp(-softening * (kappa - 1.0))) / kappa
    damage_ref[...] = damage
    leaving = pltpu.make_async_copy(damage_ref, damage_out, sems.at[8])
    leaving.start()
    intact = (1.0 - damage) * valid

    folded = corner_load[:, :, 0:128] * intact[None, :, 0:128]
    for half in range(1, points // 128):
        cut = slice(half * 128, (half + 1) * 128)
        folded = folded + corner_load[:, :, cut] * intact[None, :, cut]
    owner = spread_rows(tile_sub[...].reshape(1, tiles))
    subs, corners = corner_map.shape
    map_rows = spread_rows(jnp.concatenate([corner_map[m : m + 1, :] for m in range(subs)], axis=1))
    sums = []
    for m in range(subs):
        chosen = jnp.where((owner == float(m))[None], folded, 0.0)
        sums.append(jnp.sum(jnp.sum(chosen, axis=1), axis=1, keepdims=True))
    sub_part = jnp.broadcast_to(jnp.concatenate(sums, axis=0), (subs * corners, 128))
    target = map_rows.astype(jnp.int32) - lax.broadcasted_iota(jnp.int32, (subs * corners, 128), 1)

    def scatter(j, carry):
        held = jnp.where(j == lax.axis_index("blk"), external[...], 0.0).reshape(1, 128)
        force = jnp.sum(jnp.where(target == j * 128, sub_part, 0.0), axis=0, keepdims=True)
        parts_ref[pl.ds(j, 1), :] = held - force
        return carry

    lax.fori_loop(0, peers, scatter, 0, unroll=peers <= 8)
    leaving.wait()


def per_device(
    coords,
    strain,
    history,
    corner_load,
    tile_count,
    tile_sub,
    local_pairs,
    send_tile,
    remote_pairs,
    remote_count,
    corner_map,
    external,
):
    tiles, points = strain.shape
    halves = points // 128
    peers = lax.axis_size("blk")
    params = pltpu.CompilerParams(vmem_limit_bytes=grant)
    block = 2 * points * points

    payload, outbox = pl.pallas_call(
        functools.partial(pack_kernel, peers),
        out_shape=(
            pltpu.VMEM((5, tiles, points), f32),
            pltpu.VMEM((peers * halves * 8, 128), f32),
        ),
        in_specs=[anywhere] * 7,
        out_specs=(in_vmem, in_vmem),
        scratch_shapes=[pltpu.VMEM((tiles, points), f32)]
        + [pltpu.SMEM(v.shape, jnp.int32) for v in (tile_count, send_tile, remote_pairs, remote_count)]
        + [pltpu.VMEM(local_pairs.shape, jnp.int32), pltpu.SemaphoreType.DMA((7,))],
        compiler_params=params,
        name="pack",
    )(*(in_hbm(v) for v in (coords, strain, tile_count, send_tile, remote_pairs, remote_count, local_pairs)))

    layers = lax.axis_size("sub")
    below = lax.ppermute(payload, "sub", [(i, i + 1) for i in range(layers - 1)])
    above = lax.ppermute(payload, "sub", [(i + 1, i) for i in range(layers - 1)])
    inbox = lax.all_to_all(outbox, "blk", split_axis=0, concat_axis=0, tiled=True)

    b_own, sums = pl.pallas_call(
        functools.partial(own_kernel, local_pairs.shape[1]),
        out_shape=(
            jax.ShapeDtypeStruct((tiles, depth, points), bf16),
            jax.ShapeDtypeStruct((2, tiles, 8, points), f32),
        ),
        in_specs=[in_vmem],
        out_specs=(in_vmem,) * 2,
        scratch_shapes=[
            pltpu.VMEM((halves, tiles * pitch, 128), f32),
            pltpu.VMEM((tiles, points, 4 * depth), bf16),
            pltpu.VMEM((tiles, points, 128), f32),
            pltpu.VMEM((tiles, 4 * depth, points), bf16),
            pltpu.SMEM((8, 128), f32),
            pltpu.SemaphoreType.DMA((1,)),
        ],
        compiler_params=params,
        cost_estimate=pl.CostEstimate(
            flops=3 * tiles * block * depth, bytes_accessed=1 << 20, transcendentals=3 * tiles * points * points
        ),
        name="own",
    )(payload)

    damage, parts = pl.pallas_call(
        functools.partial(rest_kernel, peers),
        out_shape=(
            jax.ShapeDtypeStruct((tiles, points), f32),
            jax.ShapeDtypeStruct((peers, 128), f32),
        ),
        in_specs=[in_vmem] * 6 + [anywhere] * 8,
        out_specs=(anywhere, in_vmem),
        scratch_shapes=[pltpu.VMEM(v.shape, v.dtype) for v in (strain, history, corner_load, external, tile_sub, corner_map)]
        + [
            pltpu.VMEM((halves, tiles * pitch, 128), f32),
            pltpu.VMEM((halves, 2 * peers * pitch, 128), f32),
            pltpu.VMEM((tiles, 4 * depth, points), bf16),
            pltpu.VMEM(sums.shape, f32),
        ]
        + [pltpu.SMEM(v.shape, jnp.int32) for v in (send_tile, remote_pairs, remote_count)]
        + [pltpu.SMEM((2 * peers,), jnp.int32)] * 2
        + [pltpu.SemaphoreType.DMA((9,))],
        compiler_params=params,
        cost_estimate=pl.CostEstimate(
            flops=4 * tiles * block * depth, bytes_accessed=1 << 21, transcendentals=4 * tiles * points * points
        ),
        name="rest",
    )(
        below,
        above,
        inbox,
        b_own,
        sums,
        payload,
        *(
            in_hbm(v)
            for v in (
                history,
                corner_load,
                external,
                tile_sub,
                corner_map,
                send_tile,
                remote_pairs,
                remote_count,
            )
        ),
    )
    gathered = lax.all_to_all(parts, "blk", split_axis=0, concat_axis=0, tiled=True)
    return damage, jnp.sum(gathered, axis=0)


def solution(mesh):
    placed = (
        P(None, ("sub", "blk"), None),
        P(("sub", "blk"), None),
        P(("sub", "blk"), None),
        P(None, ("sub", "blk"), None),
        P(("sub", "blk")),
        P(("sub", "blk")),
        P(None, ("sub", "blk")),
        P(("sub", "blk")),
        P(None, ("sub", "blk")),
        P(("sub", "blk")),
        P(("sub", "blk"), None),
        P(("sub", "blk")),
    )
    return jax.shard_map(
        per_device,
        mesh=mesh,
        in_specs=placed,
        out_specs=(P(("sub", "blk"), None), P(("sub", "blk"))),
        check_vma=False,
    )
```

```python
import functools
import math

import jax
import jax.numpy as jnp
from jax import lax
from jax.experimental import pallas as pl
from jax.experimental.pallas import tpu as pltpu
from jax.sharding import PartitionSpec as P

gauss_rate = 4.0
keep_share = 0.05
softening = 0.5
coord_scale = math.sqrt(gauss_rate * math.log2(math.e))
far_off = 2048.0
depth = 32
pitch = depth + 1
grant = 24 * 1024 * 1024

f32 = jnp.float32
bf16 = jnp.bfloat16
in_vmem = pl.BlockSpec(memory_space=pltpu.VMEM)
anywhere = pl.BlockSpec(memory_space=pl.ANY)


def in_hbm(value):
    return value if value.size == 1 else pltpu.with_memory_space_constraint(value, pltpu.HBM)


def pieces(value):
    high = value.astype(bf16).astype(f32)
    rest = value - high
    middle = rest.astype(bf16).astype(f32)
    low = (rest - middle).astype(bf16).astype(f32)
    return high, middle, low


def put_rows(rows_ref, base, rows):
    for r, row in enumerate(rows):
        tiles = row.shape[0]
        for half in range(row.shape[1] // 128):
            rows_ref[half, pl.ds(base * pitch + r, tiles, stride=pitch), :] = row[:, half * 128 : (half + 1) * 128]


def point_rows(planes):
    scaled = [p * coord_scale for p in planes[:3]]
    split = [pieces(s) for s in scaled]
    norm = scaled[0] * scaled[0] + scaled[1] * scaled[1] + scaled[2] * scaled[2]
    return split, norm + jnp.where(planes[3] > 0.0, 0.0, far_off)


def put_source(planes, rows_ref, base):
    split, norm = point_rows(planes)
    ones = jnp.ones_like(norm)
    rows = []
    for high, middle, low in split:
        rows += [high, high, middle, high, low, middle]
    rows += list(pieces(-norm)) + [ones, ones, ones] + [planes[3]]
    rows += [jnp.zeros_like(norm)] * (depth - len(rows))
    put_rows(rows_ref, base, rows)


def put_target(planes, rows_ref):
    split, norm = point_rows(planes)
    ones = jnp.ones_like(norm)
    rows = []
    for high, middle, low in split:
        rows += [2.0 * v for v in (high, middle, high, low, high, middle)]
    rows += [ones, ones, ones] + list(pieces(-norm))
    rows += [jnp.zeros_like(norm)] * (depth - len(rows))
    put_rows(rows_ref, 0, rows)


def turn_group(rows_ref, group):
    turned = jnp.concatenate(
        [
            jnp.concatenate([rows_ref[half, pl.ds((group * 4 + j) * pitch, depth), :] for j in range(4)], axis=0).T
            for half in range(rows_ref.shape[0])
        ],
        axis=0,
    )
    left = turned.astype(bf16)
    column = lax.broadcasted_iota(jnp.int32, (1, 128), 1) // depth
    operands = []
    for j in range(4):
        mask = (column == j).astype(f32).astype(bf16)
        lane = depth * j + 24
        operands.append((left * mask, jnp.broadcast_to(turned[:, lane : lane + 1], turned.shape)))
    return operands


def fold(x):
    return jnp.sum(x.reshape(x.shape[0] // 8, 8, x.shape[1]), axis=0)


def column_sums(weight, s):
    load = jnp.concatenate([s] * (weight.shape[1] // 128), axis=1)
    return fold(weight * load), fold(weight)


def add_pair(sums_ref, t, a, s, b, live=None):
    weight = jnp.exp2(jnp.dot(a, b, preferred_element_type=f32))
    num, den = column_sums(weight, s)
    if live is not None:
        num, den = num * live, den * live
    sums_ref[0, t] = sums_ref[0, t] + num
    sums_ref[1, t] = sums_ref[1, t] + den


def fetch(sources, targets, sems):
    copies = [pltpu.make_async_copy(src, dst, sems.at[i]) for i, (src, dst) in enumerate(zip(sources, targets))]
    for copy in copies:
        copy.start()
    return copies


def pack_kernel(
    peers,
    coords,
    strain,
    tile_count_in,
    send_tile_in,
    remote_pairs_in,
    remote_count_in,
    local_pairs_in,
    payload,
    outbox,
    strain_here,
    tile_count,
    send_tile,
    remote_pairs,
    remote_count,
    local_pairs,
    sems,
):
    tiles, points = strain.shape
    copies = fetch(
        (coords, strain, tile_count_in, send_tile_in, remote_pairs_in, remote_count_in, local_pairs_in),
        (payload.at[0:3], strain_here, tile_count, send_tile, remote_pairs, remote_count, local_pairs),
        sems,
    )
    payload[4] = jnp.zeros((tiles, points), f32)
    for copy in copies:
        copy.wait()
    payload[4, 0:2, 0 : local_pairs.shape[1]] = local_pairs[...].astype(f32)
    lane = lax.broadcasted_iota(jnp.int32, (1, points), 1)
    for t in range(tiles):
        payload[3, t : t + 1, :] = jnp.where(lane < tile_count[t], strain_here[t : t + 1, :], 0.0)

    halves = points // 128

    def put(h, first, t, live):
        for k in range(4):
            row = payload[k, pl.ds(t, 1), :]
            if k == 3 and live is not None:
                row = row * live
            for half in range(halves):
                outbox[pl.ds((h * halves + half) * 8 + first + k, 1), :] = row[:, half * 128 : (half + 1) * 128]

    def sent(h, carry):
        put(h, 0, send_tile[h], None)
        return carry

    def listed(i, carry):
        put(remote_pairs[1, i], 4, remote_pairs[0, i], (i < remote_count[0]).astype(f32))
        return carry

    lax.fori_loop(0, peers, sent, 0, unroll=peers <= 8)
    lax.fori_loop(0, peers, listed, 0, unroll=peers <= 8)


def spread_rows(values):
    n = values.shape[1]
    wide = jnp.concatenate([values.astype(f32), jnp.zeros((1, 128 - n), f32)], axis=1)
    return jnp.broadcast_to(wide, (128, 128)).T[0:n]


def own_kernel(pairs, payload, b_ref, sums_ref, rows_ref, a_ref, s_ref, local_pairs, sems):
    tiles = payload.shape[1]
    copies = fetch((payload.at[4, 0:8, 0:128],), (local_pairs,), sems)
    planes = [payload[k] for k in range(4)]
    put_target(planes, rows_ref)

    def set_target(group, carry):
        for t in [group * 4 + i for i in range(4)]:
            rows = pl.ds(t * pitch, depth)
            for half in range(rows_ref.shape[0]):
                block = rows_ref[half, rows, :].astype(bf16)
                for j in range(4):
                    b_ref[t, depth * j : depth * (j + 1), half * 128 : (half + 1) * 128] = block
        return carry

    lax.fori_loop(0, tiles // 4, set_target, 0)
    put_source(planes, rows_ref, 0)
    sums_ref[...] = jnp.zeros_like(sums_ref)
    for copy in copies:
        copy.wait()

    def own(step, carry):
        for group in [4 * step + g for g in range(4)]:
            for i, (a, s) in enumerate(turn_group(rows_ref, group)):
                t = group * 4 + i
                a_ref[t] = a
                s_ref[t] = s
                add_pair(sums_ref, t, a, s, b_ref[t])
        return carry

    lax.fori_loop(0, tiles // 16, own, 0)

    def listed(step, carry):
        for i in range(16):
            one = local_pairs[0, step * 16 + i].astype(jnp.int32)
            two = local_pairs[1, step * 16 + i].astype(jnp.int32)
            add_pair(sums_ref, two, a_ref[one], s_ref[one], b_ref[two])
            add_pair(sums_ref, one, a_ref[two], s_ref[two], b_ref[one])
        return carry

    lax.fori_loop(0, pairs // 16, listed, 0)


def rest_kernel(
    peers,
    below,
    above,
    inbox,
    b_ref,
    sums_in,
    payload,
    history_in,
    corner_load_in,
    external_in,
    tile_sub_in,
    corner_map_in,
    send_tile_in,
    remote_pairs_in,
    remote_count_in,
    damage_ref,
    parts_ref,
    history,
    corner_load,
    external,
    tile_sub,
    corner_map,
    rows_ref,
    far_rows,
    sums_ref,
    send_tile,
    remote_pairs,
    remote_count,
    far_tile,
    far_live,
    sems,
):
    tiles, points = history.shape
    halves = points // 128
    groups = tiles // 4
    count = lax.axis_size("sub")
    layer = lax.axis_index("sub")
    copies = fetch(
        (
            send_tile_in,
            remote_pairs_in,
            remote_count_in,
            history_in,
            corner_load_in,
            external_in,
            tile_sub_in,
            corner_map_in,
        ),
        (send_tile, remote_pairs, remote_count, history, corner_load, external, tile_sub, corner_map),
        sems,
    )

    sums_ref[...] = sums_in[...]

    def border(shift):
        def some(step, carry):
            for group in [4 * step + g for g in range(4)]:
                for i, (a, s) in enumerate(turn_group(rows_ref, group)):
                    for place in (i, i + shift):
                        t = lax.rem(group * 4 + place + tiles, tiles)
                        add_pair(sums_ref, t, a, s, b_ref[t])
            return carry

        lax.fori_loop(0, groups // 4, some, 0)

    @pl.when(layer > 0)
    def lower():
        put_source([below[k] for k in range(4)], rows_ref, 0)
        border(-1)

    @pl.when(layer < count - 1)
    def upper():
        put_source([above[k] for k in range(4)], rows_ref, 0)
        border(1)

    for copy in copies:
        copy.wait()
    for which in range(2):
        planes = [
            jnp.concatenate(
                [inbox[pl.ds(half * 8 + 4 * which + k, peers, stride=8 * halves), :] for half in range(halves)], axis=1
            )
            for k in range(4)
        ]
        put_source(planes, far_rows, which * peers)

    def place(i, carry):
        h = remote_pairs[1, i]
        far_tile[h] = remote_pairs[0, i]
        far_live[h] = (i < remote_count[0]).astype(jnp.int32)
        far_tile[peers + i] = send_tile[i]
        far_live[peers + i] = 1
        return carry

    lax.fori_loop(0, peers, place, 0, unroll=peers <= 8)

    def far(step, carry):
        for group in (2 * step, 2 * step + 1):
            for i, (a, s) in enumerate(turn_group(far_rows, group)):
                t = far_tile[group * 4 + i]
                add_pair(sums_ref, t, a, s, b_ref[t], far_live[group * 4 + i].astype(f32))
        return carry

    lax.fori_loop(0, 2 * peers // 8, far, 0)

    valid = (payload[3] > 0.0).astype(f32)
    num, den = jnp.sum(sums_ref[...], axis=2)
    strain_bar = num / (den + 1.0 - valid)
    kappa = jnp.maximum(strain_bar, history[...])
    damage = 1.0 - (keep_share + (1.0 - keep_share) * jnp.exp(-softening * (kappa - 1.0))) / kappa
    damage_ref[...] = damage
    intact = (1.0 - damage) * valid

    folded = corner_load[:, :, 0:128] * intact[None, :, 0:128]
    for half in range(1, points // 128):
        cut = slice(half * 128, (half + 1) * 128)
        folded = folded + corner_load[:, :, cut] * intact[None, :, cut]
    owner = spread_rows(tile_sub[...].reshape(1, tiles))
    subs, corners = corner_map.shape
    map_rows = spread_rows(jnp.concatenate([corner_map[m : m + 1, :] for m in range(subs)], axis=1))
    sums = []
    for m in range(subs):
        chosen = jnp.where((owner == float(m))[None], folded, 0.0)
        sums.append(jnp.sum(jnp.sum(chosen, axis=1), axis=1, keepdims=True))
    sub_part = jnp.broadcast_to(jnp.concatenate(sums, axis=0), (subs * corners, 128))
    target = map_rows.astype(jnp.int32) - lax.broadcasted_iota(jnp.int32, (subs * corners, 128), 1)

    def scatter(j, carry):
        held = jnp.where(j == lax.axis_index("blk"), external[...], 0.0).reshape(1, 128)
        force = jnp.sum(jnp.where(target == j * 128, sub_part, 0.0), axis=0, keepdims=True)
        parts_ref[pl.ds(j, 1), :] = held - force
        return carry

    lax.fori_loop(0, peers, scatter, 0, unroll=peers <= 8)


def leave_kernel(damage, damage_out, sem):
    copy = pltpu.make_async_copy(damage, damage_out, sem)
    copy.start()
    copy.wait()


def per_device(
    coords,
    strain,
    history,
    corner_load,
    tile_count,
    tile_sub,
    local_pairs,
    send_tile,
    remote_pairs,
    remote_count,
    corner_map,
    external,
):
    tiles, points = strain.shape
    halves = points // 128
    peers = lax.axis_size("blk")
    params = pltpu.CompilerParams(vmem_limit_bytes=grant)
    block = 2 * points * points

    payload, outbox = pl.pallas_call(
        functools.partial(pack_kernel, peers),
        out_shape=(
            pltpu.VMEM((5, tiles, points), f32),
            pltpu.VMEM((peers * halves * 8, 128), f32),
        ),
        in_specs=[anywhere] * 7,
        out_specs=(in_vmem, in_vmem),
        scratch_shapes=[pltpu.VMEM((tiles, points), f32)]
        + [pltpu.SMEM(v.shape, jnp.int32) for v in (tile_count, send_tile, remote_pairs, remote_count)]
        + [pltpu.VMEM(local_pairs.shape, jnp.int32), pltpu.SemaphoreType.DMA((7,))],
        compiler_params=params,
        name="pack",
    )(*(in_hbm(v) for v in (coords, strain, tile_count, send_tile, remote_pairs, remote_count, local_pairs)))

    layers = lax.axis_size("sub")
    below = lax.ppermute(payload, "sub", [(i, i + 1) for i in range(layers - 1)])
    above = lax.ppermute(payload, "sub", [(i + 1, i) for i in range(layers - 1)])
    inbox = lax.all_to_all(outbox, "blk", split_axis=0, concat_axis=0, tiled=True)

    b_own, sums = pl.pallas_call(
        functools.partial(own_kernel, local_pairs.shape[1]),
        out_shape=(
            jax.ShapeDtypeStruct((tiles, 4 * depth, points), bf16),
            jax.ShapeDtypeStruct((2, tiles, 8, points), f32),
        ),
        in_specs=[in_vmem],
        out_specs=(in_vmem,) * 2,
        scratch_shapes=[
            pltpu.VMEM((halves, tiles * pitch, 128), f32),
            pltpu.VMEM((tiles, points, 4 * depth), bf16),
            pltpu.VMEM((tiles, points, 128), f32),
            pltpu.SMEM((8, 128), f32),
            pltpu.SemaphoreType.DMA((1,)),
        ],
        compiler_params=params,
        cost_estimate=pl.CostEstimate(
            flops=3 * tiles * block * depth, bytes_accessed=1 << 20, transcendentals=3 * tiles * points * points
        ),
        name="own",
    )(payload)

    damage, parts = pl.pallas_call(
        functools.partial(rest_kernel, peers),
        out_shape=(
            pltpu.VMEM((tiles, points), f32),
            pltpu.VMEM((peers, 128), f32),
        ),
        in_specs=[in_vmem] * 6 + [anywhere] * 8,
        out_specs=(in_vmem, in_vmem),
        scratch_shapes=[pltpu.VMEM(v.shape, v.dtype) for v in (history, corner_load, external, tile_sub, corner_map)]
        + [
            pltpu.VMEM((halves, tiles * pitch, 128), f32),
            pltpu.VMEM((halves, 2 * peers * pitch, 128), f32),
            pltpu.VMEM(sums.shape, f32),
        ]
        + [pltpu.SMEM(v.shape, jnp.int32) for v in (send_tile, remote_pairs, remote_count)]
        + [pltpu.SMEM((2 * peers,), jnp.int32)] * 2
        + [pltpu.SemaphoreType.DMA((8,))],
        compiler_params=params,
        cost_estimate=pl.CostEstimate(
            flops=4 * tiles * block * depth, bytes_accessed=1 << 21, transcendentals=4 * tiles * points * points
        ),
        name="rest",
    )(
        below,
        above,
        inbox,
        b_own,
        sums,
        payload,
        *(
            in_hbm(v)
            for v in (
                history,
                corner_load,
                external,
                tile_sub,
                corner_map,
                send_tile,
                remote_pairs,
                remote_count,
            )
        ),
    )
    gathered = lax.all_to_all(parts, "blk", split_axis=0, concat_axis=0, tiled=True)
    damage = pl.pallas_call(
        leave_kernel,
        out_shape=jax.ShapeDtypeStruct((tiles, points), f32),
        in_specs=[in_vmem],
        out_specs=anywhere,
        scratch_shapes=[pltpu.SemaphoreType.DMA],
        compiler_params=params,
        cost_estimate=pl.CostEstimate(flops=0, bytes_accessed=1 << 22, transcendentals=0),
        name="leave",
    )(damage)
    return damage, jnp.sum(gathered, axis=0)


def solution(mesh):
    placed = (
        P(None, ("sub", "blk"), None),
        P(("sub", "blk"), None),
        P(("sub", "blk"), None),
        P(None, ("sub", "blk"), None),
        P(("sub", "blk")),
        P(("sub", "blk")),
        P(None, ("sub", "blk")),
        P(("sub", "blk")),
        P(None, ("sub", "blk")),
        P(("sub", "blk")),
        P(("sub", "blk"), None),
        P(("sub", "blk")),
    )
    return jax.shard_map(
        per_device,
        mesh=mesh,
        in_specs=placed,
        out_specs=(P(("sub", "blk"), None), P(("sub", "blk"))),
        check_vma=False,
    )
```

```python
import functools
import math

import jax
import jax.numpy as jnp
from jax import lax
from jax.experimental import pallas as pl
from jax.experimental.pallas import tpu as pltpu
from jax.sharding import PartitionSpec as P

gauss_rate = 4.0
keep_share = 0.05
softening = 0.5
coord_scale = math.sqrt(gauss_rate * math.log2(math.e))
far_off = 2048.0
depth = 32
pitch = depth + 1
grant = 24 * 1024 * 1024

f32 = jnp.float32
bf16 = jnp.bfloat16
in_vmem = pl.BlockSpec(memory_space=pltpu.VMEM)
anywhere = pl.BlockSpec(memory_space=pl.ANY)


def in_hbm(value):
    return value if value.size == 1 else pltpu.with_memory_space_constraint(value, pltpu.HBM)


def pieces(value):
    high = value.astype(bf16).astype(f32)
    rest = value - high
    middle = rest.astype(bf16).astype(f32)
    low = (rest - middle).astype(bf16).astype(f32)
    return high, middle, low


def put_rows(rows_ref, base, rows):
    for r, row in enumerate(rows):
        tiles = row.shape[0]
        for half in range(row.shape[1] // 128):
            rows_ref[half, pl.ds(base * pitch + r, tiles, stride=pitch), :] = row[:, half * 128 : (half + 1) * 128]


def point_rows(planes):
    scaled = [p * coord_scale for p in planes[:3]]
    split = [pieces(s) for s in scaled]
    norm = scaled[0] * scaled[0] + scaled[1] * scaled[1] + scaled[2] * scaled[2]
    return split, norm + jnp.where(planes[3] > 0.0, 0.0, far_off)


def put_source(planes, rows_ref, base):
    split, norm = point_rows(planes)
    ones = jnp.ones_like(norm)
    rows = []
    for high, middle, low in split:
        rows += [high, high, middle, high, low, middle]
    rows += list(pieces(-norm)) + [ones, ones, ones] + [planes[3]]
    rows += [jnp.zeros_like(norm)] * (depth - len(rows))
    put_rows(rows_ref, base, rows)


def put_target(planes, rows_ref):
    split, norm = point_rows(planes)
    ones = jnp.ones_like(norm)
    rows = []
    for high, middle, low in split:
        rows += [2.0 * v for v in (high, middle, high, low, high, middle)]
    rows += [ones, ones, ones] + list(pieces(-norm))
    rows += [jnp.zeros_like(norm)] * (depth - len(rows))
    put_rows(rows_ref, 0, rows)


def turn_group(rows_ref, group):
    turned = jnp.concatenate(
        [
            jnp.concatenate([rows_ref[half, pl.ds((group * 4 + j) * pitch, depth), :] for j in range(4)], axis=0).T
            for half in range(rows_ref.shape[0])
        ],
        axis=0,
    )
    left = turned.astype(bf16)
    column = lax.broadcasted_iota(jnp.int32, (1, 128), 1) // depth
    operands = []
    for j in range(4):
        mask = (column == j).astype(f32).astype(bf16)
        lane = depth * j + 24
        operands.append((left * mask, jnp.broadcast_to(turned[:, lane : lane + 1], turned.shape)))
    return operands


def fold(x):
    return jnp.sum(x.reshape(x.shape[0] // 8, 8, x.shape[1]), axis=0)


def column_sums(weight, s):
    load = jnp.concatenate([s] * (weight.shape[1] // 128), axis=1)
    return fold(weight * load), fold(weight)


def add_pair(sums_ref, t, a, s, b, live=None):
    weight = jnp.exp2(jnp.dot(a, b, preferred_element_type=f32))
    num, den = column_sums(weight, s)
    if live is not None:
        num, den = num * live, den * live
    sums_ref[0, t] = sums_ref[0, t] + num
    sums_ref[1, t] = sums_ref[1, t] + den


def repeat_target(compact, b_ref):
    def some_tiles(step, carry):
        for t in [step * 4 + i for i in range(4)]:
            block = compact[t]
            for j in range(4):
                b_ref[t, depth * j : depth * (j + 1), :] = block
        return carry

    lax.fori_loop(0, compact.shape[0] // 4, some_tiles, 0)


def fetch(sources, targets, sems):
    copies = [pltpu.make_async_copy(src, dst, sems.at[i]) for i, (src, dst) in enumerate(zip(sources, targets))]
    for copy in copies:
        copy.start()
    return copies


def pack_kernel(
    peers,
    coords,
    strain,
    tile_count_in,
    send_tile_in,
    remote_pairs_in,
    remote_count_in,
    local_pairs_in,
    payload,
    outbox,
    strain_here,
    tile_count,
    send_tile,
    remote_pairs,
    remote_count,
    local_pairs,
    sems,
):
    tiles, points = strain.shape
    copies = fetch(
        (coords, strain, tile_count_in, send_tile_in, remote_pairs_in, remote_count_in, local_pairs_in),
        (payload.at[0:3], strain_here, tile_count, send_tile, remote_pairs, remote_count, local_pairs),
        sems,
    )
    payload[4] = jnp.zeros((tiles, points), f32)
    for copy in copies:
        copy.wait()
    payload[4, 0:2, 0 : local_pairs.shape[1]] = local_pairs[...].astype(f32)
    lane = lax.broadcasted_iota(jnp.int32, (1, points), 1)
    for t in range(tiles):
        payload[3, t : t + 1, :] = jnp.where(lane < tile_count[t], strain_here[t : t + 1, :], 0.0)

    halves = points // 128

    def put(h, first, t, live):
        for k in range(4):
            row = payload[k, pl.ds(t, 1), :]
            if k == 3 and live is not None:
                row = row * live
            for half in range(halves):
                outbox[pl.ds((h * halves + half) * 8 + first + k, 1), :] = row[:, half * 128 : (half + 1) * 128]

    def sent(h, carry):
        put(h, 0, send_tile[h], None)
        return carry

    def listed(i, carry):
        put(remote_pairs[1, i], 4, remote_pairs[0, i], (i < remote_count[0]).astype(f32))
        return carry

    lax.fori_loop(0, peers, sent, 0, unroll=peers <= 8)
    lax.fori_loop(0, peers, listed, 0, unroll=peers <= 8)


def spread_rows(values):
    n = values.shape[1]
    wide = jnp.concatenate([values.astype(f32), jnp.zeros((1, 128 - n), f32)], axis=1)
    return jnp.broadcast_to(wide, (128, 128)).T[0:n]


def own_kernel(pairs, payload, b_out, sums_ref, rows_ref, a_ref, s_ref, b_ref, local_pairs, sems):
    tiles = payload.shape[1]
    copies = fetch((payload.at[4, 0:8, 0:128],), (local_pairs,), sems)
    planes = [payload[k] for k in range(4)]
    put_target(planes, rows_ref)

    def set_target(group, carry):
        for t in [group * 4 + i for i in range(4)]:
            rows = pl.ds(t * pitch, depth)
            for half in range(rows_ref.shape[0]):
                b_out[t, :, half * 128 : (half + 1) * 128] = rows_ref[half, rows, :].astype(bf16)
        return carry

    lax.fori_loop(0, tiles // 4, set_target, 0)
    repeat_target(b_out, b_ref)
    put_source(planes, rows_ref, 0)
    sums_ref[...] = jnp.zeros_like(sums_ref)
    for copy in copies:
        copy.wait()

    def own(step, carry):
        for group in [4 * step + g for g in range(4)]:
            for i, (a, s) in enumerate(turn_group(rows_ref, group)):
                t = group * 4 + i
                a_ref[t] = a
                s_ref[t] = s
                add_pair(sums_ref, t, a, s, b_ref[t])
        return carry

    lax.fori_loop(0, tiles // 16, own, 0)

    def listed(step, carry):
        for i in range(16):
            one = local_pairs[0, step * 16 + i].astype(jnp.int32)
            two = local_pairs[1, step * 16 + i].astype(jnp.int32)
            add_pair(sums_ref, two, a_ref[one], s_ref[one], b_ref[two])
            add_pair(sums_ref, one, a_ref[two], s_ref[two], b_ref[one])
        return carry

    lax.fori_loop(0, pairs // 16, listed, 0)


def rest_kernel(
    peers,
    late,
    soon,
    inbox,
    b_in,
    sums_in,
    payload,
    history_in,
    corner_load_in,
    external_in,
    tile_sub_in,
    corner_map_in,
    send_tile_in,
    remote_pairs_in,
    remote_count_in,
    damage_out,
    parts_ref,
    damage_ref,
    history,
    corner_load,
    external,
    tile_sub,
    corner_map,
    rows_ref,
    far_rows,
    b_ref,
    sums_ref,
    send_tile,
    remote_pairs,
    remote_count,
    far_tile,
    far_live,
    sems,
):
    tiles, points = history.shape
    halves = points // 128
    groups = tiles // 4
    count = lax.axis_size("sub")
    layer = lax.axis_index("sub")
    copies = fetch(
        (
            send_tile_in,
            remote_pairs_in,
            remote_count_in,
            history_in,
            corner_load_in,
            external_in,
            tile_sub_in,
            corner_map_in,
        ),
        (send_tile, remote_pairs, remote_count, history, corner_load, external, tile_sub, corner_map),
        sems.at[0:8],
    )

    sums_ref[...] = sums_in[...]
    repeat_target(b_in, b_ref)

    def border(tiles_in, partner, shift):
        def some(step, carry):
            for group in [4 * step + g for g in range(4)]:
                for i, (a, s) in enumerate(turn_group(rows_ref, group)):
                    u = group * 4 + i
                    add_pair(sums_ref, u, a, s, b_ref[u])
                    t = lax.rem(u + shift + tiles, tiles)
                    add_pair(sums_ref, t, a, s, b_ref[t])
            return carry

        @pl.when((partner >= 0) & (partner < count))
        def both():
            put_source([tiles_in[k] for k in range(4)], rows_ref, 0)
            lax.fori_loop(0, groups // 4, some, 0)

    up = 1 - 2 * lax.rem(layer, 2)
    border(soon, layer - up, -up)
    border(late, layer + up, up)

    for copy in copies:
        copy.wait()
    for which in range(2):
        planes = [
            jnp.concatenate(
                [inbox[pl.ds(half * 8 + 4 * which + k, peers, stride=8 * halves), :] for half in range(halves)], axis=1
            )
            for k in range(4)
        ]
        put_source(planes, far_rows, which * peers)

    def place(i, carry):
        h = remote_pairs[1, i]
        far_tile[h] = remote_pairs[0, i]
        far_live[h] = (i < remote_count[0]).astype(jnp.int32)
        far_tile[peers + i] = send_tile[i]
        far_live[peers + i] = 1
        return carry

    lax.fori_loop(0, peers, place, 0, unroll=peers <= 8)

    def far(step, carry):
        for group in [4 * step + g for g in range(4)]:
            for i, (a, s) in enumerate(turn_group(far_rows, group)):
                t = far_tile[group * 4 + i]
                add_pair(sums_ref, t, a, s, b_ref[t], far_live[group * 4 + i].astype(f32))
        return carry

    lax.fori_loop(0, 2 * peers // 16, far, 0)

    valid = (payload[3] > 0.0).astype(f32)
    num, den = jnp.sum(sums_ref[...], axis=2)
    strain_bar = num / (den + 1.0 - valid)
    kappa = jnp.maximum(strain_bar, history[...])
    damage = 1.0 - (keep_share + (1.0 - keep_share) * jnp.exp(-softening * (kappa - 1.0))) / kappa
    damage_ref[...] = damage
    leaving = pltpu.make_async_copy(damage_ref, damage_out, sems.at[8])
    leaving.start()
    intact = (1.0 - damage) * valid

    folded = corner_load[:, :, 0:128] * intact[None, :, 0:128]
    for half in range(1, points // 128):
        cut = slice(half * 128, (half + 1) * 128)
        folded = folded + corner_load[:, :, cut] * intact[None, :, cut]
    owner = spread_rows(tile_sub[...].reshape(1, tiles))
    subs, corners = corner_map.shape
    map_rows = spread_rows(jnp.concatenate([corner_map[m : m + 1, :] for m in range(subs)], axis=1))
    sums = []
    for m in range(subs):
        chosen = jnp.where((owner == float(m))[None], folded, 0.0)
        sums.append(jnp.sum(jnp.sum(chosen, axis=1), axis=1, keepdims=True))
    sub_part = jnp.broadcast_to(jnp.concatenate(sums, axis=0), (subs * corners, 128))
    target = map_rows.astype(jnp.int32) - lax.broadcasted_iota(jnp.int32, (subs * corners, 128), 1)

    def scatter(j, carry):
        held = jnp.where(j == lax.axis_index("blk"), external[...], 0.0).reshape(1, 128)
        force = jnp.sum(jnp.where(target == j * 128, sub_part, 0.0), axis=0, keepdims=True)
        parts_ref[pl.ds(j, 1), :] = held - force
        return carry

    lax.fori_loop(0, peers, scatter, 0, unroll=peers <= 8)
    leaving.wait()


def per_device(
    coords,
    strain,
    history,
    corner_load,
    tile_count,
    tile_sub,
    local_pairs,
    send_tile,
    remote_pairs,
    remote_count,
    corner_map,
    external,
):
    tiles, points = strain.shape
    halves = points // 128
    peers = lax.axis_size("blk")
    params = pltpu.CompilerParams(vmem_limit_bytes=grant)
    block = 2 * points * points

    payload, outbox = pl.pallas_call(
        functools.partial(pack_kernel, peers),
        out_shape=(
            pltpu.VMEM((5, tiles, points), f32),
            pltpu.VMEM((peers * halves * 8, 128), f32),
        ),
        in_specs=[anywhere] * 7,
        out_specs=(in_vmem, in_vmem),
        scratch_shapes=[pltpu.VMEM((tiles, points), f32)]
        + [pltpu.SMEM(v.shape, jnp.int32) for v in (tile_count, send_tile, remote_pairs, remote_count)]
        + [pltpu.VMEM(local_pairs.shape, jnp.int32), pltpu.SemaphoreType.DMA((7,))],
        compiler_params=params,
        name="pack",
    )(*(in_hbm(v) for v in (coords, strain, tile_count, send_tile, remote_pairs, remote_count, local_pairs)))

    layers = lax.axis_size("sub")
    late, soon = [
        lax.ppermute(payload, "sub", [p for i in range(first, layers - 1, 2) for p in ((i, i + 1), (i + 1, i))])
        for first in (0, 1)
    ]
    inbox = lax.all_to_all(outbox, "blk", split_axis=0, concat_axis=0, tiled=True)

    b_own, sums = pl.pallas_call(
        functools.partial(own_kernel, local_pairs.shape[1]),
        out_shape=(
            jax.ShapeDtypeStruct((tiles, depth, points), bf16),
            jax.ShapeDtypeStruct((2, tiles, 8, points), f32),
        ),
        in_specs=[in_vmem],
        out_specs=(in_vmem,) * 2,
        scratch_shapes=[
            pltpu.VMEM((halves, tiles * pitch, 128), f32),
            pltpu.VMEM((tiles, points, 4 * depth), bf16),
            pltpu.VMEM((tiles, points, 128), f32),
            pltpu.VMEM((tiles, 4 * depth, points), bf16),
            pltpu.SMEM((8, 128), f32),
            pltpu.SemaphoreType.DMA((1,)),
        ],
        compiler_params=params,
        cost_estimate=pl.CostEstimate(
            flops=3 * tiles * block * depth, bytes_accessed=1 << 20, transcendentals=3 * tiles * points * points
        ),
        name="own",
    )(payload)

    damage, parts = pl.pallas_call(
        functools.partial(rest_kernel, peers),
        out_shape=(
            jax.ShapeDtypeStruct((tiles, points), f32),
            jax.ShapeDtypeStruct((peers, 128), f32),
        ),
        in_specs=[in_vmem] * 6 + [anywhere] * 8,
        out_specs=(anywhere, in_vmem),
        scratch_shapes=[pltpu.VMEM(v.shape, v.dtype) for v in (strain, history, corner_load, external, tile_sub, corner_map)]
        + [
            pltpu.VMEM((halves, tiles * pitch, 128), f32),
            pltpu.VMEM((halves, 2 * peers * pitch, 128), f32),
            pltpu.VMEM((tiles, 4 * depth, points), bf16),
            pltpu.VMEM(sums.shape, f32),
        ]
        + [pltpu.SMEM(v.shape, jnp.int32) for v in (send_tile, remote_pairs, remote_count)]
        + [pltpu.SMEM((2 * peers,), jnp.int32)] * 2
        + [pltpu.SemaphoreType.DMA((9,))],
        compiler_params=params,
        cost_estimate=pl.CostEstimate(
            flops=4 * tiles * block * depth, bytes_accessed=1 << 21, transcendentals=4 * tiles * points * points
        ),
        name="rest",
    )(
        late,
        soon,
        inbox,
        b_own,
        sums,
        payload,
        *(
            in_hbm(v)
            for v in (
                history,
                corner_load,
                external,
                tile_sub,
                corner_map,
                send_tile,
                remote_pairs,
                remote_count,
            )
        ),
    )
    gathered = lax.all_to_all(parts, "blk", split_axis=0, concat_axis=0, tiled=True)
    return damage, jnp.sum(gathered, axis=0)


def solution(mesh):
    placed = (
        P(None, ("sub", "blk"), None),
        P(("sub", "blk"), None),
        P(("sub", "blk"), None),
        P(None, ("sub", "blk"), None),
        P(("sub", "blk")),
        P(("sub", "blk")),
        P(None, ("sub", "blk")),
        P(("sub", "blk")),
        P(None, ("sub", "blk")),
        P(("sub", "blk")),
        P(("sub", "blk"), None),
        P(("sub", "blk")),
    )
    return jax.shard_map(
        per_device,
        mesh=mesh,
        in_specs=placed,
        out_specs=(P(("sub", "blk"), None), P(("sub", "blk"))),
        check_vma=False,
    )
```

```python
import functools
import math

import jax
import jax.numpy as jnp
from jax import lax
from jax.experimental import pallas as pl
from jax.experimental.pallas import tpu as pltpu
from jax.sharding import PartitionSpec as P

gauss_rate = 4.0
keep_share = 0.05
softening = 0.5
coord_scale = math.sqrt(gauss_rate * math.log2(math.e))
far_off = 2048.0
depth = 32
pitch = depth + 1
grant = 24 * 1024 * 1024

f32 = jnp.float32
bf16 = jnp.bfloat16
in_vmem = pl.BlockSpec(memory_space=pltpu.VMEM)
anywhere = pl.BlockSpec(memory_space=pl.ANY)


def in_hbm(value):
    return value if value.size == 1 else pltpu.with_memory_space_constraint(value, pltpu.HBM)


def pieces(value):
    high = value.astype(bf16).astype(f32)
    rest = value - high
    middle = rest.astype(bf16).astype(f32)
    low = (rest - middle).astype(bf16).astype(f32)
    return high, middle, low


def put_rows(rows_ref, base, rows):
    for r, row in enumerate(rows):
        tiles = row.shape[0]
        for half in range(row.shape[1] // 128):
            rows_ref[half, pl.ds(base * pitch + r, tiles, stride=pitch), :] = row[:, half * 128 : (half + 1) * 128]


def point_rows(planes):
    scaled = [p * coord_scale for p in planes[:3]]
    split = [pieces(s) for s in scaled]
    norm = scaled[0] * scaled[0] + scaled[1] * scaled[1] + scaled[2] * scaled[2]
    return split, norm + jnp.where(planes[3] > 0.0, 0.0, far_off)


def put_source(planes, rows_ref, base):
    split, norm = point_rows(planes)
    ones = jnp.ones_like(norm)
    rows = []
    for high, middle, low in split:
        rows += [high, high, middle, high, low, middle]
    rows += list(pieces(-norm)) + [ones, ones, ones] + [planes[3]]
    rows += [jnp.zeros_like(norm)] * (depth - len(rows))
    put_rows(rows_ref, base, rows)


def put_target(planes, rows_ref):
    split, norm = point_rows(planes)
    ones = jnp.ones_like(norm)
    rows = []
    for high, middle, low in split:
        rows += [2.0 * v for v in (high, middle, high, low, high, middle)]
    rows += [ones, ones, ones] + list(pieces(-norm))
    rows += [jnp.zeros_like(norm)] * (depth - len(rows))
    put_rows(rows_ref, 0, rows)


def turn_group(rows_ref, group):
    turned = jnp.concatenate(
        [
            jnp.concatenate([rows_ref[half, pl.ds((group * 4 + j) * pitch, depth), :] for j in range(4)], axis=0).T
            for half in range(rows_ref.shape[0])
        ],
        axis=0,
    )
    lanes = [depth * j + 24 for j in range(4)]
    return turned.astype(bf16), [jnp.broadcast_to(turned[:, n : n + 1], turned.shape) for n in lanes]


def placed(b, j):
    above, below = [jnp.zeros((depth * n, b.shape[1]), bf16) for n in (j, 3 - j)]
    return jnp.concatenate([above] * (j > 0) + [b] + [below] * (j < 3), axis=0)


def fold(x):
    return jnp.sum(x.reshape(x.shape[0] // 8, 8, x.shape[1]), axis=0)


def column_sums(weight, s):
    load = jnp.concatenate([s] * (weight.shape[1] // 128), axis=1)
    return fold(weight * load), fold(weight)


def add_pair(sums_ref, t, a, s, b, live=None):
    weight = jnp.exp2(jnp.dot(a, b, preferred_element_type=f32))
    num, den = column_sums(weight, s)
    if live is not None:
        num, den = num * live, den * live
    sums_ref[0, t] = sums_ref[0, t] + num
    sums_ref[1, t] = sums_ref[1, t] + den


def repeat_target(compact, b_ref):
    def some_tiles(step, carry):
        for t in [step * 4 + i for i in range(4)]:
            block = compact[t]
            for j in range(4):
                b_ref[t, depth * j : depth * (j + 1), :] = block
        return carry

    lax.fori_loop(0, compact.shape[0] // 4, some_tiles, 0)


def fetch(sources, targets, sems):
    copies = [pltpu.make_async_copy(src, dst, sems.at[i]) for i, (src, dst) in enumerate(zip(sources, targets))]
    for copy in copies:
        copy.start()
    return copies


def pack_kernel(
    peers,
    coords,
    strain,
    tile_count_in,
    send_tile_in,
    remote_pairs_in,
    remote_count_in,
    local_pairs_in,
    payload,
    outbox,
    strain_here,
    tile_count,
    send_tile,
    remote_pairs,
    remote_count,
    local_pairs,
    sems,
):
    tiles, points = strain.shape
    copies = fetch(
        (coords, strain, tile_count_in, send_tile_in, remote_pairs_in, remote_count_in, local_pairs_in),
        (payload.at[0:3], strain_here, tile_count, send_tile, remote_pairs, remote_count, local_pairs),
        sems,
    )
    payload[4] = jnp.zeros((tiles, points), f32)
    for copy in copies:
        copy.wait()
    payload[4, 0:2, 0 : local_pairs.shape[1]] = local_pairs[...].astype(f32)
    lane = lax.broadcasted_iota(jnp.int32, (1, points), 1)
    for t in range(tiles):
        payload[3, t : t + 1, :] = jnp.where(lane < tile_count[t], strain_here[t : t + 1, :], 0.0)

    halves = points // 128

    def put(h, first, t, live):
        for k in range(4):
            row = payload[k, pl.ds(t, 1), :]
            if k == 3 and live is not None:
                row = row * live
            for half in range(halves):
                outbox[pl.ds((h * halves + half) * 8 + first + k, 1), :] = row[:, half * 128 : (half + 1) * 128]

    def sent(h, carry):
        put(h, 0, send_tile[h], None)
        return carry

    def listed(i, carry):
        put(remote_pairs[1, i], 4, remote_pairs[0, i], (i < remote_count[0]).astype(f32))
        return carry

    lax.fori_loop(0, peers, sent, 0, unroll=peers <= 8)
    lax.fori_loop(0, peers, listed, 0, unroll=peers <= 8)


def spread_rows(values):
    n = values.shape[1]
    wide = jnp.concatenate([values.astype(f32), jnp.zeros((1, 128 - n), f32)], axis=1)
    return jnp.broadcast_to(wide, (128, 128)).T[0:n]


def own_kernel(pairs, payload, b_out, sums_ref, rows_ref, a_ref, s_ref, b_ref, local_pairs, sems):
    tiles = payload.shape[1]
    copies = fetch((payload.at[4, 0:8, 0:128],), (local_pairs,), sems)
    planes = [payload[k] for k in range(4)]
    put_target(planes, rows_ref)

    def set_target(group, carry):
        for t in [group * 4 + i for i in range(4)]:
            rows = pl.ds(t * pitch, depth)
            for half in range(rows_ref.shape[0]):
                b_out[t, :, half * 128 : (half + 1) * 128] = rows_ref[half, rows, :].astype(bf16)
        return carry

    lax.fori_loop(0, tiles // 4, set_target, 0)
    repeat_target(b_out, b_ref)
    put_source(planes, rows_ref, 0)
    sums_ref[...] = jnp.zeros_like(sums_ref)
    for copy in copies:
        copy.wait()

    column = lax.broadcasted_iota(jnp.int32, (1, 4 * depth), 1) // depth

    def own(step, carry):
        for group in [8 * step + g for g in range(8)]:
            left, loads = turn_group(rows_ref, group)
            for i, s in enumerate(loads):
                t = group * 4 + i
                a = left * (column == i).astype(f32).astype(bf16)
                a_ref[t] = a
                s_ref[t] = s
                add_pair(sums_ref, t, a, s, b_ref[t])
        return carry

    lax.fori_loop(0, tiles // 32, own, 0)

    def listed(step, carry):
        for i in range(32):
            one = local_pairs[0, step * 32 + i].astype(jnp.int32)
            two = local_pairs[1, step * 32 + i].astype(jnp.int32)
            add_pair(sums_ref, two, a_ref[one], s_ref[one], b_ref[two])
            add_pair(sums_ref, one, a_ref[two], s_ref[two], b_ref[one])
        return carry

    lax.fori_loop(0, pairs // 32, listed, 0)


def rest_kernel(
    peers,
    late,
    soon,
    inbox,
    b_ref,
    sums_in,
    payload,
    history_in,
    corner_load_in,
    external_in,
    tile_sub_in,
    corner_map_in,
    send_tile_in,
    remote_pairs_in,
    remote_count_in,
    damage_out,
    parts_ref,
    damage_ref,
    history,
    corner_load,
    external,
    tile_sub,
    corner_map,
    rows_ref,
    far_rows,
    sums_ref,
    send_tile,
    remote_pairs,
    remote_count,
    far_tile,
    far_live,
    sems,
):
    tiles, points = history.shape
    halves = points // 128
    groups = tiles // 4
    count = lax.axis_size("sub")
    layer = lax.axis_index("sub")
    copies = fetch(
        (
            send_tile_in,
            remote_pairs_in,
            remote_count_in,
            history_in,
            corner_load_in,
            external_in,
            tile_sub_in,
            corner_map_in,
        ),
        (send_tile, remote_pairs, remote_count, history, corner_load, external, tile_sub, corner_map),
        sems.at[0:8],
    )

    sums_ref[...] = sums_in[...]

    def border(tiles_in, partner, shift):
        def some(step, carry):
            for group in [8 * step + g for g in range(8)]:
                left, loads = turn_group(rows_ref, group)
                for i, s in enumerate(loads):
                    u = group * 4 + i
                    add_pair(sums_ref, u, left, s, placed(b_ref[u], i))
                    t = lax.rem(u + shift + tiles, tiles)
                    add_pair(sums_ref, t, left, s, placed(b_ref[t], i))
            return carry

        @pl.when((partner >= 0) & (partner < count))
        def both():
            put_source([tiles_in[k] for k in range(4)], rows_ref, 0)
            lax.fori_loop(0, groups // 8, some, 0)

    up = 1 - 2 * lax.rem(layer, 2)
    border(soon, layer - up, -up)
    border(late, layer + up, up)

    for copy in copies:
        copy.wait()
    for which in range(2):
        planes = [
            jnp.concatenate(
                [inbox[pl.ds(half * 8 + 4 * which + k, peers, stride=8 * halves), :] for half in range(halves)], axis=1
            )
            for k in range(4)
        ]
        put_source(planes, far_rows, which * peers)

    def place(i, carry):
        h = remote_pairs[1, i]
        far_tile[h] = remote_pairs[0, i]
        far_live[h] = (i < remote_count[0]).astype(jnp.int32)
        far_tile[peers + i] = send_tile[i]
        far_live[peers + i] = 1
        return carry

    lax.fori_loop(0, peers, place, 0, unroll=peers <= 8)

    def far(step, carry):
        for group in [4 * step + g for g in range(4)]:
            left, loads = turn_group(far_rows, group)
            for i, s in enumerate(loads):
                t = far_tile[group * 4 + i]
                add_pair(sums_ref, t, left, s, placed(b_ref[t], i), far_live[group * 4 + i].astype(f32))
        return carry

    lax.fori_loop(0, 2 * peers // 16, far, 0)

    valid = (payload[3] > 0.0).astype(f32)
    num, den = jnp.sum(sums_ref[...], axis=2)
    strain_bar = num / (den + 1.0 - valid)
    kappa = jnp.maximum(strain_bar, history[...])
    damage = 1.0 - (keep_share + (1.0 - keep_share) * jnp.exp(-softening * (kappa - 1.0))) / kappa
    damage_ref[...] = damage
    leaving = pltpu.make_async_copy(damage_ref, damage_out, sems.at[8])
    leaving.start()
    intact = (1.0 - damage) * valid

    folded = corner_load[:, :, 0:128] * intact[None, :, 0:128]
    for half in range(1, points // 128):
        cut = slice(half * 128, (half + 1) * 128)
        folded = folded + corner_load[:, :, cut] * intact[None, :, cut]
    owner = spread_rows(tile_sub[...].reshape(1, tiles))
    subs, corners = corner_map.shape
    map_rows = spread_rows(jnp.concatenate([corner_map[m : m + 1, :] for m in range(subs)], axis=1))
    sums = []
    for m in range(subs):
        chosen = jnp.where((owner == float(m))[None], folded, 0.0)
        sums.append(jnp.sum(jnp.sum(chosen, axis=1), axis=1, keepdims=True))
    sub_part = jnp.broadcast_to(jnp.concatenate(sums, axis=0), (subs * corners, 128))
    target = map_rows.astype(jnp.int32) - lax.broadcasted_iota(jnp.int32, (subs * corners, 128), 1)

    def scatter(j, carry):
        held = jnp.where(j == lax.axis_index("blk"), external[...], 0.0).reshape(1, 128)
        force = jnp.sum(jnp.where(target == j * 128, sub_part, 0.0), axis=0, keepdims=True)
        parts_ref[pl.ds(j, 1), :] = held - force
        return carry

    lax.fori_loop(0, peers, scatter, 0, unroll=peers <= 8)
    leaving.wait()


def per_device(
    coords,
    strain,
    history,
    corner_load,
    tile_count,
    tile_sub,
    local_pairs,
    send_tile,
    remote_pairs,
    remote_count,
    corner_map,
    external,
):
    tiles, points = strain.shape
    halves = points // 128
    peers = lax.axis_size("blk")
    params = pltpu.CompilerParams(vmem_limit_bytes=grant)
    block = 2 * points * points

    payload, outbox = pl.pallas_call(
        functools.partial(pack_kernel, peers),
        out_shape=(
            pltpu.VMEM((5, tiles, points), f32),
            pltpu.VMEM((peers * halves * 8, 128), f32),
        ),
        in_specs=[anywhere] * 7,
        out_specs=(in_vmem, in_vmem),
        scratch_shapes=[pltpu.VMEM((tiles, points), f32)]
        + [pltpu.SMEM(v.shape, jnp.int32) for v in (tile_count, send_tile, remote_pairs, remote_count)]
        + [pltpu.VMEM(local_pairs.shape, jnp.int32), pltpu.SemaphoreType.DMA((7,))],
        compiler_params=params,
        name="pack",
    )(*(in_hbm(v) for v in (coords, strain, tile_count, send_tile, remote_pairs, remote_count, local_pairs)))

    layers = lax.axis_size("sub")
    late, soon = [
        lax.ppermute(payload, "sub", [p for i in range(first, layers - 1, 2) for p in ((i, i + 1), (i + 1, i))])
        for first in (0, 1)
    ]
    inbox = lax.all_to_all(outbox, "blk", split_axis=0, concat_axis=0, tiled=True)

    b_own, sums = pl.pallas_call(
        functools.partial(own_kernel, local_pairs.shape[1]),
        out_shape=(
            jax.ShapeDtypeStruct((tiles, depth, points), bf16),
            jax.ShapeDtypeStruct((2, tiles, 8, points), f32),
        ),
        in_specs=[in_vmem],
        out_specs=(in_vmem,) * 2,
        scratch_shapes=[
            pltpu.VMEM((halves, tiles * pitch, 128), f32),
            pltpu.VMEM((tiles, points, 4 * depth), bf16),
            pltpu.VMEM((tiles, points, 128), f32),
            pltpu.VMEM((tiles, 4 * depth, points), bf16),
            pltpu.SMEM((8, 128), f32),
            pltpu.SemaphoreType.DMA((1,)),
        ],
        compiler_params=params,
        cost_estimate=pl.CostEstimate(
            flops=3 * tiles * block * depth, bytes_accessed=1 << 20, transcendentals=3 * tiles * points * points
        ),
        name="own",
    )(payload)

    damage, parts = pl.pallas_call(
        functools.partial(rest_kernel, peers),
        out_shape=(
            jax.ShapeDtypeStruct((tiles, points), f32),
            jax.ShapeDtypeStruct((peers, 128), f32),
        ),
        in_specs=[in_vmem] * 6 + [anywhere] * 8,
        out_specs=(anywhere, in_vmem),
        scratch_shapes=[pltpu.VMEM(v.shape, v.dtype) for v in (strain, history, corner_load, external, tile_sub, corner_map)]
        + [
            pltpu.VMEM((halves, tiles * pitch, 128), f32),
            pltpu.VMEM((halves, 2 * peers * pitch, 128), f32),
            pltpu.VMEM(sums.shape, f32),
        ]
        + [pltpu.SMEM(v.shape, jnp.int32) for v in (send_tile, remote_pairs, remote_count)]
        + [pltpu.SMEM((2 * peers,), jnp.int32)] * 2
        + [pltpu.SemaphoreType.DMA((9,))],
        compiler_params=params,
        cost_estimate=pl.CostEstimate(
            flops=4 * tiles * block * depth, bytes_accessed=1 << 21, transcendentals=4 * tiles * points * points
        ),
        name="rest",
    )(
        late,
        soon,
        inbox,
        b_own,
        sums,
        payload,
        *(
            in_hbm(v)
            for v in (
                history,
                corner_load,
                external,
                tile_sub,
                corner_map,
                send_tile,
                remote_pairs,
                remote_count,
            )
        ),
    )
    gathered = lax.all_to_all(parts, "blk", split_axis=0, concat_axis=0, tiled=True)
    return damage, jnp.sum(gathered, axis=0)


def solution(mesh):
    placed = (
        P(None, ("sub", "blk"), None),
        P(("sub", "blk"), None),
        P(("sub", "blk"), None),
        P(None, ("sub", "blk"), None),
        P(("sub", "blk")),
        P(("sub", "blk")),
        P(None, ("sub", "blk")),
        P(("sub", "blk")),
        P(None, ("sub", "blk")),
        P(("sub", "blk")),
        P(("sub", "blk"), None),
        P(("sub", "blk")),
    )
    return jax.shard_map(
        per_device,
        mesh=mesh,
        in_specs=placed,
        out_specs=(P(("sub", "blk"), None), P(("sub", "blk"))),
        check_vma=False,
    )
```

```python
import functools
import math

import jax
import jax.numpy as jnp
from jax import lax
from jax.experimental import pallas as pl
from jax.experimental.pallas import tpu as pltpu
from jax.sharding import PartitionSpec as P

gauss_rate = 4.0
keep_share = 0.05
softening = 0.5
coord_scale = math.sqrt(gauss_rate * math.log2(math.e))
far_off = 2048.0
depth = 32
pitch = depth + 1
grant = 24 * 1024 * 1024

f32 = jnp.float32
bf16 = jnp.bfloat16
in_vmem = pl.BlockSpec(memory_space=pltpu.VMEM)
anywhere = pl.BlockSpec(memory_space=pl.ANY)


def in_hbm(value):
    return value if value.size == 1 else pltpu.with_memory_space_constraint(value, pltpu.HBM)


def pieces(value):
    high = value.astype(bf16).astype(f32)
    rest = value - high
    middle = rest.astype(bf16).astype(f32)
    low = (rest - middle).astype(bf16).astype(f32)
    return high, middle, low


def put_rows(rows_ref, base, rows):
    for r, row in enumerate(rows):
        tiles = row.shape[0]
        for half in range(row.shape[1] // 128):
            rows_ref[half, pl.ds(base * pitch + r, tiles, stride=pitch), :] = row[:, half * 128 : (half + 1) * 128]


def point_rows(planes):
    scaled = [p * coord_scale for p in planes[:3]]
    split = [pieces(s) for s in scaled]
    norm = scaled[0] * scaled[0] + scaled[1] * scaled[1] + scaled[2] * scaled[2]
    return split, norm + jnp.where(planes[3] > 0.0, 0.0, far_off)


def put_source(planes, rows_ref, base):
    split, norm = point_rows(planes)
    ones = jnp.ones_like(norm)
    rows = []
    for high, middle, low in split:
        rows += [high, high, middle, high, low, middle]
    rows += list(pieces(-norm)) + [ones, ones, ones] + [planes[3]]
    rows += [jnp.zeros_like(norm)] * (depth - len(rows))
    put_rows(rows_ref, base, rows)


def put_target(planes, rows_ref):
    split, norm = point_rows(planes)
    ones = jnp.ones_like(norm)
    rows = []
    for high, middle, low in split:
        rows += [2.0 * v for v in (high, middle, high, low, high, middle)]
    rows += [ones, ones, ones] + list(pieces(-norm))
    rows += [jnp.zeros_like(norm)] * (depth - len(rows))
    put_rows(rows_ref, 0, rows)


def turn_group(rows_ref, group):
    turned = jnp.concatenate(
        [
            jnp.concatenate([rows_ref[half, pl.ds((group * 4 + j) * pitch, depth), :] for j in range(4)], axis=0).T
            for half in range(rows_ref.shape[0])
        ],
        axis=0,
    )
    lanes = [depth * j + 24 for j in range(4)]
    return turned.astype(bf16), [jnp.broadcast_to(turned[:, n : n + 1], turned.shape) for n in lanes]


def placed(b, j):
    above, below = [jnp.zeros((depth * n, b.shape[1]), bf16) for n in (j, 3 - j)]
    return jnp.concatenate([above] * (j > 0) + [b] + [below] * (j < 3), axis=0)


def fold(x):
    return jnp.sum(x.reshape(x.shape[0] // 8, 8, x.shape[1]), axis=0)


def column_sums(weight, s):
    load = jnp.concatenate([s] * (weight.shape[1] // 128), axis=1)
    return fold(weight * load), fold(weight)


def add_pair(sums_ref, t, a, s, b, live=None):
    weight = jnp.exp2(jnp.dot(a, b, preferred_element_type=f32))
    num, den = column_sums(weight, s)
    if live is not None:
        num, den = num * live, den * live
    sums_ref[0, t] = sums_ref[0, t] + num
    sums_ref[1, t] = sums_ref[1, t] + den


def repeat_target(compact, b_ref):
    def some_tiles(step, carry):
        for t in [step * 4 + i for i in range(4)]:
            block = compact[t]
            for j in range(4):
                b_ref[t, depth * j : depth * (j + 1), :] = block
        return carry

    lax.fori_loop(0, compact.shape[0] // 4, some_tiles, 0)


def fetch(sources, targets, sems):
    copies = [pltpu.make_async_copy(src, dst, sems.at[i]) for i, (src, dst) in enumerate(zip(sources, targets))]
    for copy in copies:
        copy.start()
    return copies


def pack_kernel(
    peers,
    coords,
    strain,
    tile_count_in,
    send_tile_in,
    remote_pairs_in,
    remote_count_in,
    local_pairs_in,
    payload,
    outbox,
    strain_here,
    tile_count,
    send_tile,
    remote_pairs,
    remote_count,
    own_tile,
    own_live,
    blocks,
    local_pairs,
    sems,
):
    tiles, points = strain.shape
    copies = fetch(
        (coords, strain, tile_count_in, send_tile_in, remote_pairs_in, remote_count_in, local_pairs_in),
        (payload.at[0:3], strain_here, tile_count, send_tile, remote_pairs, remote_count, local_pairs),
        sems,
    )
    payload[4] = jnp.zeros((tiles, points), f32)
    for copy in copies:
        copy.wait()
    payload[4, 0:2, 0 : local_pairs.shape[1]] = local_pairs[...].astype(f32)
    lane = lax.broadcasted_iota(jnp.int32, (1, points), 1)
    for t in range(tiles):
        payload[3, t : t + 1, :] = jnp.where(lane < tile_count[t], strain_here[t : t + 1, :], 0.0)

    halves = points // 128
    for k in range(4):
        for half in range(halves):
            rows = payload[k, 0:4, half * 128 : (half + 1) * 128]
            for first in (0, 4):
                blocks[pl.ds(half * 8 + first + k, 4, stride=8 * halves), :] = rows

    def listed(i, carry):
        h = remote_pairs[1, i]
        own_tile[h] = remote_pairs[0, i]
        own_live[h] = (i < remote_count[0]).astype(jnp.int32)
        return carry

    lax.fori_loop(0, peers, listed, 0, unroll=peers <= 8)
    row = lax.broadcasted_iota(jnp.int32, (8, 128), 0)

    def message(h, carry):
        masked = (row == 7) & (own_live[h] == 0)
        for half in range(halves):
            sent, own = [
                blocks[pl.ds(pl.multiple_of((t * halves + half) * 8, 8), 8), :] for t in (send_tile[h], own_tile[h])
            ]
            both = jnp.where(row < 4, sent, jnp.where(masked, 0.0, own))
            outbox[pl.ds(pl.multiple_of((h * halves + half) * 8, 8), 8), :] = both
        return carry

    lax.fori_loop(0, peers, message, 0, unroll=peers <= 8)


def spread_rows(values):
    n = values.shape[1]
    wide = jnp.concatenate([values.astype(f32), jnp.zeros((1, 128 - n), f32)], axis=1)
    return jnp.broadcast_to(wide, (128, 128)).T[0:n]


def own_kernel(pairs, payload, b_out, sums_ref, rows_ref, a_ref, s_ref, b_ref, local_pairs, sems):
    tiles = payload.shape[1]
    copies = fetch((payload.at[4, 0:8, 0:128],), (local_pairs,), sems)
    planes = [payload[k] for k in range(4)]
    put_target(planes, rows_ref)

    def set_target(group, carry):
        for t in [group * 4 + i for i in range(4)]:
            rows = pl.ds(t * pitch, depth)
            for half in range(rows_ref.shape[0]):
                b_out[t, :, half * 128 : (half + 1) * 128] = rows_ref[half, rows, :].astype(bf16)
        return carry

    lax.fori_loop(0, tiles // 4, set_target, 0)
    repeat_target(b_out, b_ref)
    put_source(planes, rows_ref, 0)
    sums_ref[...] = jnp.zeros_like(sums_ref)
    for copy in copies:
        copy.wait()

    column = lax.broadcasted_iota(jnp.int32, (1, 4 * depth), 1) // depth

    def own(step, carry):
        for group in [8 * step + g for g in range(8)]:
            left, loads = turn_group(rows_ref, group)
            for i, s in enumerate(loads):
                t = group * 4 + i
                a = left * (column == i).astype(f32).astype(bf16)
                a_ref[t] = a
                s_ref[t] = s
                add_pair(sums_ref, t, a, s, b_ref[t])
        return carry

    lax.fori_loop(0, tiles // 32, own, 0)

    def listed(step, carry):
        for i in range(32):
            one = local_pairs[0, step * 32 + i].astype(jnp.int32)
            two = local_pairs[1, step * 32 + i].astype(jnp.int32)
            add_pair(sums_ref, two, a_ref[one], s_ref[one], b_ref[two])
            add_pair(sums_ref, one, a_ref[two], s_ref[two], b_ref[one])
        return carry

    lax.fori_loop(0, pairs // 32, listed, 0)


def rest_kernel(
    peers,
    late,
    soon,
    inbox,
    b_ref,
    sums_in,
    payload,
    history_in,
    corner_load_in,
    external_in,
    tile_sub_in,
    corner_map_in,
    send_tile_in,
    remote_pairs_in,
    remote_count_in,
    damage_out,
    parts_ref,
    damage_ref,
    history,
    corner_load,
    external,
    tile_sub,
    corner_map,
    rows_ref,
    far_rows,
    sums_ref,
    send_tile,
    remote_pairs,
    remote_count,
    far_tile,
    far_live,
    sems,
):
    tiles, points = history.shape
    halves = points // 128
    groups = tiles // 4
    count = lax.axis_size("sub")
    layer = lax.axis_index("sub")
    copies = fetch(
        (
            send_tile_in,
            remote_pairs_in,
            remote_count_in,
            history_in,
            corner_load_in,
            external_in,
            tile_sub_in,
            corner_map_in,
        ),
        (send_tile, remote_pairs, remote_count, history, corner_load, external, tile_sub, corner_map),
        sems.at[0:8],
    )

    sums_ref[...] = sums_in[...]

    def border(tiles_in, partner, shift):
        def some(step, carry):
            for group in [8 * step + g for g in range(8)]:
                left, loads = turn_group(rows_ref, group)
                for i, s in enumerate(loads):
                    u = group * 4 + i
                    add_pair(sums_ref, u, left, s, placed(b_ref[u], i))
                    t = lax.rem(u + shift + tiles, tiles)
                    add_pair(sums_ref, t, left, s, placed(b_ref[t], i))
            return carry

        @pl.when((partner >= 0) & (partner < count))
        def both():
            put_source([tiles_in[k] for k in range(4)], rows_ref, 0)
            lax.fori_loop(0, groups // 8, some, 0)

    up = 1 - 2 * lax.rem(layer, 2)
    border(soon, layer - up, -up)
    border(late, layer + up, up)

    for copy in copies:
        copy.wait()
    for which in range(2):
        planes = [
            jnp.concatenate(
                [inbox[pl.ds(half * 8 + 4 * which + k, peers, stride=8 * halves), :] for half in range(halves)], axis=1
            )
            for k in range(4)
        ]
        put_source(planes, far_rows, which * peers)

    def place(i, carry):
        h = remote_pairs[1, i]
        far_tile[h] = remote_pairs[0, i]
        far_live[h] = (i < remote_count[0]).astype(jnp.int32)
        far_tile[peers + i] = send_tile[i]
        far_live[peers + i] = 1
        return carry

    lax.fori_loop(0, peers, place, 0, unroll=peers <= 8)

    def far(step, carry):
        for group in [4 * step + g for g in range(4)]:
            left, loads = turn_group(far_rows, group)
            for i, s in enumerate(loads):
                t = far_tile[group * 4 + i]
                add_pair(sums_ref, t, left, s, placed(b_ref[t], i), far_live[group * 4 + i].astype(f32))
        return carry

    lax.fori_loop(0, 2 * peers // 16, far, 0)

    valid = (payload[3] > 0.0).astype(f32)
    num, den = jnp.sum(sums_ref[...], axis=2)
    strain_bar = num / (den + 1.0 - valid)
    kappa = jnp.maximum(strain_bar, history[...])
    damage = 1.0 - (keep_share + (1.0 - keep_share) * jnp.exp(-softening * (kappa - 1.0))) / kappa
    damage_ref[...] = damage
    leaving = pltpu.make_async_copy(damage_ref, damage_out, sems.at[8])
    leaving.start()
    intact = (1.0 - damage) * valid

    folded = corner_load[:, :, 0:128] * intact[None, :, 0:128]
    for half in range(1, points // 128):
        cut = slice(half * 128, (half + 1) * 128)
        folded = folded + corner_load[:, :, cut] * intact[None, :, cut]
    owner = spread_rows(tile_sub[...].reshape(1, tiles))
    subs, corners = corner_map.shape
    map_rows = spread_rows(jnp.concatenate([corner_map[m : m + 1, :] for m in range(subs)], axis=1))
    sums = []
    for m in range(subs):
        chosen = jnp.where((owner == float(m))[None], folded, 0.0)
        sums.append(jnp.sum(jnp.sum(chosen, axis=1), axis=1, keepdims=True))
    sub_part = jnp.broadcast_to(jnp.concatenate(sums, axis=0), (subs * corners, 128))
    target = map_rows.astype(jnp.int32) - lax.broadcasted_iota(jnp.int32, (subs * corners, 128), 1)

    def scatter(j, carry):
        held = jnp.where(j == lax.axis_index("blk"), external[...], 0.0).reshape(1, 128)
        force = jnp.sum(jnp.where(target == j * 128, sub_part, 0.0), axis=0, keepdims=True)
        parts_ref[pl.ds(j, 1), :] = held - force
        return carry

    lax.fori_loop(0, peers, scatter, 0, unroll=peers <= 8)
    leaving.wait()


def per_device(
    coords,
    strain,
    history,
    corner_load,
    tile_count,
    tile_sub,
    local_pairs,
    send_tile,
    remote_pairs,
    remote_count,
    corner_map,
    external,
):
    tiles, points = strain.shape
    halves = points // 128
    peers = lax.axis_size("blk")
    params = pltpu.CompilerParams(vmem_limit_bytes=grant)
    block = 2 * points * points

    payload, outbox = pl.pallas_call(
        functools.partial(pack_kernel, peers),
        out_shape=(
            pltpu.VMEM((5, tiles, points), f32),
            pltpu.VMEM((peers * halves * 8, 128), f32),
        ),
        in_specs=[anywhere] * 7,
        out_specs=(in_vmem, in_vmem),
        scratch_shapes=[pltpu.VMEM((tiles, points), f32)]
        + [pltpu.SMEM(v.shape, jnp.int32) for v in (tile_count, send_tile, remote_pairs, remote_count)]
        + [pltpu.SMEM((peers,), jnp.int32)] * 2
        + [pltpu.VMEM((4 * halves * 8, 128), f32)]
        + [pltpu.VMEM(local_pairs.shape, jnp.int32), pltpu.SemaphoreType.DMA((7,))],
        compiler_params=params,
        name="pack",
    )(*(in_hbm(v) for v in (coords, strain, tile_count, send_tile, remote_pairs, remote_count, local_pairs)))

    layers = lax.axis_size("sub")
    late, soon = [
        lax.ppermute(payload, "sub", [p for i in range(first, layers - 1, 2) for p in ((i, i + 1), (i + 1, i))])
        for first in (0, 1)
    ]
    inbox = lax.all_to_all(outbox, "blk", split_axis=0, concat_axis=0, tiled=True)

    b_own, sums = pl.pallas_call(
        functools.partial(own_kernel, local_pairs.shape[1]),
        out_shape=(
            jax.ShapeDtypeStruct((tiles, depth, points), bf16),
            jax.ShapeDtypeStruct((2, tiles, 8, points), f32),
        ),
        in_specs=[in_vmem],
        out_specs=(in_vmem,) * 2,
        scratch_shapes=[
            pltpu.VMEM((halves, tiles * pitch, 128), f32),
            pltpu.VMEM((tiles, points, 4 * depth), bf16),
            pltpu.VMEM((tiles, points, 128), f32),
            pltpu.VMEM((tiles, 4 * depth, points), bf16),
            pltpu.SMEM((8, 128), f32),
            pltpu.SemaphoreType.DMA((1,)),
        ],
        compiler_params=params,
        cost_estimate=pl.CostEstimate(
            flops=3 * tiles * block * depth, bytes_accessed=1 << 20, transcendentals=3 * tiles * points * points
        ),
        name="own",
    )(payload)

    damage, parts = pl.pallas_call(
        functools.partial(rest_kernel, peers),
        out_shape=(
            jax.ShapeDtypeStruct((tiles, points), f32),
            jax.ShapeDtypeStruct((peers, 128), f32),
        ),
        in_specs=[in_vmem] * 6 + [anywhere] * 8,
        out_specs=(anywhere, in_vmem),
        scratch_shapes=[pltpu.VMEM(v.shape, v.dtype) for v in (strain, history, corner_load, external, tile_sub, corner_map)]
        + [
            pltpu.VMEM((halves, tiles * pitch, 128), f32),
            pltpu.VMEM((halves, 2 * peers * pitch, 128), f32),
            pltpu.VMEM(sums.shape, f32),
        ]
        + [pltpu.SMEM(v.shape, jnp.int32) for v in (send_tile, remote_pairs, remote_count)]
        + [pltpu.SMEM((2 * peers,), jnp.int32)] * 2
        + [pltpu.SemaphoreType.DMA((9,))],
        compiler_params=params,
        cost_estimate=pl.CostEstimate(
            flops=4 * tiles * block * depth, bytes_accessed=1 << 21, transcendentals=4 * tiles * points * points
        ),
        name="rest",
    )(
        late,
        soon,
        inbox,
        b_own,
        sums,
        payload,
        *(
            in_hbm(v)
            for v in (
                history,
                corner_load,
                external,
                tile_sub,
                corner_map,
                send_tile,
                remote_pairs,
                remote_count,
            )
        ),
    )
    gathered = lax.all_to_all(parts, "blk", split_axis=0, concat_axis=0, tiled=True)
    return damage, jnp.sum(gathered, axis=0)


def solution(mesh):
    placed = (
        P(None, ("sub", "blk"), None),
        P(("sub", "blk"), None),
        P(("sub", "blk"), None),
        P(None, ("sub", "blk"), None),
        P(("sub", "blk")),
        P(("sub", "blk")),
        P(None, ("sub", "blk")),
        P(("sub", "blk")),
        P(None, ("sub", "blk")),
        P(("sub", "blk")),
        P(("sub", "blk"), None),
        P(("sub", "blk")),
    )
    return jax.shard_map(
        per_device,
        mesh=mesh,
        in_specs=placed,
        out_specs=(P(("sub", "blk"), None), P(("sub", "blk"))),
        check_vma=False,
    )
```

```python
import functools
import math

import jax
import jax.numpy as jnp
from jax import lax
from jax.experimental import pallas as pl
from jax.experimental.pallas import tpu as pltpu
from jax.sharding import PartitionSpec as P

gauss_rate = 4.0
keep_share = 0.05
softening = 0.5
coord_scale = math.sqrt(gauss_rate * math.log2(math.e))
far_off = 2048.0
depth = 32
pitch = depth + 1
grant = 24 * 1024 * 1024

f32 = jnp.float32
bf16 = jnp.bfloat16
in_vmem = pl.BlockSpec(memory_space=pltpu.VMEM)
anywhere = pl.BlockSpec(memory_space=pl.ANY)


def in_hbm(value):
    return value if value.size == 1 else pltpu.with_memory_space_constraint(value, pltpu.HBM)


def pieces(value):
    high = value.astype(bf16).astype(f32)
    rest = value - high
    middle = rest.astype(bf16).astype(f32)
    low = (rest - middle).astype(bf16).astype(f32)
    return high, middle, low


def put_rows(rows_ref, base, rows):
    for r, row in enumerate(rows):
        tiles = row.shape[0]
        for half in range(row.shape[1] // 128):
            rows_ref[half, pl.ds(base * pitch + r, tiles, stride=pitch), :] = row[:, half * 128 : (half + 1) * 128]


def point_rows(planes):
    scaled = [p * coord_scale for p in planes[:3]]
    split = [pieces(s) for s in scaled]
    norm = scaled[0] * scaled[0] + scaled[1] * scaled[1] + scaled[2] * scaled[2]
    return split, norm + jnp.where(planes[3] > 0.0, 0.0, far_off)


def put_source(planes, rows_ref, base):
    split, norm = point_rows(planes)
    ones = jnp.ones_like(norm)
    rows = []
    for high, middle, low in split:
        rows += [high, high, middle, high, low, middle]
    rows += list(pieces(-norm)) + [ones, ones, ones] + [planes[3]]
    rows += [jnp.zeros_like(norm)] * (depth - len(rows))
    put_rows(rows_ref, base, rows)


def put_target(planes, rows_ref):
    split, norm = point_rows(planes)
    ones = jnp.ones_like(norm)
    rows = []
    for high, middle, low in split:
        rows += [2.0 * v for v in (high, middle, high, low, high, middle)]
    rows += [ones, ones, ones] + list(pieces(-norm))
    rows += [jnp.zeros_like(norm)] * (depth - len(rows))
    put_rows(rows_ref, 0, rows)


def turn_group(rows_ref, group):
    turned = jnp.concatenate(
        [
            jnp.concatenate([rows_ref[half, pl.ds((group * 4 + j) * pitch, depth), :] for j in range(4)], axis=0).T
            for half in range(rows_ref.shape[0])
        ],
        axis=0,
    )
    lanes = [depth * j + 24 for j in range(4)]
    return turned.astype(bf16), [jnp.broadcast_to(turned[:, n : n + 1], turned.shape) for n in lanes]


def placed(b, j):
    above, below = [jnp.zeros((depth * n, b.shape[1]), bf16) for n in (j, 3 - j)]
    return jnp.concatenate([above] * (j > 0) + [b] + [below] * (j < 3), axis=0)


def fold(x):
    return jnp.sum(x.reshape(x.shape[0] // 8, 8, x.shape[1]), axis=0)


def column_sums(weight, s):
    load = jnp.concatenate([s] * (weight.shape[1] // 128), axis=1)
    return fold(weight * load), fold(weight)


def add_pair(sums_ref, t, a, s, b, live=None):
    weight = jnp.exp2(jnp.dot(a, b, preferred_element_type=f32))
    num, den = column_sums(weight, s)
    if live is not None:
        num, den = num * live, den * live
    sums_ref[0, t] = sums_ref[0, t] + num
    sums_ref[1, t] = sums_ref[1, t] + den


def repeat_target(compact, b_ref):
    def some_tiles(step, carry):
        for t in [step * 4 + i for i in range(4)]:
            block = compact[t]
            for j in range(4):
                b_ref[t, depth * j : depth * (j + 1), :] = block
        return carry

    lax.fori_loop(0, compact.shape[0] // 4, some_tiles, 0)


def fetch(sources, targets, sems):
    copies = [pltpu.make_async_copy(src, dst, sems.at[i]) for i, (src, dst) in enumerate(zip(sources, targets))]
    for copy in copies:
        copy.start()
    return copies


def pack(
    peers,
    coords,
    strain,
    tile_count_in,
    send_tile_in,
    remote_pairs_in,
    remote_count_in,
    local_pairs_in,
    payload,
    outbox,
    strain_here,
    tile_count,
    send_tile,
    remote_pairs,
    remote_count,
    own_tile,
    own_live,
    blocks,
    local_pairs,
    sems,
):
    tiles, points = strain.shape
    copies = fetch(
        (coords, strain, tile_count_in, send_tile_in, remote_pairs_in, remote_count_in, local_pairs_in),
        (payload.at[0:3], strain_here, tile_count, send_tile, remote_pairs, remote_count, local_pairs),
        sems,
    )
    payload[4] = jnp.zeros((tiles, points), f32)
    for copy in copies:
        copy.wait()
    payload[4, 0:2, 0 : local_pairs.shape[1]] = local_pairs[...].astype(f32)
    lane = lax.broadcasted_iota(jnp.int32, (1, points), 1)
    for t in range(tiles):
        payload[3, t : t + 1, :] = jnp.where(lane < tile_count[t], strain_here[t : t + 1, :], 0.0)

    halves = points // 128
    for k in range(4):
        for half in range(halves):
            rows = payload[k, 0:4, half * 128 : (half + 1) * 128]
            for first in (0, 4):
                blocks[pl.ds(half * 8 + first + k, 4, stride=8 * halves), :] = rows

    def listed(i, carry):
        h = remote_pairs[1, i]
        own_tile[h] = remote_pairs[0, i]
        own_live[h] = (i < remote_count[0]).astype(jnp.int32)
        return carry

    lax.fori_loop(0, peers, listed, 0, unroll=peers <= 8)
    row = lax.broadcasted_iota(jnp.int32, (8, 128), 0)

    def message(h, carry):
        masked = (row == 7) & (own_live[h] == 0)
        for half in range(halves):
            sent, own = [
                blocks[pl.ds(pl.multiple_of((t * halves + half) * 8, 8), 8), :] for t in (send_tile[h], own_tile[h])
            ]
            both = jnp.where(row < 4, sent, jnp.where(masked, 0.0, own))
            outbox[pl.ds(pl.multiple_of((h * halves + half) * 8, 8), 8), :] = both
        return carry

    lax.fori_loop(0, peers, message, 0, unroll=peers <= 8)


def my_turn(parity):
    return lax.rem(lax.axis_index("sub"), 2) == parity


def pack_odd_kernel(peers, *refs):
    pl.when(my_turn(1))(lambda: pack(peers, *refs))


def pack_even_kernel(peers, *refs):
    arguments, (payload_in, outbox_in, payload, outbox), scratch = refs[:7], refs[7:11], refs[11:]
    pl.when(my_turn(0))(lambda: pack(peers, *arguments, payload, outbox, *scratch))

    @pl.when(my_turn(1))
    def take():
        payload[...] = payload_in[...]
        outbox[...] = outbox_in[...]


def spread_rows(values):
    n = values.shape[1]
    wide = jnp.concatenate([values.astype(f32), jnp.zeros((1, 128 - n), f32)], axis=1)
    return jnp.broadcast_to(wide, (128, 128)).T[0:n]


def own(pairs, payload, b_out, sums_ref, rows_ref, a_ref, s_ref, b_ref, local_pairs, sems):
    tiles = payload.shape[1]
    copies = fetch((payload.at[4, 0:8, 0:128],), (local_pairs,), sems)
    planes = [payload[k] for k in range(4)]
    put_target(planes, rows_ref)

    def set_target(group, carry):
        for t in [group * 4 + i for i in range(4)]:
            rows = pl.ds(t * pitch, depth)
            for half in range(rows_ref.shape[0]):
                b_out[t, :, half * 128 : (half + 1) * 128] = rows_ref[half, rows, :].astype(bf16)
        return carry

    lax.fori_loop(0, tiles // 4, set_target, 0)
    repeat_target(b_out, b_ref)
    put_source(planes, rows_ref, 0)
    sums_ref[...] = jnp.zeros_like(sums_ref)
    for copy in copies:
        copy.wait()

    column = lax.broadcasted_iota(jnp.int32, (1, 4 * depth), 1) // depth

    def alone(step, carry):
        for group in [8 * step + g for g in range(8)]:
            left, loads = turn_group(rows_ref, group)
            for i, s in enumerate(loads):
                t = group * 4 + i
                a = left * (column == i).astype(f32).astype(bf16)
                a_ref[t] = a
                s_ref[t] = s
                add_pair(sums_ref, t, a, s, b_ref[t])
        return carry

    lax.fori_loop(0, tiles // 32, alone, 0)

    def listed(step, carry):
        for i in range(32):
            one = local_pairs[0, step * 32 + i].astype(jnp.int32)
            two = local_pairs[1, step * 32 + i].astype(jnp.int32)
            add_pair(sums_ref, two, a_ref[one], s_ref[one], b_ref[two])
            add_pair(sums_ref, one, a_ref[two], s_ref[two], b_ref[one])
        return carry

    lax.fori_loop(0, pairs // 32, listed, 0)


def own_even_kernel(pairs, payload, outbox, payload_out, outbox_out, b_out, sums_ref, *scratch):
    payload_out[...] = payload[...]
    outbox_out[...] = outbox[...]
    pl.when(my_turn(0))(lambda: own(pairs, payload, b_out, sums_ref, *scratch))


def own_odd_kernel(pairs, payload, b_in, sums_in, odd_up, odd_down, b_out, sums_ref, *scratch):
    pl.when(my_turn(1))(lambda: own(pairs, payload, b_out, sums_ref, *scratch))

    @pl.when(my_turn(0))
    def take():
        b_out[...] = b_in[...]
        sums_ref[...] = sums_in[...]


def rest_kernel(
    peers,
    odd_up,
    odd_down,
    even_up,
    even_down,
    inbox,
    b_ref,
    sums_in,
    payload,
    history_in,
    corner_load_in,
    external_in,
    tile_sub_in,
    corner_map_in,
    send_tile_in,
    remote_pairs_in,
    remote_count_in,
    damage_out,
    parts_ref,
    damage_ref,
    history,
    corner_load,
    external,
    tile_sub,
    corner_map,
    rows_ref,
    far_rows,
    sums_ref,
    send_tile,
    remote_pairs,
    remote_count,
    far_tile,
    far_live,
    sems,
):
    tiles, points = history.shape
    halves = points // 128
    groups = tiles // 4
    count = lax.axis_size("sub")
    layer = lax.axis_index("sub")
    copies = fetch(
        (
            send_tile_in,
            remote_pairs_in,
            remote_count_in,
            history_in,
            corner_load_in,
            external_in,
            tile_sub_in,
            corner_map_in,
        ),
        (send_tile, remote_pairs, remote_count, history, corner_load, external, tile_sub, corner_map),
        sems.at[0:8],
    )

    sums_ref[...] = sums_in[...]

    def border(from_odd, from_even, partner, shift):
        def some(step, carry):
            for group in [8 * step + g for g in range(8)]:
                left, loads = turn_group(rows_ref, group)
                for i, s in enumerate(loads):
                    u = group * 4 + i
                    add_pair(sums_ref, u, left, s, placed(b_ref[u], i))
                    t = lax.rem(u + shift + tiles, tiles)
                    add_pair(sums_ref, t, left, s, placed(b_ref[t], i))
            return carry

        @pl.when((partner >= 0) & (partner < count))
        def both():
            put_source([jnp.where(my_turn(0), from_odd[k], from_even[k]) for k in range(4)], rows_ref, 0)
            lax.fori_loop(0, groups // 8, some, 0)

    border(odd_up, even_up, layer - 1, -1)
    border(odd_down, even_down, layer + 1, 1)

    for copy in copies:
        copy.wait()
    for which in range(2):
        planes = [
            jnp.concatenate(
                [inbox[pl.ds(half * 8 + 4 * which + k, peers, stride=8 * halves), :] for half in range(halves)], axis=1
            )
            for k in range(4)
        ]
        put_source(planes, far_rows, which * peers)

    def place(i, carry):
        h = remote_pairs[1, i]
        far_tile[h] = remote_pairs[0, i]
        far_live[h] = (i < remote_count[0]).astype(jnp.int32)
        far_tile[peers + i] = send_tile[i]
        far_live[peers + i] = 1
        return carry

    lax.fori_loop(0, peers, place, 0, unroll=peers <= 8)

    def far(step, carry):
        for group in [4 * step + g for g in range(4)]:
            left, loads = turn_group(far_rows, group)
            for i, s in enumerate(loads):
                t = far_tile[group * 4 + i]
                add_pair(sums_ref, t, left, s, placed(b_ref[t], i), far_live[group * 4 + i].astype(f32))
        return carry

    lax.fori_loop(0, 2 * peers // 16, far, 0)

    valid = (payload[3] > 0.0).astype(f32)
    num, den = jnp.sum(sums_ref[...], axis=2)
    strain_bar = num / (den + 1.0 - valid)
    kappa = jnp.maximum(strain_bar, history[...])
    damage = 1.0 - (keep_share + (1.0 - keep_share) * jnp.exp(-softening * (kappa - 1.0))) / kappa
    damage_ref[...] = damage
    leaving = pltpu.make_async_copy(damage_ref, damage_out, sems.at[8])
    leaving.start()
    intact = (1.0 - damage) * valid

    folded = corner_load[:, :, 0:128] * intact[None, :, 0:128]
    for half in range(1, points // 128):
        cut = slice(half * 128, (half + 1) * 128)
        folded = folded + corner_load[:, :, cut] * intact[None, :, cut]
    owner = spread_rows(tile_sub[...].reshape(1, tiles))
    subs, corners = corner_map.shape
    map_rows = spread_rows(jnp.concatenate([corner_map[m : m + 1, :] for m in range(subs)], axis=1))
    sums = []
    for m in range(subs):
        chosen = jnp.where((owner == float(m))[None], folded, 0.0)
        sums.append(jnp.sum(jnp.sum(chosen, axis=1), axis=1, keepdims=True))
    sub_part = jnp.broadcast_to(jnp.concatenate(sums, axis=0), (subs * corners, 128))
    target = map_rows.astype(jnp.int32) - lax.broadcasted_iota(jnp.int32, (subs * corners, 128), 1)

    def scatter(j, carry):
        held = jnp.where(j == lax.axis_index("blk"), external[...], 0.0).reshape(1, 128)
        force = jnp.sum(jnp.where(target == j * 128, sub_part, 0.0), axis=0, keepdims=True)
        parts_ref[pl.ds(j, 1), :] = held - force
        return carry

    lax.fori_loop(0, peers, scatter, 0, unroll=peers <= 8)
    leaving.wait()


def per_device(
    coords,
    strain,
    history,
    corner_load,
    tile_count,
    tile_sub,
    local_pairs,
    send_tile,
    remote_pairs,
    remote_count,
    corner_map,
    external,
):
    tiles, points = strain.shape
    halves = points // 128
    peers = lax.axis_size("blk")
    params = pltpu.CompilerParams(vmem_limit_bytes=grant)
    block = 2 * points * points

    arguments = [in_hbm(v) for v in (coords, strain, tile_count, send_tile, remote_pairs, remote_count, local_pairs)]
    messages = (pltpu.VMEM((5, tiles, points), f32), pltpu.VMEM((peers * halves * 8, 128), f32))
    pack_scratch = (
        [pltpu.VMEM((tiles, points), f32)]
        + [pltpu.SMEM(v.shape, jnp.int32) for v in (tile_count, send_tile, remote_pairs, remote_count)]
        + [pltpu.SMEM((peers,), jnp.int32)] * 2
        + [pltpu.VMEM((4 * halves * 8, 128), f32)]
        + [pltpu.VMEM(local_pairs.shape, jnp.int32), pltpu.SemaphoreType.DMA((7,))]
    )
    payload, outbox = pl.pallas_call(
        functools.partial(pack_odd_kernel, peers),
        out_shape=messages,
        in_specs=[anywhere] * 7,
        out_specs=(in_vmem, in_vmem),
        scratch_shapes=pack_scratch,
        compiler_params=params,
        name="pack_odd",
    )(*arguments)

    def send(tile_data, parity, step):
        layers = lax.axis_size("sub")
        return lax.ppermute(
            tile_data, "sub", [(i, i + step) for i in range(parity, layers, 2) if 0 <= i + step < layers]
        )

    odd_up, odd_down = send(payload, 1, 1), send(payload, 1, -1)

    payload, outbox = pl.pallas_call(
        functools.partial(pack_even_kernel, peers),
        out_shape=messages,
        in_specs=[anywhere] * 7 + [in_vmem] * 2,
        out_specs=(in_vmem, in_vmem),
        scratch_shapes=pack_scratch,
        compiler_params=params,
        cost_estimate=pl.CostEstimate(flops=1 << 36, bytes_accessed=1 << 20, transcendentals=0),
        name="pack_even",
    )(*arguments, payload, outbox)

    own_results = (
        jax.ShapeDtypeStruct((tiles, depth, points), bf16),
        jax.ShapeDtypeStruct((2, tiles, 8, points), f32),
    )
    own_scratch = [
        pltpu.VMEM((halves, tiles * pitch, 128), f32),
        pltpu.VMEM((tiles, points, 4 * depth), bf16),
        pltpu.VMEM((tiles, points, 128), f32),
        pltpu.VMEM((tiles, 4 * depth, points), bf16),
        pltpu.SMEM((8, 128), f32),
        pltpu.SemaphoreType.DMA((1,)),
    ]
    own_cost = pl.CostEstimate(flops=0, bytes_accessed=1 << 16, transcendentals=0)
    payload, outbox, b_own, sums = pl.pallas_call(
        functools.partial(own_even_kernel, local_pairs.shape[1]),
        out_shape=messages + own_results,
        in_specs=[in_vmem] * 2,
        out_specs=(in_vmem,) * 4,
        scratch_shapes=own_scratch,
        compiler_params=params,
        cost_estimate=own_cost,
        name="own_even",
    )(payload, outbox)

    even_up, even_down = send(payload, 0, 1), send(payload, 0, -1)
    inbox = lax.all_to_all(outbox, "blk", split_axis=0, concat_axis=0, tiled=True)

    b_own, sums = pl.pallas_call(
        functools.partial(own_odd_kernel, local_pairs.shape[1]),
        out_shape=own_results,
        in_specs=[in_vmem] * 3 + [anywhere] * 2,
        out_specs=(in_vmem,) * 2,
        scratch_shapes=own_scratch,
        compiler_params=params,
        cost_estimate=own_cost,
        name="own_odd",
    )(payload, b_own, sums, odd_up, odd_down)

    damage, parts = pl.pallas_call(
        functools.partial(rest_kernel, peers),
        out_shape=(
            jax.ShapeDtypeStruct((tiles, points), f32),
            jax.ShapeDtypeStruct((peers, 128), f32),
        ),
        in_specs=[in_vmem] * 8 + [anywhere] * 8,
        out_specs=(anywhere, in_vmem),
        scratch_shapes=[pltpu.VMEM(v.shape, v.dtype) for v in (strain, history, corner_load, external, tile_sub, corner_map)]
        + [
            pltpu.VMEM((halves, tiles * pitch, 128), f32),
            pltpu.VMEM((halves, 2 * peers * pitch, 128), f32),
            pltpu.VMEM(sums.shape, f32),
        ]
        + [pltpu.SMEM(v.shape, jnp.int32) for v in (send_tile, remote_pairs, remote_count)]
        + [pltpu.SMEM((2 * peers,), jnp.int32)] * 2
        + [pltpu.SemaphoreType.DMA((9,))],
        compiler_params=params,
        cost_estimate=pl.CostEstimate(
            flops=4 * tiles * block * depth, bytes_accessed=1 << 21, transcendentals=4 * tiles * points * points
        ),
        name="rest",
    )(
        odd_up,
        odd_down,
        even_up,
        even_down,
        inbox,
        b_own,
        sums,
        payload,
        *(
            in_hbm(v)
            for v in (
                history,
                corner_load,
                external,
                tile_sub,
                corner_map,
                send_tile,
                remote_pairs,
                remote_count,
            )
        ),
    )
    gathered = lax.all_to_all(parts, "blk", split_axis=0, concat_axis=0, tiled=True)
    return damage, jnp.sum(gathered, axis=0)


def solution(mesh):
    placed = (
        P(None, ("sub", "blk"), None),
        P(("sub", "blk"), None),
        P(("sub", "blk"), None),
        P(None, ("sub", "blk"), None),
        P(("sub", "blk")),
        P(("sub", "blk")),
        P(None, ("sub", "blk")),
        P(("sub", "blk")),
        P(None, ("sub", "blk")),
        P(("sub", "blk")),
        P(("sub", "blk"), None),
        P(("sub", "blk")),
    )
    return jax.shard_map(
        per_device,
        mesh=mesh,
        in_specs=placed,
        out_specs=(P(("sub", "blk"), None), P(("sub", "blk"))),
        check_vma=False,
    )
```

```python
import functools
import math

import jax
import jax.numpy as jnp
from jax import lax
from jax.experimental import pallas as pl
from jax.experimental.pallas import tpu as pltpu
from jax.sharding import PartitionSpec as P

gauss_rate = 4.0
keep_share = 0.05
softening = 0.5
coord_scale = math.sqrt(gauss_rate * math.log2(math.e))
far_off = 2048.0
depth = 32
pitch = depth + 1
grant = 24 * 1024 * 1024

f32 = jnp.float32
bf16 = jnp.bfloat16
in_vmem = pl.BlockSpec(memory_space=pltpu.VMEM)
anywhere = pl.BlockSpec(memory_space=pl.ANY)


def in_hbm(value):
    return value if value.size == 1 else pltpu.with_memory_space_constraint(value, pltpu.HBM)


def pieces(value):
    high = value.astype(bf16).astype(f32)
    rest = value - high
    middle = rest.astype(bf16).astype(f32)
    low = (rest - middle).astype(bf16).astype(f32)
    return high, middle, low


def put_rows(rows_ref, base, rows):
    for r, row in enumerate(rows):
        tiles = row.shape[0]
        for half in range(row.shape[1] // 128):
            rows_ref[half, pl.ds(base * pitch + r, tiles, stride=pitch), :] = row[:, half * 128 : (half + 1) * 128]


def point_rows(planes):
    scaled = [p * coord_scale for p in planes[:3]]
    split = [pieces(s) for s in scaled]
    norm = scaled[0] * scaled[0] + scaled[1] * scaled[1] + scaled[2] * scaled[2]
    return split, norm + jnp.where(planes[3] > 0.0, 0.0, far_off)


def put_source(planes, rows_ref, base):
    split, norm = point_rows(planes)
    ones = jnp.ones_like(norm)
    rows = []
    for high, middle, low in split:
        rows += [high, high, middle, high, low, middle]
    rows += list(pieces(-norm)) + [ones, ones, ones] + [planes[3]]
    rows += [jnp.zeros_like(norm)] * (depth - len(rows))
    put_rows(rows_ref, base, rows)


def put_target(planes, rows_ref):
    split, norm = point_rows(planes)
    ones = jnp.ones_like(norm)
    rows = []
    for high, middle, low in split:
        rows += [2.0 * v for v in (high, middle, high, low, high, middle)]
    rows += [ones, ones, ones] + list(pieces(-norm))
    rows += [jnp.zeros_like(norm)] * (depth - len(rows))
    put_rows(rows_ref, 0, rows)


def steps(count, body):
    if count == 1:
        body(0, 0)
    else:
        lax.fori_loop(0, count, body, 0)


def turn_group(rows_ref, group):
    turned = jnp.concatenate(
        [
            jnp.concatenate([rows_ref[half, pl.ds((group * 4 + j) * pitch, depth), :] for j in range(4)], axis=0).T
            for half in range(rows_ref.shape[0])
        ],
        axis=0,
    )
    lanes = [depth * j + 24 for j in range(4)]
    return turned.astype(bf16), [jnp.broadcast_to(turned[:, n : n + 1], turned.shape) for n in lanes]


def placed(b, j):
    above, below = [jnp.zeros((depth * n, b.shape[1]), bf16) for n in (j, 3 - j)]
    return jnp.concatenate([above] * (j > 0) + [b] + [below] * (j < 3), axis=0)


def fold(x):
    return jnp.sum(x.reshape(x.shape[0] // 8, 8, x.shape[1]), axis=0)


def column_sums(weight, s):
    load = jnp.concatenate([s] * (weight.shape[1] // 128), axis=1)
    return fold(weight * load), fold(weight)


def add_pair(sums_ref, t, a, s, b, live=None):
    weight = jnp.exp2(jnp.dot(a, b, preferred_element_type=f32))
    num, den = column_sums(weight, s)
    if live is not None:
        num, den = num * live, den * live
    sums_ref[0, t] = sums_ref[0, t] + num
    sums_ref[1, t] = sums_ref[1, t] + den


def fetch(sources, targets, sems):
    copies = [pltpu.make_async_copy(src, dst, sems.at[i]) for i, (src, dst) in enumerate(zip(sources, targets))]
    for copy in copies:
        copy.start()
    return copies


def pack_kernel(
    peers,
    coords,
    strain,
    tile_count_in,
    send_tile_in,
    remote_pairs_in,
    remote_count_in,
    local_pairs_in,
    payload,
    outbox,
    strain_here,
    tile_count,
    send_tile,
    remote_pairs,
    remote_count,
    own_tile,
    own_live,
    blocks,
    local_pairs,
    sems,
):
    tiles, points = strain.shape
    copies = fetch(
        (coords, strain, tile_count_in, send_tile_in, remote_pairs_in, remote_count_in, local_pairs_in),
        (payload.at[0:3], strain_here, tile_count, send_tile, remote_pairs, remote_count, local_pairs),
        sems,
    )
    payload[4] = jnp.zeros((tiles, points), f32)
    for copy in copies:
        copy.wait()
    payload[4, 0:2, 0 : local_pairs.shape[1]] = local_pairs[...].astype(f32)
    lane = lax.broadcasted_iota(jnp.int32, (1, points), 1)
    for t in range(tiles):
        payload[3, t : t + 1, :] = jnp.where(lane < tile_count[t], strain_here[t : t + 1, :], 0.0)

    halves = points // 128
    for k in range(4):
        for half in range(halves):
            rows = payload[k, 0:4, half * 128 : (half + 1) * 128]
            for first in (0, 4):
                blocks[pl.ds(half * 8 + first + k, 4, stride=8 * halves), :] = rows

    def listed(i, carry):
        h = remote_pairs[1, i]
        own_tile[h] = remote_pairs[0, i]
        own_live[h] = (i < remote_count[0]).astype(jnp.int32)
        return carry

    lax.fori_loop(0, peers, listed, 0, unroll=peers <= 8)
    row = lax.broadcasted_iota(jnp.int32, (8, 128), 0)

    def message(h, carry):
        masked = (row == 7) & (own_live[h] == 0)
        for half in range(halves):
            sent, own = [
                blocks[pl.ds(pl.multiple_of((t * halves + half) * 8, 8), 8), :] for t in (send_tile[h], own_tile[h])
            ]
            both = jnp.where(row < 4, sent, jnp.where(masked, 0.0, own))
            outbox[pl.ds(pl.multiple_of((h * halves + half) * 8, 8), 8), :] = both
        return carry

    lax.fori_loop(0, peers, message, 0, unroll=peers <= 8)


def spread_rows(values):
    n = values.shape[1]
    wide = jnp.concatenate([values.astype(f32), jnp.zeros((1, 128 - n), f32)], axis=1)
    return jnp.broadcast_to(wide, (128, 128)).T[0:n]


def own_kernel(pairs, payload, b_out, sums_ref, rows_ref, a_ref, s_ref, b_ref, local_pairs, sems):
    tiles = payload.shape[1]
    copies = fetch((payload.at[4, 0:8, 0:128],), (local_pairs,), sems)
    planes = [payload[k] for k in range(4)]
    put_target(planes, rows_ref)

    for t in range(tiles):
        rows = slice(t * pitch, t * pitch + depth)
        for half in range(rows_ref.shape[0]):
            cut = slice(half * 128, (half + 1) * 128)
            block = rows_ref[half, rows, :].astype(bf16)
            b_out[t, :, cut] = block
            for j in range(4):
                b_ref[t, depth * j : depth * (j + 1), cut] = block
    put_source(planes, rows_ref, 0)
    sums_ref[...] = jnp.zeros_like(sums_ref)
    for copy in copies:
        copy.wait()

    column = lax.broadcasted_iota(jnp.int32, (1, 4 * depth), 1) // depth

    def own(step, carry):
        for group in [8 * step + g for g in range(8)]:
            left, loads = turn_group(rows_ref, group)
            for i, s in enumerate(loads):
                t = group * 4 + i
                a = left * (column == i).astype(f32).astype(bf16)
                a_ref[t] = a
                s_ref[t] = s
                add_pair(sums_ref, t, a, s, b_ref[t])
        return carry

    steps(tiles // 32, own)

    def listed(step, carry):
        for i in range(32):
            one = local_pairs[0, step * 32 + i].astype(jnp.int32)
            two = local_pairs[1, step * 32 + i].astype(jnp.int32)
            add_pair(sums_ref, two, a_ref[one], s_ref[one], b_ref[two])
            add_pair(sums_ref, one, a_ref[two], s_ref[two], b_ref[one])
        return carry

    steps(pairs // 32, listed)


def rest_kernel(
    peers,
    late,
    soon,
    inbox,
    b_ref,
    sums_in,
    payload,
    history_in,
    corner_load_in,
    external_in,
    tile_sub_in,
    corner_map_in,
    send_tile_in,
    remote_pairs_in,
    remote_count_in,
    damage_out,
    parts_ref,
    damage_ref,
    history,
    corner_load,
    external,
    tile_sub,
    corner_map,
    rows_ref,
    far_rows,
    sums_ref,
    send_tile,
    remote_pairs,
    remote_count,
    far_tile,
    far_live,
    sems,
):
    tiles, points = history.shape
    halves = points // 128
    groups = tiles // 4
    count = lax.axis_size("sub")
    layer = lax.axis_index("sub")
    copies = fetch(
        (
            send_tile_in,
            remote_pairs_in,
            remote_count_in,
            history_in,
            corner_load_in,
            external_in,
            tile_sub_in,
            corner_map_in,
        ),
        (send_tile, remote_pairs, remote_count, history, corner_load, external, tile_sub, corner_map),
        sems.at[0:8],
    )

    sums_ref[...] = sums_in[...]

    def border(tiles_in, partner, shift):
        def some(step, carry):
            for group in [8 * step + g for g in range(8)]:
                left, loads = turn_group(rows_ref, group)
                for i, s in enumerate(loads):
                    u = group * 4 + i
                    add_pair(sums_ref, u, left, s, placed(b_ref[u], i))
                    t = lax.rem(u + shift + tiles, tiles)
                    add_pair(sums_ref, t, left, s, placed(b_ref[t], i))
            return carry

        @pl.when((partner >= 0) & (partner < count))
        def both():
            put_source([tiles_in[k] for k in range(4)], rows_ref, 0)
            steps(groups // 8, some)

    up = 1 - 2 * lax.rem(layer, 2)
    border(soon, layer - up, -up)
    border(late, layer + up, up)

    for copy in copies:
        copy.wait()
    for which in range(2):
        planes = [
            jnp.concatenate(
                [inbox[pl.ds(half * 8 + 4 * which + k, peers, stride=8 * halves), :] for half in range(halves)], axis=1
            )
            for k in range(4)
        ]
        put_source(planes, far_rows, which * peers)

    def place(i, carry):
        h = remote_pairs[1, i]
        far_tile[h] = remote_pairs[0, i]
        far_live[h] = (i < remote_count[0]).astype(jnp.int32)
        far_tile[peers + i] = send_tile[i]
        far_live[peers + i] = 1
        return carry

    lax.fori_loop(0, peers, place, 0, unroll=peers <= 8)

    def far(step, carry):
        for group in [4 * step + g for g in range(4)]:
            left, loads = turn_group(far_rows, group)
            for i, s in enumerate(loads):
                t = far_tile[group * 4 + i]
                add_pair(sums_ref, t, left, s, placed(b_ref[t], i), far_live[group * 4 + i].astype(f32))
        return carry

    steps(2 * peers // 16, far)

    valid = (payload[3] > 0.0).astype(f32)
    num, den = jnp.sum(sums_ref[...], axis=2)
    strain_bar = num / (den + 1.0 - valid)
    kappa = jnp.maximum(strain_bar, history[...])
    damage = 1.0 - (keep_share + (1.0 - keep_share) * jnp.exp(-softening * (kappa - 1.0))) / kappa
    damage_ref[...] = damage
    leaving = pltpu.make_async_copy(damage_ref, damage_out, sems.at[8])
    leaving.start()
    intact = (1.0 - damage) * valid

    folded = corner_load[:, :, 0:128] * intact[None, :, 0:128]
    for half in range(1, points // 128):
        cut = slice(half * 128, (half + 1) * 128)
        folded = folded + corner_load[:, :, cut] * intact[None, :, cut]
    owner = spread_rows(tile_sub[...].reshape(1, tiles))
    subs, corners = corner_map.shape
    map_rows = spread_rows(jnp.concatenate([corner_map[m : m + 1, :] for m in range(subs)], axis=1))
    sums = []
    for m in range(subs):
        chosen = jnp.where((owner == float(m))[None], folded, 0.0)
        sums.append(jnp.sum(jnp.sum(chosen, axis=1), axis=1, keepdims=True))
    sub_part = jnp.broadcast_to(jnp.concatenate(sums, axis=0), (subs * corners, 128))
    target = map_rows.astype(jnp.int32) - lax.broadcasted_iota(jnp.int32, (subs * corners, 128), 1)

    def scatter(j, carry):
        held = jnp.where(j == lax.axis_index("blk"), external[...], 0.0).reshape(1, 128)
        force = jnp.sum(jnp.where(target == j * 128, sub_part, 0.0), axis=0, keepdims=True)
        parts_ref[pl.ds(j, 1), :] = held - force
        return carry

    lax.fori_loop(0, peers, scatter, 0, unroll=peers <= 8)
    leaving.wait()


def per_device(
    coords,
    strain,
    history,
    corner_load,
    tile_count,
    tile_sub,
    local_pairs,
    send_tile,
    remote_pairs,
    remote_count,
    corner_map,
    external,
):
    tiles, points = strain.shape
    halves = points // 128
    peers = lax.axis_size("blk")
    params = pltpu.CompilerParams(vmem_limit_bytes=grant)
    block = 2 * points * points

    payload, outbox = pl.pallas_call(
        functools.partial(pack_kernel, peers),
        out_shape=(
            pltpu.VMEM((5, tiles, points), f32),
            pltpu.VMEM((peers * halves * 8, 128), f32),
        ),
        in_specs=[anywhere] * 7,
        out_specs=(in_vmem, in_vmem),
        scratch_shapes=[pltpu.VMEM((tiles, points), f32)]
        + [pltpu.SMEM(v.shape, jnp.int32) for v in (tile_count, send_tile, remote_pairs, remote_count)]
        + [pltpu.SMEM((peers,), jnp.int32)] * 2
        + [pltpu.VMEM((4 * halves * 8, 128), f32)]
        + [pltpu.VMEM(local_pairs.shape, jnp.int32), pltpu.SemaphoreType.DMA((7,))],
        compiler_params=params,
        name="pack",
    )(*(in_hbm(v) for v in (coords, strain, tile_count, send_tile, remote_pairs, remote_count, local_pairs)))

    layers = lax.axis_size("sub")
    late, soon = [
        lax.ppermute(payload, "sub", [p for i in range(first, layers - 1, 2) for p in ((i, i + 1), (i + 1, i))])
        for first in (0, 1)
    ]
    inbox = lax.all_to_all(outbox, "blk", split_axis=0, concat_axis=0, tiled=True)

    b_own, sums = pl.pallas_call(
        functools.partial(own_kernel, local_pairs.shape[1]),
        out_shape=(
            jax.ShapeDtypeStruct((tiles, depth, points), bf16),
            jax.ShapeDtypeStruct((2, tiles, 8, points), f32),
        ),
        in_specs=[in_vmem],
        out_specs=(in_vmem,) * 2,
        scratch_shapes=[
            pltpu.VMEM((halves, tiles * pitch, 128), f32),
            pltpu.VMEM((tiles, points, 4 * depth), bf16),
            pltpu.VMEM((tiles, points, 128), f32),
            pltpu.VMEM((tiles, 4 * depth, points), bf16),
            pltpu.SMEM((8, 128), f32),
            pltpu.SemaphoreType.DMA((1,)),
        ],
        compiler_params=params,
        cost_estimate=pl.CostEstimate(
            flops=3 * tiles * block * depth, bytes_accessed=1 << 20, transcendentals=3 * tiles * points * points
        ),
        name="own",
    )(payload)

    damage, parts = pl.pallas_call(
        functools.partial(rest_kernel, peers),
        out_shape=(
            jax.ShapeDtypeStruct((tiles, points), f32),
            jax.ShapeDtypeStruct((peers, 128), f32),
        ),
        in_specs=[in_vmem] * 6 + [anywhere] * 8,
        out_specs=(anywhere, in_vmem),
        scratch_shapes=[pltpu.VMEM(v.shape, v.dtype) for v in (strain, history, corner_load, external, tile_sub, corner_map)]
        + [
            pltpu.VMEM((halves, tiles * pitch, 128), f32),
            pltpu.VMEM((halves, 2 * peers * pitch, 128), f32),
            pltpu.VMEM(sums.shape, f32),
        ]
        + [pltpu.SMEM(v.shape, jnp.int32) for v in (send_tile, remote_pairs, remote_count)]
        + [pltpu.SMEM((2 * peers,), jnp.int32)] * 2
        + [pltpu.SemaphoreType.DMA((9,))],
        compiler_params=params,
        cost_estimate=pl.CostEstimate(
            flops=4 * tiles * block * depth, bytes_accessed=1 << 21, transcendentals=4 * tiles * points * points
        ),
        name="rest",
    )(
        late,
        soon,
        inbox,
        b_own,
        sums,
        payload,
        *(
            in_hbm(v)
            for v in (
                history,
                corner_load,
                external,
                tile_sub,
                corner_map,
                send_tile,
                remote_pairs,
                remote_count,
            )
        ),
    )
    gathered = lax.all_to_all(parts, "blk", split_axis=0, concat_axis=0, tiled=True)
    return damage, jnp.sum(gathered, axis=0)


def solution(mesh):
    placed = (
        P(None, ("sub", "blk"), None),
        P(("sub", "blk"), None),
        P(("sub", "blk"), None),
        P(None, ("sub", "blk"), None),
        P(("sub", "blk")),
        P(("sub", "blk")),
        P(None, ("sub", "blk")),
        P(("sub", "blk")),
        P(None, ("sub", "blk")),
        P(("sub", "blk")),
        P(("sub", "blk"), None),
        P(("sub", "blk")),
    )
    return jax.shard_map(
        per_device,
        mesh=mesh,
        in_specs=placed,
        out_specs=(P(("sub", "blk"), None), P(("sub", "blk"))),
        check_vma=False,
    )
```

```python
import functools
import math

import jax
import jax.numpy as jnp
from jax import lax
from jax.experimental import pallas as pl
from jax.experimental.pallas import tpu as pltpu
from jax.sharding import PartitionSpec as P

gauss_rate = 4.0
keep_share = 0.05
softening = 0.5
coord_scale = math.sqrt(gauss_rate * math.log2(math.e))
far_off = 2048.0
depth = 32
pitch = depth + 1
grant = 24 * 1024 * 1024

f32 = jnp.float32
bf16 = jnp.bfloat16
in_vmem = pl.BlockSpec(memory_space=pltpu.VMEM)
anywhere = pl.BlockSpec(memory_space=pl.ANY)


def in_hbm(value):
    return value if value.size == 1 else pltpu.with_memory_space_constraint(value, pltpu.HBM)


def pieces(value):
    high = value.astype(bf16).astype(f32)
    rest = value - high
    middle = rest.astype(bf16).astype(f32)
    low = (rest - middle).astype(bf16).astype(f32)
    return high, middle, low


def put_rows(rows_ref, base, rows):
    for r, row in enumerate(rows):
        tiles = row.shape[0]
        for half in range(row.shape[1] // 128):
            rows_ref[half, pl.ds(base * pitch + r, tiles, stride=pitch), :] = row[:, half * 128 : (half + 1) * 128]


def point_rows(planes):
    scaled = [p * coord_scale for p in planes[:3]]
    split = [pieces(s) for s in scaled]
    norm = scaled[0] * scaled[0] + scaled[1] * scaled[1] + scaled[2] * scaled[2]
    return split, norm + jnp.where(planes[3] > 0.0, 0.0, far_off)


def put_source(planes, rows_ref, base):
    split, norm = point_rows(planes)
    ones = jnp.ones_like(norm)
    rows = []
    for high, middle, low in split:
        rows += [high, high, middle, high, low, middle]
    rows += list(pieces(-norm)) + [ones, ones, ones] + [planes[3]]
    rows += [jnp.zeros_like(norm)] * (depth - len(rows))
    put_rows(rows_ref, base, rows)


def put_target(planes, rows_ref):
    split, norm = point_rows(planes)
    ones = jnp.ones_like(norm)
    rows = []
    for high, middle, low in split:
        rows += [2.0 * v for v in (high, middle, high, low, high, middle)]
    rows += [ones, ones, ones] + list(pieces(-norm))
    rows += [jnp.zeros_like(norm)] * (depth - len(rows))
    put_rows(rows_ref, 0, rows)


def turn_group(rows_ref, group):
    turned = jnp.concatenate(
        [
            jnp.concatenate([rows_ref[half, pl.ds((group * 4 + j) * pitch, depth), :] for j in range(4)], axis=0).T
            for half in range(rows_ref.shape[0])
        ],
        axis=0,
    )
    lanes = [depth * j + 24 for j in range(4)]
    return turned.astype(bf16), [jnp.broadcast_to(turned[:, n : n + 1], turned.shape) for n in lanes]


def placed(b, j):
    above, below = [jnp.zeros((depth * n, b.shape[1]), bf16) for n in (j, 3 - j)]
    return jnp.concatenate([above] * (j > 0) + [b] + [below] * (j < 3), axis=0)


def fold(x):
    return jnp.sum(x.reshape(x.shape[0] // 8, 8, x.shape[1]), axis=0)


def column_sums(weight, s):
    load = jnp.concatenate([s] * (weight.shape[1] // 128), axis=1)
    return fold(weight * load), fold(weight)


def add_pair(sums_ref, t, a, s, b, live=None):
    weight = jnp.exp2(jnp.dot(a, b, preferred_element_type=f32))
    num, den = column_sums(weight, s)
    if live is not None:
        num, den = num * live, den * live
    sums_ref[0, t] = sums_ref[0, t] + num
    sums_ref[1, t] = sums_ref[1, t] + den


def repeat_target(compact, b_ref):
    def some_tiles(step, carry):
        for t in [step * 4 + i for i in range(4)]:
            block = compact[t]
            for j in range(4):
                b_ref[t, depth * j : depth * (j + 1), :] = block
        return carry

    lax.fori_loop(0, compact.shape[0] // 4, some_tiles, 0)


def fetch(sources, targets, sems):
    copies = [pltpu.make_async_copy(src, dst, sems.at[i]) for i, (src, dst) in enumerate(zip(sources, targets))]
    for copy in copies:
        copy.start()
    return copies


def pack_kernel(
    peers,
    coords,
    strain,
    tile_count_in,
    send_tile_in,
    remote_pairs_in,
    remote_count_in,
    local_pairs_in,
    twice,
    outbox,
    strain_here,
    tile_count,
    send_tile,
    remote_pairs,
    remote_count,
    own_tile,
    own_live,
    blocks,
    local_pairs,
    sems,
):
    tiles, points = strain.shape
    payload = twice.at[0]
    copies = fetch(
        (coords, strain, tile_count_in, send_tile_in, remote_pairs_in, remote_count_in, local_pairs_in),
        (payload.at[0:3], strain_here, tile_count, send_tile, remote_pairs, remote_count, local_pairs),
        sems,
    )
    payload[4] = jnp.zeros((tiles, points), f32)
    for copy in copies:
        copy.wait()
    payload[4, 0:2, 0 : local_pairs.shape[1]] = local_pairs[...].astype(f32)
    lane = lax.broadcasted_iota(jnp.int32, (1, points), 1)
    for t in range(tiles):
        payload[3, t : t + 1, :] = jnp.where(lane < tile_count[t], strain_here[t : t + 1, :], 0.0)

    twice[1] = twice[0]
    halves = points // 128
    for k in range(4):
        for half in range(halves):
            rows = payload[k, 0:4, half * 128 : (half + 1) * 128]
            for first in (0, 4):
                blocks[pl.ds(half * 8 + first + k, 4, stride=8 * halves), :] = rows

    def listed(i, carry):
        h = remote_pairs[1, i]
        own_tile[h] = remote_pairs[0, i]
        own_live[h] = (i < remote_count[0]).astype(jnp.int32)
        return carry

    lax.fori_loop(0, peers, listed, 0, unroll=peers <= 8)
    row = lax.broadcasted_iota(jnp.int32, (8, 128), 0)

    def message(h, carry):
        masked = (row == 7) & (own_live[h] == 0)
        for half in range(halves):
            sent, own = [
                blocks[pl.ds(pl.multiple_of((t * halves + half) * 8, 8), 8), :] for t in (send_tile[h], own_tile[h])
            ]
            both = jnp.where(row < 4, sent, jnp.where(masked, 0.0, own))
            outbox[pl.ds(pl.multiple_of((h * halves + half) * 8, 8), 8), :] = both
        return carry

    lax.fori_loop(0, peers, message, 0, unroll=peers <= 8)


def spread_rows(values):
    n = values.shape[1]
    wide = jnp.concatenate([values.astype(f32), jnp.zeros((1, 128 - n), f32)], axis=1)
    return jnp.broadcast_to(wide, (128, 128)).T[0:n]


def own_kernel(pairs, twice, b_out, sums_ref, rows_ref, a_ref, s_ref, b_ref, local_pairs, sems):
    payload = twice.at[0]
    tiles = payload.shape[1]
    copies = fetch((payload.at[4, 0:8, 0:128],), (local_pairs,), sems)
    planes = [payload[k] for k in range(4)]
    put_target(planes, rows_ref)

    def set_target(group, carry):
        for t in [group * 4 + i for i in range(4)]:
            rows = pl.ds(t * pitch, depth)
            for half in range(rows_ref.shape[0]):
                b_out[t, :, half * 128 : (half + 1) * 128] = rows_ref[half, rows, :].astype(bf16)
        return carry

    lax.fori_loop(0, tiles // 4, set_target, 0)
    repeat_target(b_out, b_ref)
    put_source(planes, rows_ref, 0)
    sums_ref[...] = jnp.zeros_like(sums_ref)
    for copy in copies:
        copy.wait()

    column = lax.broadcasted_iota(jnp.int32, (1, 4 * depth), 1) // depth

    def own(step, carry):
        for group in [8 * step + g for g in range(8)]:
            left, loads = turn_group(rows_ref, group)
            for i, s in enumerate(loads):
                t = group * 4 + i
                a = left * (column == i).astype(f32).astype(bf16)
                a_ref[t] = a
                s_ref[t] = s
                add_pair(sums_ref, t, a, s, b_ref[t])
        return carry

    lax.fori_loop(0, tiles // 32, own, 0)

    def listed(step, carry):
        for i in range(32):
            one = local_pairs[0, step * 32 + i].astype(jnp.int32)
            two = local_pairs[1, step * 32 + i].astype(jnp.int32)
            add_pair(sums_ref, two, a_ref[one], s_ref[one], b_ref[two])
            add_pair(sums_ref, one, a_ref[two], s_ref[two], b_ref[one])
        return carry

    lax.fori_loop(0, pairs // 32, listed, 0)


def rest_kernel(
    peers,
    late,
    soon,
    inbox,
    b_ref,
    sums_in,
    twice,
    history_in,
    corner_load_in,
    external_in,
    tile_sub_in,
    corner_map_in,
    send_tile_in,
    remote_pairs_in,
    remote_count_in,
    damage_out,
    parts_ref,
    damage_ref,
    history,
    corner_load,
    external,
    tile_sub,
    corner_map,
    rows_ref,
    far_rows,
    sums_ref,
    send_tile,
    remote_pairs,
    remote_count,
    far_tile,
    far_live,
    sems,
):
    tiles, points = history.shape
    payload = twice.at[0]
    halves = points // 128
    groups = tiles // 4
    count = lax.axis_size("sub")
    layer = lax.axis_index("sub")
    copies = fetch(
        (
            send_tile_in,
            remote_pairs_in,
            remote_count_in,
            history_in,
            corner_load_in,
            external_in,
            tile_sub_in,
            corner_map_in,
        ),
        (send_tile, remote_pairs, remote_count, history, corner_load, external, tile_sub, corner_map),
        sems.at[0:8],
    )

    sums_ref[...] = sums_in[...]

    def border(tiles_in, place, partner, shift):
        def some(step, carry):
            for group in [8 * step + g for g in range(8)]:
                left, loads = turn_group(rows_ref, group)
                for i, s in enumerate(loads):
                    u = group * 4 + i
                    add_pair(sums_ref, u, left, s, placed(b_ref[u], i))
                    t = lax.rem(u + shift + tiles, tiles)
                    add_pair(sums_ref, t, left, s, placed(b_ref[t], i))
            return carry

        @pl.when((partner >= 0) & (partner < count))
        def both():
            put_source([tiles_in[place, k] for k in range(4)], rows_ref, 0)
            lax.fori_loop(0, groups // 8, some, 0)

    up = 1 - 2 * lax.rem(layer, 2)
    odd = lax.rem(layer, 2)
    border(soon, odd, layer - up, -up)
    border(late, 1 - odd, layer + up, up)

    for copy in copies:
        copy.wait()
    for which in range(2):
        planes = [
            jnp.concatenate(
                [inbox[pl.ds(half * 8 + 4 * which + k, peers, stride=8 * halves), :] for half in range(halves)], axis=1
            )
            for k in range(4)
        ]
        put_source(planes, far_rows, which * peers)

    def place(i, carry):
        h = remote_pairs[1, i]
        far_tile[h] = remote_pairs[0, i]
        far_live[h] = (i < remote_count[0]).astype(jnp.int32)
        far_tile[peers + i] = send_tile[i]
        far_live[peers + i] = 1
        return carry

    lax.fori_loop(0, peers, place, 0, unroll=peers <= 8)

    def far(step, carry):
        for group in [4 * step + g for g in range(4)]:
            left, loads = turn_group(far_rows, group)
            for i, s in enumerate(loads):
                t = far_tile[group * 4 + i]
                add_pair(sums_ref, t, left, s, placed(b_ref[t], i), far_live[group * 4 + i].astype(f32))
        return carry

    lax.fori_loop(0, 2 * peers // 16, far, 0)

    valid = (payload[3] > 0.0).astype(f32)
    num, den = jnp.sum(sums_ref[...], axis=2)
    strain_bar = num / (den + 1.0 - valid)
    kappa = jnp.maximum(strain_bar, history[...])
    damage = 1.0 - (keep_share + (1.0 - keep_share) * jnp.exp(-softening * (kappa - 1.0))) / kappa
    damage_ref[...] = damage
    leaving = pltpu.make_async_copy(damage_ref, damage_out, sems.at[8])
    leaving.start()
    intact = (1.0 - damage) * valid

    folded = corner_load[:, :, 0:128] * intact[None, :, 0:128]
    for half in range(1, points // 128):
        cut = slice(half * 128, (half + 1) * 128)
        folded = folded + corner_load[:, :, cut] * intact[None, :, cut]
    owner = spread_rows(tile_sub[...].reshape(1, tiles))
    subs, corners = corner_map.shape
    map_rows = spread_rows(jnp.concatenate([corner_map[m : m + 1, :] for m in range(subs)], axis=1))
    sums = []
    for m in range(subs):
        chosen = jnp.where((owner == float(m))[None], folded, 0.0)
        sums.append(jnp.sum(jnp.sum(chosen, axis=1), axis=1, keepdims=True))
    sub_part = jnp.broadcast_to(jnp.concatenate(sums, axis=0), (subs * corners, 128))
    target = map_rows.astype(jnp.int32) - lax.broadcasted_iota(jnp.int32, (subs * corners, 128), 1)

    def scatter(j, carry):
        held = jnp.where(j == lax.axis_index("blk"), external[...], 0.0).reshape(1, 128)
        force = jnp.sum(jnp.where(target == j * 128, sub_part, 0.0), axis=0, keepdims=True)
        parts_ref[pl.ds(j, 1), :] = held - force
        return carry

    lax.fori_loop(0, peers, scatter, 0, unroll=peers <= 8)
    leaving.wait()


def per_device(
    coords,
    strain,
    history,
    corner_load,
    tile_count,
    tile_sub,
    local_pairs,
    send_tile,
    remote_pairs,
    remote_count,
    corner_map,
    external,
):
    tiles, points = strain.shape
    halves = points // 128
    peers = lax.axis_size("blk")
    params = pltpu.CompilerParams(vmem_limit_bytes=grant)
    block = 2 * points * points

    payload, outbox = pl.pallas_call(
        functools.partial(pack_kernel, peers),
        out_shape=(
            pltpu.VMEM((2, 5, tiles, points), f32),
            pltpu.VMEM((peers * halves * 8, 128), f32),
        ),
        in_specs=[anywhere] * 7,
        out_specs=(in_vmem, in_vmem),
        scratch_shapes=[pltpu.VMEM((tiles, points), f32)]
        + [pltpu.SMEM(v.shape, jnp.int32) for v in (tile_count, send_tile, remote_pairs, remote_count)]
        + [pltpu.SMEM((peers,), jnp.int32)] * 2
        + [pltpu.VMEM((4 * halves * 8, 128), f32)]
        + [pltpu.VMEM(local_pairs.shape, jnp.int32), pltpu.SemaphoreType.DMA((7,))],
        compiler_params=params,
        name="pack",
    )(*(in_hbm(v) for v in (coords, strain, tile_count, send_tile, remote_pairs, remote_count, local_pairs)))

    layers = lax.axis_size("sub")
    soon, late = [
        lax.all_to_all(
            payload,
            "sub",
            split_axis=0,
            concat_axis=0,
            axis_index_groups=[sorted((i, (i + 1) % layers)) for i in range(first, layers, 2)],
            tiled=True,
        )
        for first in (1, 0)
    ]
    inbox = lax.all_to_all(outbox, "blk", split_axis=0, concat_axis=0, tiled=True)

    b_own, sums = pl.pallas_call(
        functools.partial(own_kernel, local_pairs.shape[1]),
        out_shape=(
            jax.ShapeDtypeStruct((tiles, depth, points), bf16),
            jax.ShapeDtypeStruct((2, tiles, 8, points), f32),
        ),
        in_specs=[in_vmem],
        out_specs=(in_vmem,) * 2,
        scratch_shapes=[
            pltpu.VMEM((halves, tiles * pitch, 128), f32),
            pltpu.VMEM((tiles, points, 4 * depth), bf16),
            pltpu.VMEM((tiles, points, 128), f32),
            pltpu.VMEM((tiles, 4 * depth, points), bf16),
            pltpu.SMEM((8, 128), f32),
            pltpu.SemaphoreType.DMA((1,)),
        ],
        compiler_params=params,
        cost_estimate=pl.CostEstimate(
            flops=3 * tiles * block * depth, bytes_accessed=1 << 20, transcendentals=3 * tiles * points * points
        ),
        name="own",
    )(payload)

    damage, parts = pl.pallas_call(
        functools.partial(rest_kernel, peers),
        out_shape=(
            jax.ShapeDtypeStruct((tiles, points), f32),
            jax.ShapeDtypeStruct((peers, 128), f32),
        ),
        in_specs=[in_vmem] * 6 + [anywhere] * 8,
        out_specs=(anywhere, in_vmem),
        scratch_shapes=[pltpu.VMEM(v.shape, v.dtype) for v in (strain, history, corner_load, external, tile_sub, corner_map)]
        + [
            pltpu.VMEM((halves, tiles * pitch, 128), f32),
            pltpu.VMEM((halves, 2 * peers * pitch, 128), f32),
            pltpu.VMEM(sums.shape, f32),
        ]
        + [pltpu.SMEM(v.shape, jnp.int32) for v in (send_tile, remote_pairs, remote_count)]
        + [pltpu.SMEM((2 * peers,), jnp.int32)] * 2
        + [pltpu.SemaphoreType.DMA((9,))],
        compiler_params=params,
        cost_estimate=pl.CostEstimate(
            flops=4 * tiles * block * depth, bytes_accessed=1 << 21, transcendentals=4 * tiles * points * points
        ),
        name="rest",
    )(
        late,
        soon,
        inbox,
        b_own,
        sums,
        payload,
        *(
            in_hbm(v)
            for v in (
                history,
                corner_load,
                external,
                tile_sub,
                corner_map,
                send_tile,
                remote_pairs,
                remote_count,
            )
        ),
    )
    gathered = lax.all_to_all(parts, "blk", split_axis=0, concat_axis=0, tiled=True)
    return damage, jnp.sum(gathered, axis=0)


def solution(mesh):
    placed = (
        P(None, ("sub", "blk"), None),
        P(("sub", "blk"), None),
        P(("sub", "blk"), None),
        P(None, ("sub", "blk"), None),
        P(("sub", "blk")),
        P(("sub", "blk")),
        P(None, ("sub", "blk")),
        P(("sub", "blk")),
        P(None, ("sub", "blk")),
        P(("sub", "blk")),
        P(("sub", "blk"), None),
        P(("sub", "blk")),
    )
    return jax.shard_map(
        per_device,
        mesh=mesh,
        in_specs=placed,
        out_specs=(P(("sub", "blk"), None), P(("sub", "blk"))),
        check_vma=False,
    )
```

```python
import functools
import math

import jax
import jax.numpy as jnp
from jax import lax
from jax.experimental import pallas as pl
from jax.experimental.pallas import tpu as pltpu
from jax.sharding import PartitionSpec as P

gauss_rate = 4.0
keep_share = 0.05
softening = 0.5
coord_scale = math.sqrt(gauss_rate * math.log2(math.e))
far_off = 2048.0
depth = 32
pitch = depth + 1
grant = 24 * 1024 * 1024

f32 = jnp.float32
bf16 = jnp.bfloat16
in_vmem = pl.BlockSpec(memory_space=pltpu.VMEM)
anywhere = pl.BlockSpec(memory_space=pl.ANY)


def in_hbm(value):
    return value if value.size == 1 else pltpu.with_memory_space_constraint(value, pltpu.HBM)


def pieces(value):
    high = value.astype(bf16).astype(f32)
    rest = value - high
    middle = rest.astype(bf16).astype(f32)
    low = (rest - middle).astype(bf16).astype(f32)
    return high, middle, low


def put_rows(rows_ref, base, rows):
    for r, row in enumerate(rows):
        tiles = row.shape[0]
        for half in range(row.shape[1] // 128):
            rows_ref[half, pl.ds(base * pitch + r, tiles, stride=pitch), :] = row[:, half * 128 : (half + 1) * 128]


def point_rows(planes):
    scaled = [p * coord_scale for p in planes[:3]]
    split = [pieces(s) for s in scaled]
    norm = scaled[0] * scaled[0] + scaled[1] * scaled[1] + scaled[2] * scaled[2]
    return split, norm + jnp.where(planes[3] > 0.0, 0.0, far_off)


def put_source(planes, rows_ref, base):
    split, norm = point_rows(planes)
    ones = jnp.ones_like(norm)
    rows = []
    for high, middle, low in split:
        rows += [high, high, middle, high, low, middle]
    rows += list(pieces(-norm)) + [ones, ones, ones] + [planes[3]]
    rows += [jnp.zeros_like(norm)] * (depth - len(rows))
    put_rows(rows_ref, base, rows)


def put_target(planes, rows_ref):
    split, norm = point_rows(planes)
    ones = jnp.ones_like(norm)
    rows = []
    for high, middle, low in split:
        rows += [2.0 * v for v in (high, middle, high, low, high, middle)]
    rows += [ones, ones, ones] + list(pieces(-norm))
    rows += [jnp.zeros_like(norm)] * (depth - len(rows))
    put_rows(rows_ref, 0, rows)


def turn_group(rows_ref, group):
    turned = jnp.concatenate(
        [
            jnp.concatenate([rows_ref[half, pl.ds((group * 4 + j) * pitch, depth), :] for j in range(4)], axis=0).T
            for half in range(rows_ref.shape[0])
        ],
        axis=0,
    )
    lanes = [depth * j + 24 for j in range(4)]
    return turned.astype(bf16), [jnp.broadcast_to(turned[:, n : n + 1], turned.shape) for n in lanes]


def placed(b, j):
    above, below = [jnp.zeros((depth * n, b.shape[1]), bf16) for n in (j, 3 - j)]
    return jnp.concatenate([above] * (j > 0) + [b] + [below] * (j < 3), axis=0)


def fold(x):
    return jnp.sum(x.reshape(x.shape[0] // 8, 8, x.shape[1]), axis=0)


def column_sums(weight, s):
    load = jnp.concatenate([s] * (weight.shape[1] // 128), axis=1)
    return fold(weight * load), fold(weight)


def add_pair(sums_ref, t, a, s, b, live=None, first=False, rows=None):
    num, den = 0.0, 0.0
    rows = rows or a.shape[0]
    for lo in range(0, a.shape[0], rows):
        weight = jnp.exp2(jnp.dot(a[lo : lo + rows], b, preferred_element_type=f32))
        more_num, more_den = column_sums(weight, s[lo : lo + rows])
        num, den = num + more_num, den + more_den
    if live is not None:
        num, den = num * live, den * live
    if not first:
        num, den = sums_ref[0, t] + num, sums_ref[1, t] + den
    sums_ref[0, t] = num
    sums_ref[1, t] = den


def repeat_target(compact, b_ref):
    def some_tiles(step, carry):
        for t in [step * 4 + i for i in range(4)]:
            block = compact[t]
            for j in range(4):
                b_ref[t, depth * j : depth * (j + 1), :] = block
        return carry

    lax.fori_loop(0, compact.shape[0] // 4, some_tiles, 0)


def fetch(sources, targets, sems):
    copies = [pltpu.make_async_copy(src, dst, sems.at[i]) for i, (src, dst) in enumerate(zip(sources, targets))]
    for copy in copies:
        copy.start()
    return copies


def pack_kernel(
    peers,
    coords,
    strain,
    tile_count_in,
    send_tile_in,
    remote_pairs_in,
    remote_count_in,
    local_pairs_in,
    payload,
    outbox,
    strain_here,
    tile_count,
    send_tile,
    remote_pairs,
    remote_count,
    own_tile,
    own_live,
    blocks,
    local_pairs,
    sems,
):
    tiles, points = strain.shape
    copies = fetch(
        (coords, strain, tile_count_in, send_tile_in, remote_pairs_in, remote_count_in, local_pairs_in),
        (payload.at[0:3], strain_here, tile_count, send_tile, remote_pairs, remote_count, local_pairs),
        sems,
    )
    payload[4] = jnp.zeros((tiles, points), f32)
    for copy in copies:
        copy.wait()
    payload[4, 0:2, 0 : local_pairs.shape[1]] = local_pairs[...].astype(f32)
    lane = lax.broadcasted_iota(jnp.int32, (1, points), 1)
    for t in range(tiles):
        payload[3, t : t + 1, :] = jnp.where(lane < tile_count[t], strain_here[t : t + 1, :], 0.0)

    halves = points // 128
    for k in range(4):
        for half in range(halves):
            rows = payload[k, 0:4, half * 128 : (half + 1) * 128]
            for first in (0, 4):
                blocks[pl.ds(half * 8 + first + k, 4, stride=8 * halves), :] = rows

    def listed(i, carry):
        h = remote_pairs[1, i]
        own_tile[h] = remote_pairs[0, i]
        own_live[h] = (i < remote_count[0]).astype(jnp.int32)
        return carry

    lax.fori_loop(0, peers, listed, 0, unroll=peers <= 8)
    row = lax.broadcasted_iota(jnp.int32, (8, 128), 0)

    def message(h, carry):
        masked = (row == 7) & (own_live[h] == 0)
        for half in range(halves):
            sent, own = [
                blocks[pl.ds(pl.multiple_of((t * halves + half) * 8, 8), 8), :] for t in (send_tile[h], own_tile[h])
            ]
            both = jnp.where(row < 4, sent, jnp.where(masked, 0.0, own))
            outbox[pl.ds(pl.multiple_of((h * halves + half) * 8, 8), 8), :] = both
        return carry

    lax.fori_loop(0, peers, message, 0, unroll=peers <= 8)


def spread_rows(values):
    n = values.shape[1]
    wide = jnp.concatenate([values.astype(f32), jnp.zeros((1, 128 - n), f32)], axis=1)
    return jnp.broadcast_to(wide, (128, 128)).T[0:n]


def own_kernel(pairs, payload, b_out, sums_ref, rows_ref, a_ref, s_ref, b_ref, local_pairs, sems):
    tiles = payload.shape[1]
    copies = fetch((payload.at[4, 0:8, 0:128],), (local_pairs,), sems)
    planes = [payload[k] for k in range(4)]
    put_target(planes, rows_ref)

    def set_target(group, carry):
        for t in [group * 4 + i for i in range(4)]:
            rows = pl.ds(t * pitch, depth)
            for half in range(rows_ref.shape[0]):
                b_out[t, :, half * 128 : (half + 1) * 128] = rows_ref[half, rows, :].astype(bf16)
        return carry

    lax.fori_loop(0, tiles // 4, set_target, 0)
    repeat_target(b_out, b_ref)
    put_source(planes, rows_ref, 0)
    for copy in copies:
        copy.wait()

    column = lax.broadcasted_iota(jnp.int32, (1, 4 * depth), 1) // depth

    def own(step, carry):
        for group in [8 * step + g for g in range(8)]:
            left, loads = turn_group(rows_ref, group)
            for i, s in enumerate(loads):
                t = group * 4 + i
                a = left * (column == i).astype(f32).astype(bf16)
                a_ref[t] = a
                s_ref[t] = s
                add_pair(sums_ref, t, a, s, b_ref[t], first=True, rows=128)
        return carry

    lax.fori_loop(0, tiles // 32, own, 0)

    def listed(step, carry):
        for i in range(32):
            one = local_pairs[0, step * 32 + i].astype(jnp.int32)
            two = local_pairs[1, step * 32 + i].astype(jnp.int32)
            add_pair(sums_ref, two, a_ref[one], s_ref[one], b_ref[two], rows=128)
            add_pair(sums_ref, one, a_ref[two], s_ref[two], b_ref[one], rows=128)
        return carry

    lax.fori_loop(0, pairs // 32, listed, 0)


def rest_kernel(
    peers,
    late,
    soon,
    inbox,
    b_ref,
    sums_in,
    payload,
    history_in,
    corner_load_in,
    external_in,
    tile_sub_in,
    corner_map_in,
    send_tile_in,
    remote_pairs_in,
    remote_count_in,
    damage_out,
    parts_ref,
    damage_ref,
    history,
    corner_load,
    external,
    tile_sub,
    corner_map,
    rows_ref,
    far_rows,
    sums_ref,
    send_tile,
    remote_pairs,
    remote_count,
    far_tile,
    far_live,
    sems,
):
    tiles, points = history.shape
    halves = points // 128
    groups = tiles // 4
    count = lax.axis_size("sub")
    layer = lax.axis_index("sub")
    copies = fetch(
        (
            send_tile_in,
            remote_pairs_in,
            remote_count_in,
            history_in,
            corner_load_in,
            external_in,
            tile_sub_in,
            corner_map_in,
        ),
        (send_tile, remote_pairs, remote_count, history, corner_load, external, tile_sub, corner_map),
        sems.at[0:8],
    )

    sums_ref[...] = sums_in[...]

    up = 1 - 2 * lax.rem(layer, 2)

    def border(side, carry):
        shift = jnp.where(side == 0, -up, up)
        partner = layer + shift

        def some(step, carry):
            for group in [8 * step + g for g in range(8)]:
                left, loads = turn_group(rows_ref, group)
                for i, s in enumerate(loads):
                    u = group * 4 + i
                    add_pair(sums_ref, u, left, s, placed(b_ref[u], i))
                    t = lax.rem(u + shift + tiles, tiles)
                    add_pair(sums_ref, t, left, s, placed(b_ref[t], i))
            return carry

        @pl.when((partner >= 0) & (partner < count))
        def both():
            put_source([jnp.where(side == 0, soon[k], late[k]) for k in range(4)], rows_ref, 0)
            lax.fori_loop(0, groups // 8, some, 0)

        return carry

    lax.fori_loop(0, 2, border, 0)

    for copy in copies:
        copy.wait()
    for which in range(2):
        planes = [
            jnp.concatenate(
                [inbox[pl.ds(half * 8 + 4 * which + k, peers, stride=8 * halves), :] for half in range(halves)], axis=1
            )
            for k in range(4)
        ]
        put_source(planes, far_rows, which * peers)

    def place(i, carry):
        h = remote_pairs[1, i]
        far_tile[h] = remote_pairs[0, i]
        far_live[h] = (i < remote_count[0]).astype(jnp.int32)
        far_tile[peers + i] = send_tile[i]
        far_live[peers + i] = 1
        return carry

    lax.fori_loop(0, peers, place, 0, unroll=peers <= 8)

    def far(step, carry):
        for group in [4 * step + g for g in range(4)]:
            left, loads = turn_group(far_rows, group)
            for i, s in enumerate(loads):
                t = far_tile[group * 4 + i]
                add_pair(sums_ref, t, left, s, placed(b_ref[t], i), far_live[group * 4 + i].astype(f32))
        return carry

    lax.fori_loop(0, 2 * peers // 16, far, 0)

    valid = (payload[3] > 0.0).astype(f32)
    num, den = jnp.sum(sums_ref[...], axis=2)
    strain_bar = num / (den + 1.0 - valid)
    kappa = jnp.maximum(strain_bar, history[...])
    damage = 1.0 - (keep_share + (1.0 - keep_share) * jnp.exp(-softening * (kappa - 1.0))) / kappa
    damage_ref[...] = damage
    leaving = pltpu.make_async_copy(damage_ref, damage_out, sems.at[8])
    leaving.start()
    intact = (1.0 - damage) * valid

    folded = corner_load[:, :, 0:128] * intact[None, :, 0:128]
    for half in range(1, points // 128):
        cut = slice(half * 128, (half + 1) * 128)
        folded = folded + corner_load[:, :, cut] * intact[None, :, cut]
    owner = spread_rows(tile_sub[...].reshape(1, tiles))
    subs, corners = corner_map.shape
    map_rows = spread_rows(jnp.concatenate([corner_map[m : m + 1, :] for m in range(subs)], axis=1))
    sums = []
    for m in range(subs):
        chosen = jnp.where((owner == float(m))[None], folded, 0.0)
        sums.append(jnp.sum(jnp.sum(chosen, axis=1), axis=1, keepdims=True))
    sub_part = jnp.broadcast_to(jnp.concatenate(sums, axis=0), (subs * corners, 128))
    target = map_rows.astype(jnp.int32) - lax.broadcasted_iota(jnp.int32, (subs * corners, 128), 1)

    def scatter(j, carry):
        held = jnp.where(j == lax.axis_index("blk"), external[...], 0.0).reshape(1, 128)
        force = jnp.sum(jnp.where(target == j * 128, sub_part, 0.0), axis=0, keepdims=True)
        parts_ref[pl.ds(j, 1), :] = held - force
        return carry

    lax.fori_loop(0, peers, scatter, 0, unroll=peers <= 8)
    leaving.wait()


def per_device(
    coords,
    strain,
    history,
    corner_load,
    tile_count,
    tile_sub,
    local_pairs,
    send_tile,
    remote_pairs,
    remote_count,
    corner_map,
    external,
):
    tiles, points = strain.shape
    halves = points // 128
    peers = lax.axis_size("blk")
    params = pltpu.CompilerParams(vmem_limit_bytes=grant)
    block = 2 * points * points

    payload, outbox = pl.pallas_call(
        functools.partial(pack_kernel, peers),
        out_shape=(
            pltpu.VMEM((5, tiles, points), f32),
            pltpu.VMEM((peers * halves * 8, 128), f32),
        ),
        in_specs=[anywhere] * 7,
        out_specs=(in_vmem, in_vmem),
        scratch_shapes=[pltpu.VMEM((tiles, points), f32)]
        + [pltpu.SMEM(v.shape, jnp.int32) for v in (tile_count, send_tile, remote_pairs, remote_count)]
        + [pltpu.SMEM((peers,), jnp.int32)] * 2
        + [pltpu.VMEM((4 * halves * 8, 128), f32)]
        + [pltpu.VMEM(local_pairs.shape, jnp.int32), pltpu.SemaphoreType.DMA((7,))],
        compiler_params=params,
        name="pack",
    )(*(in_hbm(v) for v in (coords, strain, tile_count, send_tile, remote_pairs, remote_count, local_pairs)))

    layers = lax.axis_size("sub")
    late, soon = [
        lax.ppermute(payload, "sub", [p for i in range(first, layers - 1, 2) for p in ((i, i + 1), (i + 1, i))])
        for first in (0, 1)
    ]
    inbox = lax.all_to_all(outbox, "blk", split_axis=0, concat_axis=0, tiled=True)

    b_own, sums = pl.pallas_call(
        functools.partial(own_kernel, local_pairs.shape[1]),
        out_shape=(
            jax.ShapeDtypeStruct((tiles, depth, points), bf16),
            jax.ShapeDtypeStruct((2, tiles, 8, points), f32),
        ),
        in_specs=[in_vmem],
        out_specs=(in_vmem,) * 2,
        scratch_shapes=[
            pltpu.VMEM((halves, tiles * pitch, 128), f32),
            pltpu.VMEM((tiles, points, 4 * depth), bf16),
            pltpu.VMEM((tiles, points, 128), f32),
            pltpu.VMEM((tiles, 4 * depth, points), bf16),
            pltpu.SMEM((8, 128), f32),
            pltpu.SemaphoreType.DMA((1,)),
        ],
        compiler_params=params,
        cost_estimate=pl.CostEstimate(
            flops=3 * tiles * block * depth, bytes_accessed=1 << 20, transcendentals=3 * tiles * points * points
        ),
        name="own",
    )(payload)

    damage, parts = pl.pallas_call(
        functools.partial(rest_kernel, peers),
        out_shape=(
            jax.ShapeDtypeStruct((tiles, points), f32),
            jax.ShapeDtypeStruct((peers, 128), f32),
        ),
        in_specs=[in_vmem] * 6 + [anywhere] * 8,
        out_specs=(anywhere, in_vmem),
        scratch_shapes=[pltpu.VMEM(v.shape, v.dtype) for v in (strain, history, corner_load, external, tile_sub, corner_map)]
        + [
            pltpu.VMEM((halves, tiles * pitch, 128), f32),
            pltpu.VMEM((halves, 2 * peers * pitch, 128), f32),
            pltpu.VMEM(sums.shape, f32),
        ]
        + [pltpu.SMEM(v.shape, jnp.int32) for v in (send_tile, remote_pairs, remote_count)]
        + [pltpu.SMEM((2 * peers,), jnp.int32)] * 2
        + [pltpu.SemaphoreType.DMA((9,))],
        compiler_params=params,
        cost_estimate=pl.CostEstimate(
            flops=4 * tiles * block * depth, bytes_accessed=1 << 21, transcendentals=4 * tiles * points * points
        ),
        name="rest",
    )(
        late,
        soon,
        inbox,
        b_own,
        sums,
        payload,
        *(
            in_hbm(v)
            for v in (
                history,
                corner_load,
                external,
                tile_sub,
                corner_map,
                send_tile,
                remote_pairs,
                remote_count,
            )
        ),
    )
    gathered = lax.all_to_all(parts, "blk", split_axis=0, concat_axis=0, tiled=True)
    return damage, jnp.sum(gathered, axis=0)


def solution(mesh):
    placed = (
        P(None, ("sub", "blk"), None),
        P(("sub", "blk"), None),
        P(("sub", "blk"), None),
        P(None, ("sub", "blk"), None),
        P(("sub", "blk")),
        P(("sub", "blk")),
        P(None, ("sub", "blk")),
        P(("sub", "blk")),
        P(None, ("sub", "blk")),
        P(("sub", "blk")),
        P(("sub", "blk"), None),
        P(("sub", "blk")),
    )
    return jax.shard_map(
        per_device,
        mesh=mesh,
        in_specs=placed,
        out_specs=(P(("sub", "blk"), None), P(("sub", "blk"))),
        check_vma=False,
    )
```

```python
import functools
import math

import jax
import jax.numpy as jnp
from jax import lax
from jax.experimental import pallas as pl
from jax.experimental.pallas import tpu as pltpu
from jax.sharding import PartitionSpec as P

gauss_rate = 4.0
keep_share = 0.05
softening = 0.5
coord_scale = math.sqrt(gauss_rate * math.log2(math.e))
far_off = 2048.0
depth = 32
pitch = depth + 1
grant = 24 * 1024 * 1024

f32 = jnp.float32
bf16 = jnp.bfloat16
in_vmem = pl.BlockSpec(memory_space=pltpu.VMEM)
anywhere = pl.BlockSpec(memory_space=pl.ANY)


def in_hbm(value):
    return value if value.size == 1 else pltpu.with_memory_space_constraint(value, pltpu.HBM)


def pieces(value):
    high = value.astype(bf16).astype(f32)
    rest = value - high
    middle = rest.astype(bf16).astype(f32)
    low = (rest - middle).astype(bf16).astype(f32)
    return high, middle, low


def put_rows(rows_ref, base, rows):
    for r, row in enumerate(rows):
        tiles = row.shape[0]
        for half in range(row.shape[1] // 128):
            rows_ref[half, pl.ds(base * pitch + r, tiles, stride=pitch), :] = row[:, half * 128 : (half + 1) * 128]


def point_rows(planes):
    scaled = [p * coord_scale for p in planes[:3]]
    split = [pieces(s) for s in scaled]
    norm = scaled[0] * scaled[0] + scaled[1] * scaled[1] + scaled[2] * scaled[2]
    return split, norm + jnp.where(planes[3] > 0.0, 0.0, far_off)


def put_source(planes, rows_ref, base):
    split, norm = point_rows(planes)
    ones = jnp.ones_like(norm)
    rows = []
    for high, middle, low in split:
        rows += [high, high, middle, high, low, middle]
    rows += list(pieces(-norm)) + [ones, ones, ones] + [planes[3]]
    rows += [jnp.zeros_like(norm)] * (depth - len(rows))
    put_rows(rows_ref, base, rows)


def put_target(planes, rows_ref):
    split, norm = point_rows(planes)
    ones = jnp.ones_like(norm)
    rows = []
    for high, middle, low in split:
        rows += [2.0 * v for v in (high, middle, high, low, high, middle)]
    rows += [ones, ones, ones] + list(pieces(-norm))
    rows += [jnp.zeros_like(norm)] * (depth - len(rows))
    put_rows(rows_ref, 0, rows)


def turn_group(rows_ref, group):
    turned = jnp.concatenate(
        [
            jnp.concatenate([rows_ref[half, pl.ds((group * 4 + j) * pitch, depth), :] for j in range(4)], axis=0).T
            for half in range(rows_ref.shape[0])
        ],
        axis=0,
    )
    lanes = [depth * j + 24 for j in range(4)]
    return turned.astype(bf16), [jnp.broadcast_to(turned[:, n : n + 1], turned.shape) for n in lanes]


def placed(b, j):
    above, below = [jnp.zeros((depth * n, b.shape[1]), bf16) for n in (j, 3 - j)]
    return jnp.concatenate([above] * (j > 0) + [b] + [below] * (j < 3), axis=0)


def fold(x):
    return jnp.sum(x.reshape(x.shape[0] // 8, 8, x.shape[1]), axis=0)


def column_sums(weight, s):
    load = jnp.concatenate([s] * (weight.shape[1] // 128), axis=1)
    return fold(weight * load), fold(weight)


def add_pair(sums_ref, t, a, s, b, live=None, first=False, rows=None):
    num, den = 0.0, 0.0
    rows = rows or a.shape[0]
    for lo in range(0, a.shape[0], rows):
        weight = jnp.exp2(jnp.dot(a[lo : lo + rows], b, preferred_element_type=f32))
        more_num, more_den = column_sums(weight, s[lo : lo + rows])
        num, den = num + more_num, den + more_den
    if live is not None:
        num, den = num * live, den * live
    if not first:
        num, den = sums_ref[0, t] + num, sums_ref[1, t] + den
    sums_ref[0, t] = num
    sums_ref[1, t] = den


def repeat_target(compact, b_ref):
    def some_tiles(step, carry):
        for t in [step * 4 + i for i in range(4)]:
            block = compact[t]
            for j in range(4):
                b_ref[t, depth * j : depth * (j + 1), :] = block
        return carry

    lax.fori_loop(0, compact.shape[0] // 4, some_tiles, 0)


def fetch(sources, targets, sems):
    copies = [pltpu.make_async_copy(src, dst, sems.at[i]) for i, (src, dst) in enumerate(zip(sources, targets))]
    for copy in copies:
        copy.start()
    return copies


def pack_kernel(
    peers,
    coords,
    strain,
    tile_count_in,
    send_tile_in,
    remote_pairs_in,
    remote_count_in,
    local_pairs_in,
    payload,
    outbox,
    strain_here,
    tile_count,
    send_tile,
    remote_pairs,
    remote_count,
    own_tile,
    own_live,
    blocks,
    local_pairs,
    sems,
):
    tiles, points = strain.shape
    copies = fetch(
        (coords, strain, tile_count_in, send_tile_in, remote_pairs_in, remote_count_in, local_pairs_in),
        (payload.at[0:3], strain_here, tile_count, send_tile, remote_pairs, remote_count, local_pairs),
        sems,
    )
    payload[4] = jnp.zeros((tiles, points), f32)
    for copy in copies:
        copy.wait()
    payload[4, 0:2, 0 : local_pairs.shape[1]] = local_pairs[...].astype(f32)
    lane = lax.broadcasted_iota(jnp.int32, (1, points), 1)
    for t in range(tiles):
        payload[3, t : t + 1, :] = jnp.where(lane < tile_count[t], strain_here[t : t + 1, :], 0.0)

    halves = points // 128
    for k in range(4):
        for half in range(halves):
            rows = payload[k, 0:4, half * 128 : (half + 1) * 128]
            for first in (0, 4):
                blocks[pl.ds(half * 8 + first + k, 4, stride=8 * halves), :] = rows

    def listed(i, carry):
        h = remote_pairs[1, i]
        own_tile[h] = remote_pairs[0, i]
        own_live[h] = (i < remote_count[0]).astype(jnp.int32)
        return carry

    lax.fori_loop(0, peers, listed, 0, unroll=peers <= 8)
    row = lax.broadcasted_iota(jnp.int32, (8, 128), 0)

    def message(h, carry):
        masked = (row == 7) & (own_live[h] == 0)
        for half in range(halves):
            sent, own = [
                blocks[pl.ds(pl.multiple_of((t * halves + half) * 8, 8), 8), :] for t in (send_tile[h], own_tile[h])
            ]
            both = jnp.where(row < 4, sent, jnp.where(masked, 0.0, own))
            outbox[pl.ds(pl.multiple_of((h * halves + half) * 8, 8), 8), :] = both
        return carry

    lax.fori_loop(0, peers, message, 0, unroll=peers <= 8)


def spread_rows(values):
    n = values.shape[1]
    wide = jnp.concatenate([values.astype(f32), jnp.zeros((1, 128 - n), f32)], axis=1)
    return jnp.broadcast_to(wide, (128, 128)).T[0:n]


def own_kernel(pairs, payload, b_out, sums_ref, rows_ref, a_ref, s_ref, b_ref, local_pairs, sems):
    tiles = payload.shape[1]
    copies = fetch((payload.at[4, 0:8, 0:128],), (local_pairs,), sems)
    planes = [payload[k] for k in range(4)]
    put_target(planes, rows_ref)

    def set_target(group, carry):
        for t in [group * 4 + i for i in range(4)]:
            rows = pl.ds(t * pitch, depth)
            for half in range(rows_ref.shape[0]):
                b_out[t, :, half * 128 : (half + 1) * 128] = rows_ref[half, rows, :].astype(bf16)
        return carry

    lax.fori_loop(0, tiles // 4, set_target, 0)
    repeat_target(b_out, b_ref)
    put_source(planes, rows_ref, 0)
    for copy in copies:
        copy.wait()

    column = lax.broadcasted_iota(jnp.int32, (1, 4 * depth), 1) // depth

    def own(step, carry):
        for group in [8 * step + g for g in range(8)]:
            left, loads = turn_group(rows_ref, group)
            for i, s in enumerate(loads):
                t = group * 4 + i
                a = left * (column == i).astype(f32).astype(bf16)
                a_ref[t] = a
                s_ref[t] = s
                add_pair(sums_ref, t, a, s, b_ref[t], first=True, rows=128)
        return carry

    lax.fori_loop(0, tiles // 32, own, 0)

    def listed(step, carry):
        for i in range(32):
            one = local_pairs[0, step * 32 + i].astype(jnp.int32)
            two = local_pairs[1, step * 32 + i].astype(jnp.int32)
            add_pair(sums_ref, two, a_ref[one], s_ref[one], b_ref[two], rows=128)
            add_pair(sums_ref, one, a_ref[two], s_ref[two], b_ref[one], rows=128)
        return carry

    lax.fori_loop(0, pairs // 32, listed, 0)


def rest_kernel(
    peers,
    late,
    soon,
    inbox,
    b_ref,
    sums_in,
    payload,
    history_in,
    corner_load_in,
    external_in,
    tile_sub_in,
    corner_map_in,
    send_tile_in,
    remote_pairs_in,
    remote_count_in,
    damage_out,
    parts_ref,
    damage_ref,
    history,
    corner_load,
    external,
    tile_sub,
    corner_map,
    rows_ref,
    far_rows,
    sums_ref,
    send_tile,
    remote_pairs,
    remote_count,
    far_tile,
    far_live,
    sems,
):
    tiles, points = history.shape
    halves = points // 128
    groups = tiles // 4
    count = lax.axis_size("sub")
    layer = lax.axis_index("sub")
    copies = fetch(
        (
            send_tile_in,
            remote_pairs_in,
            remote_count_in,
            history_in,
            corner_load_in,
            external_in,
            tile_sub_in,
            corner_map_in,
        ),
        (send_tile, remote_pairs, remote_count, history, corner_load, external, tile_sub, corner_map),
        sems.at[0:8],
    )

    sums_ref[...] = sums_in[...]

    up = 1 - 2 * lax.rem(layer, 2)

    def border(side, carry):
        shift = jnp.where(side == 0, -up, up)
        partner = layer + shift

        def some(step, carry):
            for group in [8 * step + g for g in range(8)]:
                left, loads = turn_group(rows_ref, group)
                for i, s in enumerate(loads):
                    u = group * 4 + i
                    add_pair(sums_ref, u, left, s, placed(b_ref[u], i))
                    t = lax.rem(u + shift + tiles, tiles)
                    add_pair(sums_ref, t, left, s, placed(b_ref[t], i))
            return carry

        @pl.when((partner >= 0) & (partner < count))
        def both():
            put_source([jnp.where(side == 0, soon[k], late[k]) for k in range(4)], rows_ref, 0)
            lax.fori_loop(0, groups // 8, some, 0)

        return carry

    lax.fori_loop(0, 2, border, 0)

    for copy in copies:
        copy.wait()
    for which in range(2):
        planes = [
            jnp.concatenate(
                [inbox[pl.ds(half * 8 + 4 * which + k, peers, stride=8 * halves), :] for half in range(halves)], axis=1
            )
            for k in range(4)
        ]
        put_source(planes, far_rows, which * peers)

    def place(i, carry):
        h = remote_pairs[1, i]
        far_tile[h] = remote_pairs[0, i]
        far_live[h] = (i < remote_count[0]).astype(jnp.int32)
        far_tile[peers + i] = send_tile[i]
        far_live[peers + i] = 1
        return carry

    lax.fori_loop(0, peers, place, 0, unroll=peers <= 8)

    owner = spread_rows(tile_sub[...].reshape(1, tiles))
    subs, corners = corner_map.shape
    map_rows = spread_rows(jnp.concatenate([corner_map[m : m + 1, :] for m in range(subs)], axis=1))
    leaving = []

    def finish(lo, hi):
        valid = (payload[3, lo:hi] > 0.0).astype(f32)
        num, den = jnp.sum(sums_ref[:, lo:hi], axis=2)
        strain_bar = num / (den + 1.0 - valid)
        kappa = jnp.maximum(strain_bar, history[lo:hi])
        damage = 1.0 - (keep_share + (1.0 - keep_share) * jnp.exp(-softening * (kappa - 1.0))) / kappa
        damage_ref[lo:hi] = damage
        leaving.append(
            pltpu.make_async_copy(damage_ref.at[lo:hi], damage_out.at[lo:hi], sems.at[8 + len(leaving)])
        )
        leaving[-1].start()
        intact = (1.0 - damage) * valid
        folded = 0.0
        for half in range(halves):
            cut = slice(half * 128, (half + 1) * 128)
            folded = folded + corner_load[:, lo:hi, cut] * intact[None, :, cut]
        sums = []
        for m in range(subs):
            chosen = jnp.where((owner[lo:hi] == float(m))[None], folded, 0.0)
            sums.append(jnp.sum(chosen.reshape(corners, (hi - lo) // 8, 8, 128), axis=1))
        return sums

    def far(step, carry):
        for group in [4 * step + g for g in range(4)]:
            left, loads = turn_group(far_rows, group)
            for i, s in enumerate(loads):
                t = far_tile[group * 4 + i]
                add_pair(sums_ref, t, left, s, placed(b_ref[t], i), far_live[group * 4 + i].astype(f32))
        return carry

    settled = finish(8, tiles)
    turns = 2 * peers // 16
    if turns == 1:
        far(0, 0)
    else:
        lax.fori_loop(0, turns, far, 0)
    sums = [jnp.sum(x + y, axis=1) for x, y in zip(settled, finish(0, 8))]
    sub_part = jnp.concatenate([jnp.sum(x, axis=1, keepdims=True) for x in sums], axis=0)
    sub_part = jnp.broadcast_to(sub_part, (subs * corners, 128))
    target = map_rows.astype(jnp.int32) - lax.broadcasted_iota(jnp.int32, (subs * corners, 128), 1)

    def scatter(j, carry):
        held = jnp.where(j == lax.axis_index("blk"), external[...], 0.0).reshape(1, 128)
        force = jnp.sum(jnp.where(target == j * 128, sub_part, 0.0), axis=0, keepdims=True)
        parts_ref[pl.ds(j, 1), :] = held - force
        return carry

    lax.fori_loop(0, peers, scatter, 0, unroll=peers <= 8)
    for copy in leaving:
        copy.wait()


def per_device(
    coords,
    strain,
    history,
    corner_load,
    tile_count,
    tile_sub,
    local_pairs,
    send_tile,
    remote_pairs,
    remote_count,
    corner_map,
    external,
):
    tiles, points = strain.shape
    halves = points // 128
    peers = lax.axis_size("blk")
    params = pltpu.CompilerParams(vmem_limit_bytes=grant)
    block = 2 * points * points

    payload, outbox = pl.pallas_call(
        functools.partial(pack_kernel, peers),
        out_shape=(
            pltpu.VMEM((5, tiles, points), f32),
            pltpu.VMEM((peers * halves * 8, 128), f32),
        ),
        in_specs=[anywhere] * 7,
        out_specs=(in_vmem, in_vmem),
        scratch_shapes=[pltpu.VMEM((tiles, points), f32)]
        + [pltpu.SMEM(v.shape, jnp.int32) for v in (tile_count, send_tile, remote_pairs, remote_count)]
        + [pltpu.SMEM((peers,), jnp.int32)] * 2
        + [pltpu.VMEM((4 * halves * 8, 128), f32)]
        + [pltpu.VMEM(local_pairs.shape, jnp.int32), pltpu.SemaphoreType.DMA((7,))],
        compiler_params=params,
        name="pack",
    )(*(in_hbm(v) for v in (coords, strain, tile_count, send_tile, remote_pairs, remote_count, local_pairs)))

    layers = lax.axis_size("sub")
    late, soon = [
        lax.ppermute(payload, "sub", [p for i in range(first, layers - 1, 2) for p in ((i, i + 1), (i + 1, i))])
        for first in (0, 1)
    ]
    inbox = lax.all_to_all(outbox, "blk", split_axis=0, concat_axis=0, tiled=True)

    b_own, sums = pl.pallas_call(
        functools.partial(own_kernel, local_pairs.shape[1]),
        out_shape=(
            jax.ShapeDtypeStruct((tiles, depth, points), bf16),
            jax.ShapeDtypeStruct((2, tiles, 8, points), f32),
        ),
        in_specs=[in_vmem],
        out_specs=(in_vmem,) * 2,
        scratch_shapes=[
            pltpu.VMEM((halves, tiles * pitch, 128), f32),
            pltpu.VMEM((tiles, points, 4 * depth), bf16),
            pltpu.VMEM((tiles, points, 128), f32),
            pltpu.VMEM((tiles, 4 * depth, points), bf16),
            pltpu.SMEM((8, 128), f32),
            pltpu.SemaphoreType.DMA((1,)),
        ],
        compiler_params=params,
        cost_estimate=pl.CostEstimate(
            flops=3 * tiles * block * depth, bytes_accessed=1 << 20, transcendentals=3 * tiles * points * points
        ),
        name="own",
    )(payload)

    damage, parts = pl.pallas_call(
        functools.partial(rest_kernel, peers),
        out_shape=(
            jax.ShapeDtypeStruct((tiles, points), f32),
            jax.ShapeDtypeStruct((peers, 128), f32),
        ),
        in_specs=[in_vmem] * 6 + [anywhere] * 8,
        out_specs=(anywhere, in_vmem),
        scratch_shapes=[pltpu.VMEM(v.shape, v.dtype) for v in (strain, history, corner_load, external, tile_sub, corner_map)]
        + [
            pltpu.VMEM((halves, tiles * pitch, 128), f32),
            pltpu.VMEM((halves, 2 * peers * pitch, 128), f32),
            pltpu.VMEM(sums.shape, f32),
        ]
        + [pltpu.SMEM(v.shape, jnp.int32) for v in (send_tile, remote_pairs, remote_count)]
        + [pltpu.SMEM((2 * peers,), jnp.int32)] * 2
        + [pltpu.SemaphoreType.DMA((10,))],
        compiler_params=params,
        cost_estimate=pl.CostEstimate(
            flops=4 * tiles * block * depth, bytes_accessed=1 << 21, transcendentals=4 * tiles * points * points
        ),
        name="rest",
    )(
        late,
        soon,
        inbox,
        b_own,
        sums,
        payload,
        *(
            in_hbm(v)
            for v in (
                history,
                corner_load,
                external,
                tile_sub,
                corner_map,
                send_tile,
                remote_pairs,
                remote_count,
            )
        ),
    )
    gathered = lax.all_to_all(parts, "blk", split_axis=0, concat_axis=0, tiled=True)
    return damage, jnp.sum(gathered, axis=0)


def solution(mesh):
    placed = (
        P(None, ("sub", "blk"), None),
        P(("sub", "blk"), None),
        P(("sub", "blk"), None),
        P(None, ("sub", "blk"), None),
        P(("sub", "blk")),
        P(("sub", "blk")),
        P(None, ("sub", "blk")),
        P(("sub", "blk")),
        P(None, ("sub", "blk")),
        P(("sub", "blk")),
        P(("sub", "blk"), None),
        P(("sub", "blk")),
    )
    return jax.shard_map(
        per_device,
        mesh=mesh,
        in_specs=placed,
        out_specs=(P(("sub", "blk"), None), P(("sub", "blk"))),
        check_vma=False,
    )
```

```python
import functools
import math

import jax
import jax.numpy as jnp
from jax import lax
from jax.experimental import pallas as pl
from jax.experimental.pallas import tpu as pltpu
from jax.sharding import PartitionSpec as P

gauss_rate = 4.0
keep_share = 0.05
softening = 0.5
coord_scale = math.sqrt(gauss_rate * math.log2(math.e))
far_off = 2048.0
depth = 32
pitch = depth + 1
grant = 24 * 1024 * 1024

f32 = jnp.float32
bf16 = jnp.bfloat16
in_vmem = pl.BlockSpec(memory_space=pltpu.VMEM)
anywhere = pl.BlockSpec(memory_space=pl.ANY)


def in_hbm(value):
    return value if value.size == 1 else pltpu.with_memory_space_constraint(value, pltpu.HBM)


def pieces(value):
    high = value.astype(bf16).astype(f32)
    rest = value - high
    middle = rest.astype(bf16).astype(f32)
    low = (rest - middle).astype(bf16).astype(f32)
    return high, middle, low


def put_rows(rows_ref, base, rows):
    for r, row in enumerate(rows):
        tiles = row.shape[0]
        for half in range(row.shape[1] // 128):
            rows_ref[half, pl.ds(base * pitch + r, tiles, stride=pitch), :] = row[:, half * 128 : (half + 1) * 128]


def point_rows(planes):
    scaled = [p * coord_scale for p in planes[:3]]
    split = [pieces(s) for s in scaled]
    norm = scaled[0] * scaled[0] + scaled[1] * scaled[1] + scaled[2] * scaled[2]
    return split, norm + jnp.where(planes[3] > 0.0, 0.0, far_off)


def put_source(planes, rows_ref, base):
    split, norm = point_rows(planes)
    ones = jnp.ones_like(norm)
    rows = []
    for high, middle, low in split:
        rows += [high, high, middle, high, low, middle]
    rows += list(pieces(-norm)) + [ones, ones, ones] + [planes[3]]
    rows += [jnp.zeros_like(norm)] * (depth - len(rows))
    put_rows(rows_ref, base, rows)


def put_target(planes, rows_ref):
    split, norm = point_rows(planes)
    ones = jnp.ones_like(norm)
    rows = []
    for high, middle, low in split:
        rows += [2.0 * v for v in (high, middle, high, low, high, middle)]
    rows += [ones, ones, ones] + list(pieces(-norm))
    rows += [jnp.zeros_like(norm)] * (depth - len(rows))
    put_rows(rows_ref, 0, rows)


def turn_group(rows_ref, group):
    turned = jnp.concatenate(
        [
            jnp.concatenate([rows_ref[half, pl.ds((group * 4 + j) * pitch, depth), :] for j in range(4)], axis=0).T
            for half in range(rows_ref.shape[0])
        ],
        axis=0,
    )
    lanes = [depth * j + 24 for j in range(4)]
    return turned.astype(bf16), [jnp.broadcast_to(turned[:, n : n + 1], turned.shape) for n in lanes]


def placed(b, j):
    above, below = [jnp.zeros((depth * n, b.shape[1]), bf16) for n in (j, 3 - j)]
    return jnp.concatenate([above] * (j > 0) + [b] + [below] * (j < 3), axis=0)


def fold(x):
    return jnp.sum(x.reshape(x.shape[0] // 8, 8, x.shape[1]), axis=0)


def column_sums(weight, s):
    load = jnp.concatenate([s] * (weight.shape[1] // 128), axis=1)
    return fold(weight * load), fold(weight)


def add_pair(sums_ref, t, a, s, b, live=None, first=False, rows=None):
    num, den = 0.0, 0.0
    rows = rows or a.shape[0]
    for lo in range(0, a.shape[0], rows):
        weight = jnp.exp2(jnp.dot(a[lo : lo + rows], b, preferred_element_type=f32))
        more_num, more_den = column_sums(weight, s[lo : lo + rows])
        num, den = num + more_num, den + more_den
    if live is not None:
        num, den = num * live, den * live
    if not first:
        num, den = sums_ref[0, t] + num, sums_ref[1, t] + den
    sums_ref[0, t] = num
    sums_ref[1, t] = den


def repeat_target(compact, b_ref):
    def some_tiles(step, carry):
        for t in [step * 4 + i for i in range(4)]:
            block = compact[t]
            for j in range(4):
                b_ref[t, depth * j : depth * (j + 1), :] = block
        return carry

    lax.fori_loop(0, compact.shape[0] // 4, some_tiles, 0)


def fetch(sources, targets, sems):
    copies = [pltpu.make_async_copy(src, dst, sems.at[i]) for i, (src, dst) in enumerate(zip(sources, targets))]
    for copy in copies:
        copy.start()
    return copies


def pack_kernel(
    peers,
    coords,
    strain,
    tile_count_in,
    send_tile_in,
    remote_pairs_in,
    remote_count_in,
    local_pairs_in,
    payload,
    outbox,
    listing,
    strain_here,
    tile_count,
    send_tile,
    remote_pairs,
    remote_count,
    own_tile,
    own_live,
    blocks,
    local_pairs,
    sems,
):
    tiles, points = strain.shape
    copies = fetch(
        (coords, strain, tile_count_in, send_tile_in, remote_pairs_in, remote_count_in, local_pairs_in),
        (payload.at[0:3], strain_here, tile_count, send_tile, remote_pairs, remote_count, local_pairs),
        sems,
    )
    listing[...] = jnp.zeros((8, 128), f32)
    for copy in copies:
        copy.wait()
    listing[0:2, 0 : local_pairs.shape[1]] = local_pairs[...].astype(f32)
    lane = lax.broadcasted_iota(jnp.int32, (1, points), 1)
    for t in range(tiles):
        payload[3, t : t + 1, :] = jnp.where(lane < tile_count[t], strain_here[t : t + 1, :], 0.0)

    halves = points // 128
    for k in range(4):
        for half in range(halves):
            rows = payload[k, 0:4, half * 128 : (half + 1) * 128]
            for first in (0, 4):
                blocks[pl.ds(half * 8 + first + k, 4, stride=8 * halves), :] = rows

    def listed(i, carry):
        h = remote_pairs[1, i]
        own_tile[h] = remote_pairs[0, i]
        own_live[h] = (i < remote_count[0]).astype(jnp.int32)
        return carry

    lax.fori_loop(0, peers, listed, 0, unroll=peers <= 8)
    row = lax.broadcasted_iota(jnp.int32, (8, 128), 0)

    def message(h, carry):
        masked = (row == 7) & (own_live[h] == 0)
        for half in range(halves):
            sent, own = [
                blocks[pl.ds(pl.multiple_of((t * halves + half) * 8, 8), 8), :] for t in (send_tile[h], own_tile[h])
            ]
            both = jnp.where(row < 4, sent, jnp.where(masked, 0.0, own))
            outbox[pl.ds(pl.multiple_of((h * halves + half) * 8, 8), 8), :] = both
        return carry

    lax.fori_loop(0, peers, message, 0, unroll=peers <= 8)


def spread_rows(values):
    n = values.shape[1]
    wide = jnp.concatenate([values.astype(f32), jnp.zeros((1, 128 - n), f32)], axis=1)
    return jnp.broadcast_to(wide, (128, 128)).T[0:n]


def own_kernel(pairs, payload, listing, b_out, sums_ref, rows_ref, a_ref, s_ref, b_ref, local_pairs, sems):
    tiles = payload.shape[1]
    copies = fetch((listing,), (local_pairs,), sems)
    planes = [payload[k] for k in range(4)]
    put_target(planes, rows_ref)

    def set_target(group, carry):
        for t in [group * 4 + i for i in range(4)]:
            rows = pl.ds(t * pitch, depth)
            for half in range(rows_ref.shape[0]):
                b_out[t, :, half * 128 : (half + 1) * 128] = rows_ref[half, rows, :].astype(bf16)
        return carry

    lax.fori_loop(0, tiles // 4, set_target, 0)
    repeat_target(b_out, b_ref)
    put_source(planes, rows_ref, 0)
    for copy in copies:
        copy.wait()

    column = lax.broadcasted_iota(jnp.int32, (1, 4 * depth), 1) // depth

    def own(step, carry):
        for group in [8 * step + g for g in range(8)]:
            left, loads = turn_group(rows_ref, group)
            for i, s in enumerate(loads):
                t = group * 4 + i
                a = left * (column == i).astype(f32).astype(bf16)
                a_ref[t] = a
                s_ref[t] = s
                add_pair(sums_ref, t, a, s, b_ref[t], first=True, rows=128)
        return carry

    lax.fori_loop(0, tiles // 32, own, 0)

    def listed(step, carry):
        for i in range(32):
            one = local_pairs[0, step * 32 + i].astype(jnp.int32)
            two = local_pairs[1, step * 32 + i].astype(jnp.int32)
            add_pair(sums_ref, two, a_ref[one], s_ref[one], b_ref[two], rows=128)
            add_pair(sums_ref, one, a_ref[two], s_ref[two], b_ref[one], rows=128)
        return carry

    lax.fori_loop(0, pairs // 32, listed, 0)


def rest_kernel(
    peers,
    late,
    soon,
    inbox,
    b_ref,
    sums_in,
    payload,
    history_in,
    corner_load_in,
    external_in,
    tile_sub_in,
    corner_map_in,
    send_tile_in,
    remote_pairs_in,
    remote_count_in,
    damage_out,
    parts_ref,
    damage_ref,
    history,
    corner_load,
    external,
    tile_sub,
    corner_map,
    rows_ref,
    far_rows,
    sums_ref,
    send_tile,
    remote_pairs,
    remote_count,
    far_tile,
    far_live,
    sems,
):
    tiles, points = history.shape
    halves = points // 128
    groups = tiles // 4
    count = lax.axis_size("sub")
    layer = lax.axis_index("sub")
    copies = fetch(
        (
            send_tile_in,
            remote_pairs_in,
            remote_count_in,
            history_in,
            corner_load_in,
            external_in,
            tile_sub_in,
            corner_map_in,
        ),
        (send_tile, remote_pairs, remote_count, history, corner_load, external, tile_sub, corner_map),
        sems.at[0:8],
    )

    sums_ref[...] = sums_in[...]

    up = 1 - 2 * lax.rem(layer, 2)

    def border(side, carry):
        shift = jnp.where(side == 0, -up, up)
        partner = layer + shift

        def some(step, carry):
            for group in [8 * step + g for g in range(8)]:
                left, loads = turn_group(rows_ref, group)
                for i, s in enumerate(loads):
                    u = group * 4 + i
                    add_pair(sums_ref, u, left, s, placed(b_ref[u], i))
                    t = lax.rem(u + shift + tiles, tiles)
                    add_pair(sums_ref, t, left, s, placed(b_ref[t], i))
            return carry

        @pl.when((partner >= 0) & (partner < count))
        def both():
            put_source([jnp.where(side == 0, soon[k], late[k]) for k in range(4)], rows_ref, 0)
            lax.fori_loop(0, groups // 8, some, 0)

        return carry

    lax.fori_loop(0, 2, border, 0)

    for copy in copies:
        copy.wait()
    for which in range(2):
        planes = [
            jnp.concatenate(
                [inbox[pl.ds(half * 8 + 4 * which + k, peers, stride=8 * halves), :] for half in range(halves)], axis=1
            )
            for k in range(4)
        ]
        put_source(planes, far_rows, which * peers)

    def place(i, carry):
        h = remote_pairs[1, i]
        far_tile[h] = remote_pairs[0, i]
        far_live[h] = (i < remote_count[0]).astype(jnp.int32)
        far_tile[peers + i] = send_tile[i]
        far_live[peers + i] = 1
        return carry

    lax.fori_loop(0, peers, place, 0, unroll=peers <= 8)

    owner = spread_rows(tile_sub[...].reshape(1, tiles))
    subs, corners = corner_map.shape
    map_rows = spread_rows(jnp.concatenate([corner_map[m : m + 1, :] for m in range(subs)], axis=1))
    leaving = []

    def finish(lo, hi):
        valid = (payload[3, lo:hi] > 0.0).astype(f32)
        num, den = jnp.sum(sums_ref[:, lo:hi], axis=2)
        strain_bar = num / (den + 1.0 - valid)
        kappa = jnp.maximum(strain_bar, history[lo:hi])
        damage = 1.0 - (keep_share + (1.0 - keep_share) * jnp.exp(-softening * (kappa - 1.0))) / kappa
        damage_ref[lo:hi] = damage
        leaving.append(
            pltpu.make_async_copy(damage_ref.at[lo:hi], damage_out.at[lo:hi], sems.at[8 + len(leaving)])
        )
        leaving[-1].start()
        intact = (1.0 - damage) * valid
        folded = 0.0
        for half in range(halves):
            cut = slice(half * 128, (half + 1) * 128)
            folded = folded + corner_load[:, lo:hi, cut] * intact[None, :, cut]
        sums = []
        for m in range(subs):
            chosen = jnp.where((owner[lo:hi] == float(m))[None], folded, 0.0)
            sums.append(jnp.sum(chosen.reshape(corners, (hi - lo) // 8, 8, 128), axis=1))
        return sums

    def far(step, carry):
        for group in [4 * step + g for g in range(4)]:
            left, loads = turn_group(far_rows, group)
            for i, s in enumerate(loads):
                t = far_tile[group * 4 + i]
                add_pair(sums_ref, t, left, s, placed(b_ref[t], i), far_live[group * 4 + i].astype(f32))
        return carry

    settled = finish(8, tiles)
    turns = 2 * peers // 16
    if turns == 1:
        far(0, 0)
    else:
        lax.fori_loop(0, turns, far, 0)
    sums = [jnp.sum(x + y, axis=1) for x, y in zip(settled, finish(0, 8))]
    sub_part = jnp.concatenate([jnp.sum(x, axis=1, keepdims=True) for x in sums], axis=0)
    sub_part = jnp.broadcast_to(sub_part, (subs * corners, 128))
    target = map_rows.astype(jnp.int32) - lax.broadcasted_iota(jnp.int32, (subs * corners, 128), 1)

    def scatter(j, carry):
        held = jnp.where(j == lax.axis_index("blk"), external[...], 0.0).reshape(1, 128)
        force = jnp.sum(jnp.where(target == j * 128, sub_part, 0.0), axis=0, keepdims=True)
        parts_ref[pl.ds(j, 1), :] = held - force
        return carry

    lax.fori_loop(0, peers, scatter, 0, unroll=peers <= 8)
    for copy in leaving:
        copy.wait()


def per_device(
    coords,
    strain,
    history,
    corner_load,
    tile_count,
    tile_sub,
    local_pairs,
    send_tile,
    remote_pairs,
    remote_count,
    corner_map,
    external,
):
    tiles, points = strain.shape
    halves = points // 128
    peers = lax.axis_size("blk")
    params = pltpu.CompilerParams(vmem_limit_bytes=grant)
    block = 2 * points * points

    payload, outbox, listing = pl.pallas_call(
        functools.partial(pack_kernel, peers),
        out_shape=(
            pltpu.VMEM((4, tiles, points), f32),
            pltpu.VMEM((peers * halves * 8, 128), f32),
            pltpu.VMEM((8, 128), f32),
        ),
        in_specs=[anywhere] * 7,
        out_specs=(in_vmem,) * 3,
        scratch_shapes=[pltpu.VMEM((tiles, points), f32)]
        + [pltpu.SMEM(v.shape, jnp.int32) for v in (tile_count, send_tile, remote_pairs, remote_count)]
        + [pltpu.SMEM((peers,), jnp.int32)] * 2
        + [pltpu.VMEM((4 * halves * 8, 128), f32)]
        + [pltpu.VMEM(local_pairs.shape, jnp.int32), pltpu.SemaphoreType.DMA((7,))],
        compiler_params=params,
        name="pack",
    )(*(in_hbm(v) for v in (coords, strain, tile_count, send_tile, remote_pairs, remote_count, local_pairs)))

    layers = lax.axis_size("sub")
    late, soon = [
        lax.ppermute(payload, "sub", [p for i in range(first, layers - 1, 2) for p in ((i, i + 1), (i + 1, i))])
        for first in (0, 1)
    ]
    inbox = lax.all_to_all(outbox, "blk", split_axis=0, concat_axis=0, tiled=True)

    b_own, sums = pl.pallas_call(
        functools.partial(own_kernel, local_pairs.shape[1]),
        out_shape=(
            jax.ShapeDtypeStruct((tiles, depth, points), bf16),
            jax.ShapeDtypeStruct((2, tiles, 8, points), f32),
        ),
        in_specs=[in_vmem] * 2,
        out_specs=(in_vmem,) * 2,
        scratch_shapes=[
            pltpu.VMEM((halves, tiles * pitch, 128), f32),
            pltpu.VMEM((tiles, points, 4 * depth), bf16),
            pltpu.VMEM((tiles, points, 128), f32),
            pltpu.VMEM((tiles, 4 * depth, points), bf16),
            pltpu.SMEM((8, 128), f32),
            pltpu.SemaphoreType.DMA((1,)),
        ],
        compiler_params=params,
        cost_estimate=pl.CostEstimate(
            flops=3 * tiles * block * depth, bytes_accessed=1 << 20, transcendentals=3 * tiles * points * points
        ),
        name="own",
    )(payload, listing)

    damage, parts = pl.pallas_call(
        functools.partial(rest_kernel, peers),
        out_shape=(
            jax.ShapeDtypeStruct((tiles, points), f32),
            jax.ShapeDtypeStruct((peers, 128), f32),
        ),
        in_specs=[in_vmem] * 6 + [anywhere] * 8,
        out_specs=(anywhere, in_vmem),
        scratch_shapes=[pltpu.VMEM(v.shape, v.dtype) for v in (strain, history, corner_load, external, tile_sub, corner_map)]
        + [
            pltpu.VMEM((halves, tiles * pitch, 128), f32),
            pltpu.VMEM((halves, 2 * peers * pitch, 128), f32),
            pltpu.VMEM(sums.shape, f32),
        ]
        + [pltpu.SMEM(v.shape, jnp.int32) for v in (send_tile, remote_pairs, remote_count)]
        + [pltpu.SMEM((2 * peers,), jnp.int32)] * 2
        + [pltpu.SemaphoreType.DMA((10,))],
        compiler_params=params,
        cost_estimate=pl.CostEstimate(
            flops=4 * tiles * block * depth, bytes_accessed=1 << 21, transcendentals=4 * tiles * points * points
        ),
        name="rest",
    )(
        late,
        soon,
        inbox,
        b_own,
        sums,
        payload,
        *(
            in_hbm(v)
            for v in (
                history,
                corner_load,
                external,
                tile_sub,
                corner_map,
                send_tile,
                remote_pairs,
                remote_count,
            )
        ),
    )
    gathered = lax.all_to_all(parts, "blk", split_axis=0, concat_axis=0, tiled=True)
    return damage, jnp.sum(gathered, axis=0)


def solution(mesh):
    placed = (
        P(None, ("sub", "blk"), None),
        P(("sub", "blk"), None),
        P(("sub", "blk"), None),
        P(None, ("sub", "blk"), None),
        P(("sub", "blk")),
        P(("sub", "blk")),
        P(None, ("sub", "blk")),
        P(("sub", "blk")),
        P(None, ("sub", "blk")),
        P(("sub", "blk")),
        P(("sub", "blk"), None),
        P(("sub", "blk")),
    )
    return jax.shard_map(
        per_device,
        mesh=mesh,
        in_specs=placed,
        out_specs=(P(("sub", "blk"), None), P(("sub", "blk"))),
        check_vma=False,
    )
```
